128 devices in a mesh: section: 2 (over x_lo), ctx: 16 (over x_hi, y, core), wshard: 4 (over z).
Axes of the slice: x: 4 (x_hi: 2, x_lo: 2; x = x_hi * 2 + x_lo), y: 4, z: 4, core: 2. Of those that a mesh axis runs over, the one named last changes fastest.
Arguments:
- inputs: bfloat16 [2, 4, 2048, 768], P(None, 'wshard', 'ctx'), may hold values from -6 to 6
- cotangent: bfloat16 [2, 4, 2048, 768], P(None, 'wshard', 'ctx'), may hold values from -6 to 6
- attn_gain: bfloat16 [2, 768], P('section', 'wshard'), may hold values from 0.099609375 to 1.8984375
- qkv_weight: bfloat16 [2, 768, 2304], P('section', 'wshard'), may hold values from -0.21875 to 0.21875
- out_weight: bfloat16 [2, 768, 768], P('section', 'wshard'), may hold values from -6 to 6
- mlp_gain: bfloat16 [2, 768], P('section', 'wshard'), may hold values from 0.099609375 to 1.8984375
- up_weight: bfloat16 [2, 768, 2304], P('section', 'wshard'), may hold values from -0.21875 to 0.21875
- down_weight: bfloat16 [2, 1152, 768], P('section', 'wshard'), may hold values from -0.1875 to 0.1875
Outputs:
- activations: bfloat16 [2, 2, 4, 2048, 768], P('section', None, 'wshard', 'ctx')
- input_grads: bfloat16 [2, 2, 4, 2048, 768], P('section', None, 'wshard', 'ctx')
- grad_attn_gain: float32 [2, 768], P('section', 'wshard')
- grad_qkv: float32 [2, 768, 2304], P('section', 'wshard')
- grad_out: float32 [2, 768, 768], P('section', 'wshard')
- grad_mlp_gain: float32 [2, 768], P('section', 'wshard')
- grad_up: float32 [2, 768, 2304], P('section', 'wshard')
- grad_down: float32 [2, 1152, 768], P('section', 'wshard')
The draws below stay inside these ranges and needn't reach their ends.
All inputs are finite; a program needn't handle non-finite values.
Results may differ from the reference program's by a relative error of at most 0.023.
Values may be sent and summed in bfloat16 or wider, within the bound.
A program may use at most 192 MiB of HBM per device.

```python
import jax
import jax.numpy as jnp
from jax import lax

D = 768
HEADS = 12
HEAD_DIM = 64
FF = 1152
MICRO = 2
LAYERS = 2
BATCH = 4
LENGTH = 2048


def block_scale(key, shape, cuts, least, largest):
    def one(axis_at, blocks):
        steps = jax.random.uniform(jax.random.fold_in(jax.random.fold_in(key, 6), axis_at), (blocks,), jnp.float32, least / len(cuts), largest / len(cuts))
        return jnp.repeat(jnp.exp(steps), shape[axis_at] // blocks).reshape((-1,) + (1,) * (len(shape) - axis_at - 1))

    gain = one(*cuts[0])
    for cut in cuts[1:]:
        gain = gain * one(*cut)
    return gain


def normal_values(own_key, shape, width, limit, cuts=(), held_as=jnp.bfloat16):
    array = width * jax.random.normal(own_key, shape, jnp.float32)
    if cuts:
        array = array * block_scale(own_key, shape, cuts, -0.22, 0.18)
    return jnp.clip(array, -limit, limit).astype(held_as)


def setup_inputs(seed: int = 0) -> dict:
    seeds = jax.random.split(jax.random.key(seed), 9)
    inputs = normal_values(seeds[0], (MICRO, BATCH, LENGTH, D), 1.0, 6.0, ((1, 4), (2, 16)))
    cotangent = normal_values(seeds[1], (MICRO, BATCH, LENGTH, D), 1.0, 6.0, ((1, 4), (2, 16)))
    attn_gain = jnp.clip(1.0 + 0.18 * jax.random.normal(seeds[2], (LAYERS, D), jnp.float32), 0.099609375, 1.8984375).astype(jnp.bfloat16)
    qkv_weight = normal_values(seeds[3], (LAYERS, D, 3 * D), D ** -0.5, 0.21875, ((0, 2), (1, 4)))
    out_weight = normal_values(seeds[4], (LAYERS, D, D), (max(1, D * 4 // LENGTH)) ** -0.5, 6.0, ((0, 2), (1, 4)))
    mlp_gain = jnp.clip(1.0 + 0.18 * jax.random.normal(seeds[5], (LAYERS, D), jnp.float32), 0.099609375, 1.8984375).astype(jnp.bfloat16)
    up_weight = normal_values(seeds[6], (LAYERS, D, 2 * FF), D ** -0.5, 0.21875, ((0, 2), (1, 4)))
    down_weight = normal_values(seeds[7], (LAYERS, FF, D), FF ** -0.5, 0.1875, ((0, 2), (1, 4)))
    return dict(inputs=inputs, cotangent=cotangent, attn_gain=attn_gain, qkv_weight=qkv_weight, out_weight=out_weight, mlp_gain=mlp_gain, up_weight=up_weight, down_weight=down_weight)


@jax.custom_vjp
def low(v):
    return lax.optimization_barrier(v.astype(jnp.bfloat16)).astype(jnp.float32)

@jax.custom_vjp
def low_back(v):
    return v

def low_keep(v):
    return (low(v), None)

def low_pass(kept, grad):
    return (grad,)

def back_keep(v):
    return (v, None)

def back_low(kept, grad):
    return (low(grad),)
low.defvjp(low_keep, low_pass)
low_back.defvjp(back_keep, back_low)
HIGHEST = lax.Precision.HIGHEST

def norm_rows(source):
    centered = source - lax.optimization_barrier(jnp.mean(source, axis=-1, keepdims=True))
    variance = lax.optimization_barrier(jnp.mean(centered * centered, axis=-1, keepdims=True))
    return centered * lax.rsqrt(variance + 1e-05)

def rotate(heads_in, positions):
    half_width = HEAD_DIM // 2
    frequency = 1.0 / 160000.0 ** (jnp.arange(half_width, dtype=jnp.float32) * 2.0 / HEAD_DIM)
    angles = positions[:, None] * frequency[None, :]
    cosine_table = jnp.cos(angles)[:, None, :]
    sine_table = jnp.sin(angles)[:, None, :]
    first_half = heads_in[..., :half_width]
    second_half = heads_in[..., half_width:]
    return jnp.concatenate([first_half * cosine_table - second_half * sine_table, second_half * cosine_table + first_half * sine_table], axis=-1)

def block_forward(source, attn_gain, qkv_weight, out_weight, mlp_gain, up_weight, down_weight):
    length_here = source.shape[0]
    score_scale = HEAD_DIM ** (-0.5)
    normed = low(norm_rows(source) * attn_gain)
    projected = low_back(jnp.dot(normed, qkv_weight, precision=HIGHEST))
    positions = jnp.arange(length_here, dtype=jnp.float32)
    queries = low(rotate(projected[:, :D].reshape(length_here, HEADS, HEAD_DIM), positions))
    key_rows = low(rotate(projected[:, D:2 * D].reshape(length_here, HEADS, HEAD_DIM), positions))
    values = low(projected[:, 2 * D:].reshape(length_here, HEADS, HEAD_DIM))
    scores = low_back(jnp.einsum('qhd,khd->hqk', queries, key_rows, precision=HIGHEST) * score_scale)
    totals = jax.nn.logsumexp(scores, axis=-1)
    probs = low(jnp.exp(scores - totals[..., None]))
    attended = low_back(jnp.einsum('hqk,khd->qhd', probs, values, precision=HIGHEST)).reshape(length_here, D)
    branch = low_back(jnp.dot(low(attended), out_weight, precision=HIGHEST))
    hidden = source + branch
    normed_two = low(norm_rows(hidden) * mlp_gain)
    gate_up = low_back(jnp.dot(normed_two, up_weight, precision=HIGHEST))
    product = low(jax.nn.gelu(gate_up[:, :FF], approximate=False) * gate_up[:, FF:])
    return hidden + low_back(jnp.dot(product, down_weight, precision=HIGHEST))

def reference(inputs, cotangent, attn_gain, qkv_weight, out_weight, mlp_gain, up_weight, down_weight):
    weight_sets = []
    for layer_index in range(2):
        weight_sets.append(tuple((w[layer_index].astype(jnp.float32) for w in (attn_gain, qkv_weight, out_weight, mlp_gain, up_weight, down_weight))))
    full_shape = inputs.shape
    seq_total = full_shape[0] * full_shape[1]
    sequences = inputs.reshape(seq_total, LENGTH, D)
    cotangents = cotangent.reshape(seq_total, LENGTH, D)
    zero_grads = tuple((jnp.zeros(w.shape, jnp.float32) for w in weight_sets[0]))

    def per_sequence(totals_in, pieces):
        source, cot_rows = pieces
        layer_one, back_one = jax.vjp(block_forward, source.astype(jnp.float32), *weight_sets[0])
        sent_value = layer_one.astype(jnp.bfloat16)
        layer_two, back_two = jax.vjp(block_forward, sent_value.astype(jnp.float32), *weight_sets[1])
        grads_two = back_two(cot_rows.astype(jnp.float32))
        returned = grads_two[0].astype(jnp.bfloat16)
        grads_one = back_one(returned.astype(jnp.float32))
        new_totals = (tuple((x + y for x, y in zip(totals_in[0], grads_one[1:]))), tuple((x + y for x, y in zip(totals_in[1], grads_two[1:]))))
        return (new_totals, (sent_value, layer_two.astype(jnp.bfloat16), grads_one[0].astype(jnp.bfloat16), returned))
    summed, outputs = lax.scan(per_sequence, (zero_grads, zero_grads), (sequences, cotangents))
    sent_all, final_all, start_grads, returned_all = outputs
    activations = jnp.stack([sent_all.reshape(full_shape), final_all.reshape(full_shape)])
    input_grads = jnp.stack([start_grads.reshape(full_shape), returned_all.reshape(full_shape)])
    stacked = tuple((jnp.stack([x, y]) for x, y in zip(summed[0], summed[1])))
    return (activations, input_grads, stacked[0], stacked[1], stacked[2], stacked[3], stacked[4], stacked[5])
```

```python
import functools

import jax
import jax.numpy as jnp
from jax import lax
from jax.experimental import pallas as pl
from jax.experimental.pallas import tpu as pltpu
from jax.sharding import PartitionSpec as P

D = 768
HEADS = 12
HEAD_DIM = 64
FF = 1152
ROWS = 128
GROUPS = 4
GH = HEADS // GROUPS
GW = GH * HEAD_DIM
CTX = 16
SCALE = HEAD_DIM ** (-0.5)
F32 = jnp.float32
BF16 = jnp.bfloat16
MESH = pl.DeviceIdType.MESH
DMA = pltpu.SemaphoreType.DMA
ANY = pl.BlockSpec(memory_space=pl.ANY)
VM = pl.BlockSpec(memory_space=pltpu.VMEM)
VMEM_LIMIT = 56 * 1024 * 1024


def dot(a, b):
    return jnp.dot(a, b, preferred_element_type=F32)


def dot_nt(a, b):
    return lax.dot_general(a, b, (((1,), (1,)), ((), ())), preferred_element_type=F32)


def sds(shape, dtype):
    return jax.ShapeDtypeStruct(shape, dtype)


def compute_call(kernel, args, outs, scratch=(), name=None):
    return pl.pallas_call(
        kernel,
        out_shape=outs,
        in_specs=[VM] * len(args),
        out_specs=jax.tree.map(lambda _: VM, outs),
        scratch_shapes=list(scratch),
        compiler_params=pltpu.CompilerParams(vmem_limit_bytes=VMEM_LIMIT),
        name=name,
    )(*args)


def norm_parts(source):
    centered = source - jnp.mean(source, axis=-1, keepdims=True)
    variance = jnp.mean(centered * centered, axis=-1, keepdims=True)
    rstd = lax.rsqrt(variance + 1e-05)
    return centered * rstd, rstd


def norm_back(grad, normalized, rstd, gain):
    inner = grad * gain
    mean_one = jnp.mean(inner, axis=-1, keepdims=True)
    mean_two = jnp.mean(inner * normalized, axis=-1, keepdims=True)
    grad_gain = jnp.sum(grad * normalized, axis=0, keepdims=True)
    return rstd * (inner - mean_one - normalized * mean_two), grad_gain


def qkv_kernel(x_ref, gain_ref, w_ref, cos_ref, sin_ref, qkv_ref, normed_ref):
    normalized, _ = norm_parts(x_ref[...].astype(F32))
    normed = (normalized * gain_ref[...].astype(F32)).astype(BF16)
    normed_ref[...] = normed
    cos = cos_ref[...]
    sin = sin_ref[...]
    for part in range(3):
        for block in range(3):
            at = part * D + block * 256
            turned = dot(normed, w_ref[:, at : at + 256]).T
            for head_at in range(4):
                head = block * 4 + head_at
                one = turned[head_at * 64 : head_at * 64 + 32]
                two = turned[head_at * 64 + 32 : head_at * 64 + 64]
                if part < 2:
                    one, two = one * cos - two * sin, two * cos + one * sin
                if part == 0:
                    one, two = one * SCALE, two * SCALE
                row = part * GW + (head % GH) * HEAD_DIM
                qkv_ref[head // GH, row : row + 32, :] = one.astype(BF16)
                qkv_ref[head // GH, row + 32 : row + 64, :] = two.astype(BF16)


CHUNK = 256
CHUNKS = 2048 // CHUNK
PAIR = CHUNK // ROWS


def attend_kernel(q_ref, kv_ref, low_ref, wide_ref, totals_ref, s_ref):
    @pl.loop(0, GH)
    def _(h):
        at = pl.multiple_of(h * HEAD_DIM, HEAD_DIM)
        value_at = pl.multiple_of(h * HEAD_DIM + GW, HEAD_DIM)
        qt = jnp.concatenate([q_ref[i, pl.ds(at, HEAD_DIM), :] for i in range(4)], axis=1)
        top = jnp.full((8, 512), -jnp.inf, F32)
        for c in range(CHUNKS):
            keys = jnp.concatenate(
                [kv_ref[c * PAIR + i, pl.ds(at, HEAD_DIM), :].T for i in range(PAIR)], axis=0
            )
            scores = dot(keys, qt)
            s_ref[c * CHUNK : (c + 1) * CHUNK, :] = scores
            top = jnp.maximum(top, jnp.max(scores.reshape(CHUNK // 8, 8, 512), axis=0))
        top = jnp.max(top, axis=0, keepdims=True)
        total = jnp.zeros((8, 512), F32)
        acc = jnp.zeros((HEAD_DIM, 512), F32)
        for c in range(CHUNKS):
            p = jnp.exp(s_ref[c * CHUNK : (c + 1) * CHUNK, :] - top)
            total = total + jnp.sum(p.reshape(CHUNK // 8, 8, 512), axis=0)
            values = jnp.concatenate(
                [kv_ref[c * PAIR + i, pl.ds(value_at, HEAD_DIM), :] for i in range(PAIR)], axis=1
            )
            acc = acc + dot(values, p.astype(BF16))
        total = jnp.sum(total, axis=0, keepdims=True)
        out = acc / total
        totals_ref[h] = jnp.broadcast_to(top + jnp.log(total), (8, 512))
        for i in range(4):
            piece = out[:, i * ROWS : (i + 1) * ROWS]
            wide_ref[i, pl.ds(at, HEAD_DIM), :] = piece
            low_ref[i, pl.ds(at, HEAD_DIM), :] = piece.astype(BF16)


def attend_back_kernel(q_ref, kv_ref, wide_ref, totals_ref, do_ref, dq_ref, dkv_ref):
    @pl.loop(0, GH)
    def _(h):
        at = pl.multiple_of(h * HEAD_DIM, HEAD_DIM)
        value_at = pl.multiple_of(h * HEAD_DIM + GW, HEAD_DIM)
        out_at = pl.multiple_of(h * ROWS, ROWS)
        qt = jnp.concatenate([q_ref[i, pl.ds(at, HEAD_DIM), :] for i in range(4)], axis=1)
        dot_t = jnp.concatenate([do_ref[i, pl.ds(at, HEAD_DIM), :] for i in range(4)], axis=1)
        wide = jnp.concatenate([wide_ref[i, pl.ds(at, HEAD_DIM), :] for i in range(4)], axis=1)
        delta = jnp.sum(wide * dot_t.astype(F32), axis=0, keepdims=True)
        totals = totals_ref[h, 0:1, :]
        zero = jnp.zeros((512, HEAD_DIM), BF16)
        sides = jnp.concatenate(
            [
                jnp.concatenate([qt.T, zero], axis=1),
                jnp.concatenate([zero, dot_t.T], axis=1),
            ],
            axis=0,
        )

        def step(c, acc):
            keys_t = [kv_ref[c * PAIR + i, pl.ds(at, HEAD_DIM), :] for i in range(PAIR)]
            values_t = [kv_ref[c * PAIR + i, pl.ds(value_at, HEAD_DIM), :] for i in range(PAIR)]
            keys = jnp.concatenate([k.T for k in keys_t], axis=0)
            values = jnp.concatenate([v.T for v in values_t], axis=0)
            p = jnp.exp(dot(keys, qt) - totals)
            ds = (p * (dot(values, dot_t) - delta)).astype(BF16)
            both = jnp.concatenate([ds, p.astype(BF16)], axis=1)
            grads = dot(both, sides).astype(BF16)
            for i in range(PAIR):
                dkv_ref[c * PAIR + i, pl.ds(out_at, ROWS), :] = grads[i * ROWS : (i + 1) * ROWS]
            return acc + dot(jnp.concatenate(keys_t, axis=1), ds)

        acc = lax.fori_loop(0, CHUNKS, step, jnp.zeros((HEAD_DIM, 512), F32)) * SCALE
        for i in range(4):
            dq_ref[i, pl.ds(at, HEAD_DIM), :] = acc[:, i * ROWS : (i + 1) * ROWS].astype(BF16)


def mlp_kernel(
    ot_ref, x_ref, gain_ref, wo_ref, wu_ref, wd_ref,
    out_ref, hidden_ref, gate_up_ref, normed_ref, product_ref,
):
    attended = ot_ref[...].astype(F32).T.astype(BF16)
    hidden = x_ref[...].astype(F32) + dot(attended, wo_ref[...])
    hidden_ref[...] = hidden
    normalized, _ = norm_parts(hidden)
    normed = (normalized * gain_ref[...].astype(F32)).astype(BF16)
    normed_ref[...] = normed
    gate_up = dot(normed, wu_ref[...])
    gate_up_ref[...] = gate_up
    gate = gate_up[:, :FF]
    phi = 0.5 * (1.0 + lax.erf(gate * 0.5**0.5))
    product = (gate * phi * gate_up[:, FF:]).astype(BF16)
    product_ref[...] = product
    out_ref[...] = (hidden + dot(product, wd_ref[...])).astype(BF16)


def mlp_back_kernel(
    g_ref, ot_ref, hidden_ref, gate_up_ref, normed_ref, product_ref, gain_ref, wo_ref, wu_ref, wd_ref,
    dot_ref, grad_hidden_ref, d_out_ref, d_up_ref, d_down_ref, d_gain_ref,
):
    grad = g_ref[...]
    grad_product = dot_nt(grad, wd_ref[...])
    d_down_ref[...] = dot(product_ref[...].astype(F32).T.astype(BF16), grad).astype(BF16)
    gate = gate_up_ref[:, :FF]
    up = gate_up_ref[:, FF:]
    phi = 0.5 * (1.0 + lax.erf(gate * 0.5**0.5))
    density = jnp.exp(-0.5 * gate * gate) * 0.3989422804014327
    grad_gate = (grad_product * up * (phi + gate * density)).astype(BF16)
    grad_up = (grad_product * gate * phi).astype(BF16)
    normed_t = normed_ref[...].astype(F32).T.astype(BF16)
    d_up_ref[:, :FF] = dot(normed_t, grad_gate).astype(BF16)
    d_up_ref[:, FF:] = dot(normed_t, grad_up).astype(BF16)
    grad_normed = dot_nt(grad_gate, wu_ref[:, :FF]) + dot_nt(grad_up, wu_ref[:, FF:])
    normalized, rstd = norm_parts(hidden_ref[...])
    part, d_gain = norm_back(grad_normed, normalized, rstd, gain_ref[...].astype(F32))
    d_gain_ref[...] = d_gain
    grad_hidden = grad.astype(F32) + part
    grad_hidden_ref[...] = grad_hidden
    branch = grad_hidden.astype(BF16)
    d_out_ref[...] = dot(ot_ref[...], branch).astype(BF16)
    dot_ref[...] = dot_nt(branch, wo_ref[...]).T.astype(BF16)


def qkv_back_kernel(
    dq_ref, dkv_ref, x_ref, gain_ref, normed_ref, w_ref, cos_ref, sin_ref, grad_hidden_ref,
    grad_x_ref, d_qkv_ref, d_gain_ref, gp_ref,
):
    cos = cos_ref[...]
    sin = sin_ref[...]

    def back(one, two):
        return one * cos + two * sin, two * cos - one * sin

    for head in range(HEADS):
        group, inner = head // GH, head % GH
        at = inner * HEAD_DIM
        one = dq_ref[group, at : at + 32, :].astype(F32)
        two = dq_ref[group, at + 32 : at + 64, :].astype(F32)
        gq = back(one, two)
        rows = slice(inner * ROWS, (inner + 1) * ROWS)
        kv = (dkv_ref[2 * group, rows, :].astype(F32) + dkv_ref[2 * group + 1, rows, :].astype(F32)).T
        gk = back(kv[:32], kv[32:64])
        base = head * HEAD_DIM
        gp_ref[base : base + 32, :] = gq[0]
        gp_ref[base + 32 : base + 64, :] = gq[1]
        gp_ref[D + base : D + base + 32, :] = gk[0]
        gp_ref[D + base + 32 : D + base + 64, :] = gk[1]
        gp_ref[2 * D + base : 2 * D + base + 64, :] = kv[64:]
    normed_t = normed_ref[...].astype(F32).T.astype(BF16)
    grad_normed = jnp.zeros((ROWS, D), F32)
    for block in range(9):
        cols = slice(block * 256, (block + 1) * 256)
        gp = gp_ref[cols, :].T.astype(BF16)
        d_qkv_ref[:, cols] = dot(normed_t, gp).astype(BF16)
        grad_normed = grad_normed + dot_nt(gp, w_ref[:, cols])
    normalized, rstd = norm_parts(x_ref[...].astype(F32))
    part, d_gain = norm_back(grad_normed, normalized, rstd, gain_ref[...].astype(F32))
    d_gain_ref[...] = d_gain
    grad_x_ref[...] = (grad_hidden_ref[...] + part).astype(BF16)


def here():
    return lax.axis_index("section"), lax.axis_index("ctx"), lax.axis_index("wshard")


def flip(index, delta):
    for bit in (1, 2, 4, 8):
        if delta & bit:
            index = index + bit - 2 * bit * lax.rem(index // bit, 2)
    return index


def greet(peers):
    barrier = pltpu.get_barrier_semaphore()
    for peer in peers:
        pl.semaphore_signal(barrier, inc=1, device_id=peer, device_id_type=MESH)
    pl.semaphore_wait(barrier, len(peers))


def remote(src, dst, send, recv, peer):
    return pltpu.make_async_remote_copy(
        src_ref=src, dst_ref=dst, send_sem=send, recv_sem=recv, device_id=peer, device_id_type=MESH
    )


def exchange_call(kernel, args, outs, scratch, collective_id, name):
    return pl.pallas_call(
        kernel,
        out_shape=outs,
        in_specs=[ANY] * len(args),
        out_specs=jax.tree.map(lambda _: ANY, outs),
        scratch_shapes=list(scratch),
        compiler_params=pltpu.CompilerParams(
            collective_id=collective_id, has_side_effects=True, vmem_limit_bytes=VMEM_LIMIT
        ),
        name=name,
    )(*args)


def spread_kernel(qkv_ref, q_ref, kv_ref, kv_send, kv_recv, q_send, q_recv, sib_send, sib_recv, own):
    s, c, z = here()
    sibling = (s, flip(c, 1), z)
    peers = {delta: (s, flip(c, delta), z) for delta in range(2, CTX, 2)}
    greet([sibling, *peers.values()])
    kv_rows = pl.ds(GW, 2 * GW)
    q_rows = pl.ds(0, GW)
    order = [14, 10, 12, 8, 6, 4, 2]
    sends = []
    for delta in order:
        peer = peers[delta]
        copy = remote(
            qkv_ref.at[peer[1] // 4, kv_rows], kv_ref.at[c], kv_send.at[delta], kv_recv.at[delta], peer
        )
        copy.start()
        sends.append(copy)
        if delta % 4 == 0:
            copy = remote(
                qkv_ref.at[peer[1] // 4, q_rows], q_ref.at[c // 4], q_send.at[delta], q_recv.at[delta], peer
            )
            copy.start()
            sends.append(copy)
    own_kv = pltpu.make_async_copy(qkv_ref.at[c // 4, kv_rows], kv_ref.at[c], own.at[0])
    own_q = pltpu.make_async_copy(qkv_ref.at[c // 4, q_rows], q_ref.at[c // 4], own.at[1])
    own_kv.start()
    own_q.start()
    mine = remote(qkv_ref.at[c // 4, kv_rows], kv_ref.at[c], sib_send.at[0], sib_recv.at[0], sibling)
    mine.start()
    passed = [mine]
    for delta in reversed(order):
        source = flip(c, delta)
        remote(kv_ref.at[source], kv_ref.at[source], kv_send.at[delta], kv_recv.at[delta], sibling).wait_recv()
        copy = remote(kv_ref.at[source], kv_ref.at[source], sib_send.at[delta], sib_recv.at[delta], sibling)
        copy.start()
        passed.append(copy)
    own_kv.wait()
    own_q.wait()
    for delta in (4, 8, 12):
        slot = q_ref.at[flip(c, delta) // 4]
        remote(slot, slot, q_send.at[delta], q_recv.at[delta], sibling).wait_recv()
    for copy in sends:
        copy.wait_send()
    for copy in passed:
        copy.wait()


def spread(qkv, collective_id):
    return exchange_call(
        spread_kernel,
        (qkv,),
        (sds((4, GW, ROWS), BF16), sds((CTX, 2 * GW, ROWS), BF16)),
        [DMA((16,))] * 6 + [DMA((2,))],
        collective_id,
        "spread",
    )


def turn_kernel(x_ref, o_ref, send, recv, own):
    s, c, z = here()
    peers = [(s, flip(c, delta), z) for delta in (4, 8, 12)]
    greet(peers)
    copies = []
    for i, peer in enumerate(peers):
        copy = remote(x_ref.at[peer[1] // 4], o_ref.at[c // 4], send.at[i], recv.at[i], peer)
        copy.start()
        copies.append(copy)
    kept = pltpu.make_async_copy(x_ref.at[c // 4], o_ref.at[c // 4], own)
    kept.start()
    kept.wait()
    for copy in copies:
        copy.wait()


def turn(x, collective_id):
    return exchange_call(
        turn_kernel, (x,), sds((4, GW, ROWS), BF16), [DMA((3,)), DMA((3,)), DMA], collective_id, "turn"
    )


def return_kernel(
    dq_ref, dkv_ref, dqo_ref, sums_ref, mine, theirs, total, got,
    q_send, q_recv, sib_send, sib_recv, load, kv_send, kv_recv, own,
):
    s, c, z = here()
    core = lax.rem(c, 2)
    sibling = (s, flip(c, 1), z)
    peers = {delta: (s, flip(c, delta), z) for delta in range(2, CTX, 2)}
    greet([sibling, *peers.values()])
    passed = []
    for i in range(8):
        copy = remote(dkv_ref.at[2 * i + 1 - core], theirs.at[i], sib_send.at[i], sib_recv.at[i], sibling)
        copy.start()
        passed.append(copy)
    loads = []
    for i in range(8):
        copy = pltpu.make_async_copy(dkv_ref.at[2 * i + core], mine.at[i], load.at[i])
        copy.start()
        loads.append(copy)
    sends = []
    for delta in (4, 8, 12):
        peer = peers[delta]
        copy = remote(dq_ref.at[peer[1] // 4], dqo_ref.at[c // 4], q_send.at[delta], q_recv.at[delta], peer)
        copy.start()
        sends.append(copy)
    own_q = pltpu.make_async_copy(dq_ref.at[c // 4], dqo_ref.at[c // 4], own.at[0])
    own_q.start()
    for i in range(8):
        loads[i].wait()
        passed[i].wait()
        total[i] = (mine[i].astype(F32) + theirs[i].astype(F32)).astype(BF16)
    for delta in (14, 10, 12, 8, 6, 4, 2):
        peer = peers[delta]
        copy = remote(total.at[peer[1] // 2], sums_ref.at[c // 2], kv_send.at[delta], kv_recv.at[delta], peer)
        copy.start()
        sends.append(copy)
    own_kv = pltpu.make_async_copy(total.at[c // 2], sums_ref.at[c // 2], own.at[1])
    own_kv.start()
    own_kv.wait()
    own_q.wait()
    for copy in sends:
        copy.wait()


def give_back(dq, dkv, collective_id):
    block = pltpu.VMEM((8, 2 * GW, ROWS), BF16)
    return exchange_call(
        return_kernel,
        (dq, dkv),
        (sds((4, GW, ROWS), BF16), sds((8, 2 * GW, ROWS), BF16)),
        [block, block, block, pltpu.VMEM((8, ROWS), F32)]
        + [DMA((16,)), DMA((16,)), DMA((8,)), DMA((8,)), DMA((8,)), DMA((16,)), DMA((16,)), DMA((2,))],
        collective_id,
        "give_back",
    )


def rope_tables():
    positions = (lax.axis_index("ctx") * ROWS + lax.iota(jnp.int32, ROWS)).astype(F32)
    frequency = 1.0 / 160000.0 ** (jnp.arange(HEAD_DIM // 2, dtype=F32) * 2.0 / HEAD_DIM)
    angles = frequency[:, None] * positions[None, :]
    return jnp.cos(angles), jnp.sin(angles)


def forward_layer(x, weights, tables):
    gain_one, w_qkv, w_out, gain_two, w_up, w_down = weights
    qkv, normed = compute_call(
        qkv_kernel,
        (x, gain_one, w_qkv, *tables),
        (sds((4, 3 * GW, ROWS), BF16), sds((ROWS, D), BF16)),
        name="norm_qkv",
    )
    q, kv = spread(qkv, 1)
    low, wide, totals = compute_call(
        attend_kernel,
        (q, kv),
        (sds((4, GW, ROWS), BF16), sds((4, GW, ROWS), F32), sds((GH, 8, 512), F32)),
        [pltpu.VMEM((2048, 512), F32)],
        name="attend",
    )
    ot = turn(low, 2).reshape(D, ROWS)
    out, hidden, gate_up, normed_two, product = compute_call(
        mlp_kernel,
        (ot, x, gain_two, w_out, w_up, w_down),
        (sds((ROWS, D), BF16), sds((ROWS, D), F32), sds((ROWS, 2 * FF), F32),
         sds((ROWS, D), BF16), sds((ROWS, FF), BF16)),
        name="mlp",
    )
    return out, (x, normed, q, kv, wide, totals, ot, hidden, gate_up, normed_two, product)


def backward_layer(grad, stored, weights, tables):
    gain_one, w_qkv, w_out, gain_two, w_up, w_down = weights
    x, normed, q, kv, wide, totals, ot, hidden, gate_up, normed_two, product = stored
    d_ot, grad_hidden, d_out, d_up, d_down, d_gain_two = compute_call(
        mlp_back_kernel,
        (grad, ot, hidden, gate_up, normed_two, product, gain_two, w_out, w_up, w_down),
        (sds((D, ROWS), BF16), sds((ROWS, D), F32), sds((D, D), BF16),
         sds((D, 2 * FF), BF16), sds((FF, D), BF16), sds((1, D), F32)),
        name="mlp_back",
    )
    d_o = turn(d_ot.reshape(4, GW, ROWS), 2)
    dq, dkv = compute_call(
        attend_back_kernel,
        (q, kv, wide, totals, d_o),
        (sds((4, GW, ROWS), BF16), sds((CTX, 2 * GW, ROWS), BF16)),
        name="attend_back",
    )
    dq, dkv = give_back(dq, dkv, 3)
    grad_x, d_qkv, d_gain_one = compute_call(
        qkv_back_kernel,
        (dq, dkv, x, gain_one, normed, w_qkv, *tables, grad_hidden),
        (sds((ROWS, D), BF16), sds((D, 3 * D), BF16), sds((1, D), F32)),
        [pltpu.VMEM((3 * D, ROWS), F32)],
        name="qkv_back",
    )
    return grad_x, (d_gain_one, d_qkv, d_out, d_gain_two, d_up, d_down)


def gather_weights(arrays):
    gathered = []
    for a in arrays:
        whole = lax.all_gather(a[0], ("section", "wshard"), axis=0, tiled=True)
        gathered.append(whole.reshape(2, -1, whole.shape[-1]))
    return gathered


def reduce_grads(first, second):
    shards = []
    for a, b in zip(first, second):
        both = jnp.concatenate([a, b], axis=0).astype(BF16)
        part = lax.psum_scatter(both, ("section", "wshard"), scatter_dimension=0, tiled=True)
        shards.append(lax.psum(part, "ctx").astype(F32))
    return shards


def swap_layers(zero, one):
    first = lax.axis_index("section") == 0
    other = lax.ppermute(jnp.where(first, one, zero), "section", [(0, 1), (1, 0)])
    kept = jnp.where(first, zero, one)
    return jnp.stack([jnp.where(first, kept, other), jnp.where(first, other, kept)])[None, :, None]


def local(inputs, cotangent, attn_gain, qkv_weight, out_weight, mlp_gain, up_weight, down_weight):
    section = lax.axis_index("section")
    first = section == 0
    x = jnp.where(first, inputs[0, 0], inputs[1, 0])
    cot = jnp.where(first, cotangent[0, 0], cotangent[1, 0])
    w_qkv, w_out, w_up, w_down = gather_weights([qkv_weight, out_weight, up_weight, down_weight])
    gains = [
        lax.all_gather(g[0], ("section", "wshard"), axis=0, tiled=True).reshape(2, 1, D)
        for g in (attn_gain, mlp_gain)
    ]
    stacked = (gains[0], w_qkv, w_out, gains[1], w_up, w_down)
    weights = [tuple(w[layer] for w in stacked) for layer in range(2)]
    tables = rope_tables()
    mid, stored_zero = forward_layer(x, weights[0], tables)
    end, stored_one = forward_layer(mid, weights[1], tables)
    grad_mid, grads_one = backward_layer(cot, stored_one, weights[1], tables)
    grad_start, grads_zero = backward_layer(grad_mid, stored_zero, weights[0], tables)
    activations = swap_layers(mid, end)
    input_grads = swap_layers(grad_start, grad_mid)
    flat = lambda grads: [grads[0].reshape(D, 1), grads[1], grads[2], grads[3].reshape(D, 1), grads[4], grads[5]]
    reduced = reduce_grads(flat(grads_zero), flat(grads_one))
    return (
        activations,
        input_grads,
        reduced[0].reshape(1, -1),
        reduced[1][None],
        reduced[2][None],
        reduced[3].reshape(1, -1),
        reduced[4][None],
        reduced[5][None],
    )


def solution(mesh):
    placed = (
        P(None, "wshard", "ctx", None),
        P(None, "wshard", "ctx", None),
        P("section", "wshard"),
        P("section", "wshard", None),
        P("section", "wshard", None),
        P("section", "wshard"),
        P("section", "wshard", None),
        P("section", "wshard", None),
    )
    return jax.shard_map(
        local,
        mesh=mesh,
        in_specs=placed,
        out_specs=(
            P("section", None, "wshard", "ctx", None),
            P("section", None, "wshard", "ctx", None),
            P("section", "wshard"),
            P("section", "wshard", None),
            P("section", "wshard", None),
            P("section", "wshard"),
            P("section", "wshard", None),
            P("section", "wshard", None),
        ),
        check_vma=False,
    )
```

```python
import functools

import jax
import jax.numpy as jnp
from jax import lax
from jax.experimental import pallas as pl
from jax.experimental.pallas import tpu as pltpu
from jax.sharding import PartitionSpec as P

D = 768
HEADS = 12
HEAD_DIM = 64
FF = 1152
ROWS = 128
GROUPS = 4
GH = HEADS // GROUPS
GW = GH * HEAD_DIM
CTX = 16
SCALE = HEAD_DIM ** (-0.5)
F32 = jnp.float32
BF16 = jnp.bfloat16
MESH = pl.DeviceIdType.MESH
DMA = pltpu.SemaphoreType.DMA
ANY = pl.BlockSpec(memory_space=pl.ANY)
VM = pl.BlockSpec(memory_space=pltpu.VMEM)
VMEM_LIMIT = 56 * 1024 * 1024


def dot(a, b):
    return jnp.dot(a, b, preferred_element_type=F32)


def dot_nt(a, b):
    return lax.dot_general(a, b, (((1,), (1,)), ((), ())), preferred_element_type=F32)


def sds(shape, dtype):
    return jax.ShapeDtypeStruct(shape, dtype)


def compute_call(kernel, args, outs, scratch=(), name=None):
    return pl.pallas_call(
        kernel,
        out_shape=outs,
        in_specs=[VM] * len(args),
        out_specs=jax.tree.map(lambda _: VM, outs),
        scratch_shapes=list(scratch),
        compiler_params=pltpu.CompilerParams(vmem_limit_bytes=VMEM_LIMIT),
        name=name,
    )(*args)


def turned_low(x):
    return x.astype(F32).T.astype(BF16)


def norm_parts(source):
    centered = source - jnp.mean(source, axis=-1, keepdims=True)
    variance = jnp.mean(centered * centered, axis=-1, keepdims=True)
    rstd = lax.rsqrt(variance + 1e-05)
    return centered * rstd, rstd


def norm_back(grad, normalized, rstd, gain):
    inner = grad * gain
    mean_one = jnp.mean(inner, axis=-1, keepdims=True)
    mean_two = jnp.mean(inner * normalized, axis=-1, keepdims=True)
    grad_gain = jnp.sum(grad * normalized, axis=0, keepdims=True)
    return rstd * (inner - mean_one - normalized * mean_two), grad_gain


def qkv_kernel(x_ref, gain_ref, w_ref, cos_ref, sin_ref, qkv_ref, normed_ref):
    normalized, _ = norm_parts(x_ref[...].astype(F32))
    normed = (normalized * gain_ref[...].astype(F32)).astype(BF16)
    normed_ref[...] = turned_low(normed)
    cos = cos_ref[...]
    sin = sin_ref[...]
    for part in range(3):
        for block in range(3):
            at = part * D + block * 256
            turned = dot(normed, w_ref[:, at : at + 256]).T
            for head_at in range(4):
                head = block * 4 + head_at
                one = turned[head_at * 64 : head_at * 64 + 32]
                two = turned[head_at * 64 + 32 : head_at * 64 + 64]
                if part < 2:
                    one, two = one * cos - two * sin, two * cos + one * sin
                if part == 0:
                    one, two = one * SCALE, two * SCALE
                row = part * GW + (head % GH) * HEAD_DIM
                qkv_ref[head // GH, row : row + 32, :] = one.astype(BF16)
                qkv_ref[head // GH, row + 32 : row + 64, :] = two.astype(BF16)


CHUNK = 256
CHUNKS = 2048 // CHUNK
PAIR = CHUNK // ROWS


def attend_kernel(q_ref, kv_ref, low_ref, wide_ref, totals_ref, s_ref):
    @pl.loop(0, GH)
    def _(h):
        at = pl.multiple_of(h * HEAD_DIM, HEAD_DIM)
        value_at = pl.multiple_of(h * HEAD_DIM + GW, HEAD_DIM)
        qt = jnp.concatenate([q_ref[i, pl.ds(at, HEAD_DIM), :] for i in range(4)], axis=1)
        top = jnp.full((8, 512), -jnp.inf, F32)
        for c in range(CHUNKS):
            keys = jnp.concatenate(
                [kv_ref[c * PAIR + i, pl.ds(at, HEAD_DIM), :].T for i in range(PAIR)], axis=0
            )
            scores = dot(keys, qt)
            s_ref[c * CHUNK : (c + 1) * CHUNK, :] = scores
            top = jnp.maximum(top, jnp.max(scores.reshape(CHUNK // 8, 8, 512), axis=0))
        top = jnp.max(top, axis=0, keepdims=True)
        total = jnp.zeros((8, 512), F32)
        acc = jnp.zeros((HEAD_DIM, 512), F32)
        for c in range(CHUNKS):
            p = jnp.exp(s_ref[c * CHUNK : (c + 1) * CHUNK, :] - top)
            total = total + jnp.sum(p.reshape(CHUNK // 8, 8, 512), axis=0)
            values = jnp.concatenate(
                [kv_ref[c * PAIR + i, pl.ds(value_at, HEAD_DIM), :] for i in range(PAIR)], axis=1
            )
            acc = acc + dot(values, p.astype(BF16))
        total = jnp.sum(total, axis=0, keepdims=True)
        out = acc / total
        totals_ref[h] = jnp.broadcast_to(top + jnp.log(total), (8, 512))
        for i in range(4):
            piece = out[:, i * ROWS : (i + 1) * ROWS]
            wide_ref[i, pl.ds(at, HEAD_DIM), :] = piece
            low_ref[i, pl.ds(at, HEAD_DIM), :] = piece.astype(BF16)


def attend_back_kernel(q_ref, kv_ref, wide_ref, totals_ref, do_ref, dq_ref, dkv_ref):
    @pl.loop(0, GH)
    def _(h):
        at = pl.multiple_of(h * HEAD_DIM, HEAD_DIM)
        value_at = pl.multiple_of(h * HEAD_DIM + GW, HEAD_DIM)
        out_at = pl.multiple_of(h * ROWS, ROWS)
        qt = jnp.concatenate([q_ref[i, pl.ds(at, HEAD_DIM), :] for i in range(4)], axis=1)
        dot_t = jnp.concatenate([do_ref[i, pl.ds(at, HEAD_DIM), :] for i in range(4)], axis=1)
        wide = jnp.concatenate([wide_ref[i, pl.ds(at, HEAD_DIM), :] for i in range(4)], axis=1)
        delta = jnp.sum(wide * dot_t.astype(F32), axis=0, keepdims=True)
        totals = totals_ref[h, 0:1, :]
        zero = jnp.zeros((512, HEAD_DIM), BF16)
        sides = jnp.concatenate(
            [
                jnp.concatenate([qt.T, zero], axis=1),
                jnp.concatenate([zero, dot_t.T], axis=1),
            ],
            axis=0,
        )

        def step(c, acc):
            keys_t = [kv_ref[c * PAIR + i, pl.ds(at, HEAD_DIM), :] for i in range(PAIR)]
            values_t = [kv_ref[c * PAIR + i, pl.ds(value_at, HEAD_DIM), :] for i in range(PAIR)]
            keys = jnp.concatenate([k.T for k in keys_t], axis=0)
            values = jnp.concatenate([v.T for v in values_t], axis=0)
            p = jnp.exp(dot(keys, qt) - totals)
            ds = (p * (dot(values, dot_t) - delta)).astype(BF16)
            both = jnp.concatenate([ds, p.astype(BF16)], axis=1)
            grads = dot(both, sides).astype(BF16)
            for i in range(PAIR):
                dkv_ref[c * PAIR + i, pl.ds(out_at, ROWS), :] = grads[i * ROWS : (i + 1) * ROWS]
            return acc + dot(jnp.concatenate(keys_t, axis=1), ds)

        acc = lax.fori_loop(0, CHUNKS, step, jnp.zeros((HEAD_DIM, 512), F32)) * SCALE
        for i in range(4):
            dq_ref[i, pl.ds(at, HEAD_DIM), :] = acc[:, i * ROWS : (i + 1) * ROWS].astype(BF16)


def mlp_kernel(
    ot_ref, x_ref, gain_ref, wo_ref, wu_ref, wd_ref,
    out_ref, hidden_ref, gate_up_ref, normed_ref, product_ref,
):
    attended = turned_low(ot_ref[...])
    hidden = x_ref[...].astype(F32) + dot(attended, wo_ref[...])
    hidden_ref[...] = hidden
    normalized, _ = norm_parts(hidden)
    normed = (normalized * gain_ref[...].astype(F32)).astype(BF16)
    normed_ref[...] = turned_low(normed)
    gate_up = dot(normed, wu_ref[...])
    gate_up_ref[...] = gate_up
    gate = gate_up[:, :FF]
    phi = 0.5 * (1.0 + lax.erf(gate * 0.5**0.5))
    product = (gate * phi * gate_up[:, FF:]).astype(BF16)
    product_ref[...] = turned_low(product)
    out_ref[...] = (hidden + dot(product, wd_ref[...])).astype(BF16)


def mlp_back_kernel(
    g_ref, hidden_ref, gate_up_ref, gain_ref, wo_ref, wu_ref, wd_ref,
    dot_ref, grad_hidden_ref, gg_ref, branch_ref, d_gain_ref,
):
    grad = g_ref[...]
    grad_product = dot_nt(grad, wd_ref[...])
    gate = gate_up_ref[:, :FF]
    up = gate_up_ref[:, FF:]
    phi = 0.5 * (1.0 + lax.erf(gate * 0.5**0.5))
    density = jnp.exp(-0.5 * gate * gate) * 0.3989422804014327
    grad_gate = (grad_product * up * (phi + gate * density)).astype(BF16)
    grad_up = (grad_product * gate * phi).astype(BF16)
    gg_ref[:, :FF] = grad_gate
    gg_ref[:, FF:] = grad_up
    grad_normed = dot_nt(grad_gate, wu_ref[:, :FF]) + dot_nt(grad_up, wu_ref[:, FF:])
    normalized, rstd = norm_parts(hidden_ref[...])
    part, d_gain = norm_back(grad_normed, normalized, rstd, gain_ref[...].astype(F32))
    d_gain_ref[...] = d_gain
    grad_hidden = grad.astype(F32) + part
    grad_hidden_ref[...] = grad_hidden
    branch = grad_hidden.astype(BF16)
    branch_ref[...] = branch
    dot_ref[...] = dot_nt(branch, wo_ref[...]).T.astype(BF16)


def qkv_back_kernel(
    dq_ref, dkv_ref, x_ref, gain_ref, w_ref, cos_ref, sin_ref, grad_hidden_ref,
    grad_x_ref, gp_out_ref, d_gain_ref, gp_ref,
):
    cos = cos_ref[...]
    sin = sin_ref[...]

    def back(one, two):
        return one * cos + two * sin, two * cos - one * sin

    for head in range(HEADS):
        group, inner = head // GH, head % GH
        at = inner * HEAD_DIM
        one = dq_ref[group, at : at + 32, :].astype(F32)
        two = dq_ref[group, at + 32 : at + 64, :].astype(F32)
        gq = back(one, two)
        rows = slice(inner * ROWS, (inner + 1) * ROWS)
        kv = (dkv_ref[2 * group, rows, :].astype(F32) + dkv_ref[2 * group + 1, rows, :].astype(F32)).T
        gk = back(kv[:32], kv[32:64])
        base = head * HEAD_DIM
        gp_ref[base : base + 32, :] = gq[0]
        gp_ref[base + 32 : base + 64, :] = gq[1]
        gp_ref[D + base : D + base + 32, :] = gk[0]
        gp_ref[D + base + 32 : D + base + 64, :] = gk[1]
        gp_ref[2 * D + base : 2 * D + base + 64, :] = kv[64:]
    grad_normed = jnp.zeros((ROWS, D), F32)
    for block in range(9):
        cols = slice(block * 256, (block + 1) * 256)
        gp = gp_ref[cols, :].T.astype(BF16)
        gp_out_ref[:, cols] = gp
        grad_normed = grad_normed + dot_nt(gp, w_ref[:, cols])
    normalized, rstd = norm_parts(x_ref[...].astype(F32))
    part, d_gain = norm_back(grad_normed, normalized, rstd, gain_ref[...].astype(F32))
    d_gain_ref[...] = d_gain
    grad_x_ref[...] = (grad_hidden_ref[...] + part).astype(BF16)


MLP_ROWS = 576
QKV_ROWS = 320
SUM_ROWS = MLP_ROWS + QKV_ROWS


def weight_product(out_ref, shard, at, left_ref, left_sib_ref, right_ref, right_sib_ref):
    height = left_ref.shape[2]
    core = lax.rem(lax.axis_index("ctx"), 2)
    own = left_ref[shard, core]
    other = left_sib_ref[shard]
    for block in range(right_ref.shape[1] // D):
        cols = slice(block * D, (block + 1) * D)
        both = dot(own, right_ref[:, cols]) + dot(other, right_sib_ref[:, cols])
        row = at + block * height
        out_ref[shard, row : row + height, :] = both.astype(BF16)


def mlp_weights_kernel(
    normed_ref, normed_sib, product_ref, product_sib, ot_ref, ot_sib,
    gg_ref, gg_sib, grad_ref, grad_sib, branch_ref, branch_sib, out_ref,
):
    @pl.loop(0, 4)
    def _(shard):
        weight_product(out_ref, shard, 0, normed_ref, normed_sib, gg_ref, gg_sib)
        weight_product(out_ref, shard, 288, ot_ref, ot_sib, branch_ref, branch_sib)
        weight_product(out_ref, shard, 384, product_ref, product_sib, grad_ref, grad_sib)
        out_ref[shard, 528:, :] = jnp.zeros((48, D), BF16)


def qkv_weights_kernel(normed_ref, normed_sib, gp_ref, gp_sib, gain_one_ref, gain_two_ref, out_ref):
    gains = jnp.concatenate(
        [gain_one_ref[...], gain_two_ref[...], jnp.zeros((30, D), F32)], axis=0
    ).astype(BF16)

    @pl.loop(0, 4)
    def _(shard):
        weight_product(out_ref, shard, 0, normed_ref, normed_sib, gp_ref, gp_sib)
        out_ref[shard, 288:, :] = gains


def here():
    return lax.axis_index("section"), lax.axis_index("ctx"), lax.axis_index("wshard")


def flip(index, delta):
    for bit in (1, 2, 4, 8):
        if delta & bit:
            index = index + bit - 2 * bit * lax.rem(index // bit, 2)
    return index


def greet(peers):
    barrier = pltpu.get_barrier_semaphore()
    for peer in peers:
        pl.semaphore_signal(barrier, inc=1, device_id=peer, device_id_type=MESH)
    pl.semaphore_wait(barrier, len(peers))


def remote(src, dst, send, recv, peer):
    return pltpu.make_async_remote_copy(
        src_ref=src, dst_ref=dst, send_sem=send, recv_sem=recv, device_id=peer, device_id_type=MESH
    )


class Lines:
    count = 96

    def __init__(self, send, recv):
        self.send, self.recv, self.used, self.waits = send, recv, 0, []

    def make(self, src, dst, peer):
        at = self.used
        self.used += 1
        return remote(src, dst, self.send.at[at], self.recv.at[at], peer)

    def put(self, src, dst, peer):
        copy = self.make(src, dst, peer)
        copy.start()
        return copy

    def keep(self, src, dst):
        at = self.used
        self.used += 1
        copy = pltpu.make_async_copy(src, dst, self.send.at[at])
        copy.start()
        return copy


SEMS = [DMA((Lines.count,)), DMA((Lines.count,))]
ids = iter(range(1, 64))


def exchange_call(kernel, args, outs, scratch, collective_id, name):
    return pl.pallas_call(
        kernel,
        out_shape=outs,
        in_specs=[ANY] * len(args),
        out_specs=jax.tree.map(lambda _: ANY, outs),
        scratch_shapes=SEMS + list(scratch),
        compiler_params=pltpu.CompilerParams(
            collective_id=collective_id, has_side_effects=True, vmem_limit_bytes=VMEM_LIMIT
        ),
        name=name,
    )(*args)


def sibling_of(s, c, z):
    return (s, flip(c, 1), z)


def z_peers():
    s, c, z = here()
    return [(s, c, lax.rem(z + r, 4)) for r in (1, 3, 2)]


class Gather:
    def __init__(self, lines, layer, own, got, full):
        s, c, z = here()
        rows = full.shape[1] // 2
        self.half = half = pl.ds(pl.multiple_of(lax.rem(c, 2) * rows, 16), rows)
        self.lines, self.full = lines, full
        self.sibling = sibling_of(s, c, z)
        peers = z_peers()
        first = lines.used
        for source, holds in ((own, s == layer), (got, s != layer)):
            lines.used = first

            @pl.when(holds)
            def _():
                self.over = [lines.put(source.at[half], full.at[z, half], peer) for peer in peers]
                self.mine = lines.put(source.at[half], full.at[z, half], self.sibling)
                self.kept = lines.keep(source.at[half], full.at[z, half])

        lines.used = first
        block = full.at[z, half]
        self.over = [lines.make(block, block, peer) for peer in peers]
        self.mine = lines.make(block, block, self.sibling)
        at = lines.used
        self.kept = pltpu.make_async_copy(block, block, lines.send.at[at])
        lines.used += 1

    def forward(self):
        _, _, z = here()
        self.passed = [self.mine]
        for copy, r in zip(self.over, (1, 3, 2)):
            copy.wait_recv()
            block = self.full.at[lax.rem(z + 4 - r, 4), self.half]
            self.passed.append(self.lines.put(block, block, self.sibling))

    def finish(self):
        self.kept.wait()
        for copy in self.over:
            copy.wait_send()
        for copy in self.passed:
            copy.wait()


def full_shapes(pairs):
    return [sds((4, *own.shape), BF16) for own, _ in pairs]


def split_refs(refs, *counts):
    refs = list(refs)
    out = []
    for count in counts:
        out.append(refs[:count])
        refs = refs[count:]
    return out


class Scatter:
    def __init__(self, lines, comb, got):
        s, c, z = here()
        self.copies = [
            lines.put(comb.at[peer[2]], got.at[i], peer) for i, peer in enumerate(z_peers())
        ]

    def finish(self):
        for copy in self.copies:
            copy.wait()


def scatter_shapes(combs):
    return [sds((3, *comb.shape[1:]), BF16) for comb in combs]


def start_kernel(*refs):
    weights, (gain,), got, (full, gains), (send, recv) = split_refs(refs, 4, 1, 4, 2, 2)
    s, c, z = here()
    lines = Lines(send, recv)
    beside = [(1 - s, c, z), (1 - s, flip(c, 8), z)]
    across = [(1 - s, c, lax.rem(z + r, 4)) for r in range(4)]
    greet([sibling_of(s, c, z), *z_peers(), *across, beside[1]])
    copies = []

    def share(weight, target):
        rows, cols = weight.shape[0] // 2, weight.shape[1] // 2
        at = (
            pl.ds(pl.multiple_of(lax.rem(c, 2) * rows, 16), rows),
            pl.ds(pl.multiple_of(c // 8 * cols, 128), cols),
        )
        return [lines.put(weight.at[at], target.at[at], peer) for peer in beside]

    first = share(weights[0], got[0])
    copies += [lines.put(gain, gains.at[s, z], peer) for peer in (*z_peers(), *across)]
    kept = lines.keep(gain, gains.at[s, z])
    for i in range(1, 4):
        copies += share(weights[i], got[i])

    @pl.when(s == 1)
    def _():
        for copy in first:
            copy.wait_recv()

    gather = Gather(lines, 0, weights[0], got[0], full)
    gather.forward()
    gather.finish()

    @pl.when(s == 0)
    def _():
        for copy in first:
            copy.wait_recv()

    for copy in first:
        copy.wait_send()
    kept.wait()
    for copy in copies:
        copy.wait()


def start(weights, gain):
    outs = (
        *[sds(w.shape, BF16) for w in weights],
        sds((4, *weights[0].shape), BF16),
        sds((2, 4, *gain.shape), BF16),
    )
    res = exchange_call(start_kernel, (*weights, gain), outs, [], next(ids), "start")
    return res[:4], res[4], res[5]


def gather_kernel(layer, count, *refs):
    own, got, full, (send, recv) = split_refs(refs, count, count, count, 2)
    lines = Lines(send, recv)
    greet([sibling_of(*here()), *z_peers()])
    gathers = [Gather(lines, layer, *three) for three in zip(own, got, full)]
    for gather in gathers:
        gather.forward()
    for gather in gathers:
        gather.finish()


def gather(layer, pairs):
    args = [own for own, _ in pairs] + [got for _, got in pairs]
    kernel = functools.partial(gather_kernel, layer, len(pairs))
    return exchange_call(kernel, args, full_shapes(pairs), [], next(ids), "gather")


def spread_kernel(layer, count, *refs):
    (qkv_ref,), own_w, got_w, (q_ref, kv_ref), full, (send, recv) = split_refs(
        refs, 1, count, count, 2, count, 2
    )
    s, c, z = here()
    lines = Lines(send, recv)
    sibling = sibling_of(s, c, z)
    peers = {delta: (s, flip(c, delta), z) for delta in range(2, CTX, 2)}
    greet([sibling, *peers.values(), *(z_peers() if count else [])])
    kv_rows = pl.ds(GW, 2 * GW)
    q_rows = pl.ds(0, GW)
    order = [14, 10, 12, 8, 6, 4, 2]
    kv_sends, q_sends = {}, []
    for delta in order:
        peer = peers[delta]
        kv_sends[delta] = lines.put(qkv_ref.at[peer[1] // 4, kv_rows], kv_ref.at[c], peer)
        if delta % 4 == 0:
            q_sends.append(lines.put(qkv_ref.at[peer[1] // 4, q_rows], q_ref.at[c // 4], peer))
    gathers = [Gather(lines, layer, *three) for three in zip(own_w, got_w, full)]
    passed = [lines.put(qkv_ref.at[c // 4, kv_rows], kv_ref.at[c], sibling)]
    kept = [
        lines.keep(qkv_ref.at[c // 4, kv_rows], kv_ref.at[c]),
        lines.keep(qkv_ref.at[c // 4, q_rows], q_ref.at[c // 4]),
    ]
    for delta in reversed(order):
        kv_sends[delta].wait_recv()
        block = kv_ref.at[flip(c, delta)]
        passed.append(lines.put(block, block, sibling))
    for copy in kept:
        copy.wait()
    for copy in q_sends:
        copy.wait()
    for copy in kv_sends.values():
        copy.wait_send()
    for copy in passed:
        copy.wait()
    for gather in gathers:
        gather.forward()
    for gather in gathers:
        gather.finish()


def spread(qkv, layer, pairs):
    args = [qkv] + [own for own, _ in pairs] + [got for _, got in pairs]
    outs = [sds((4, GW, ROWS), BF16), sds((CTX, 2 * GW, ROWS), BF16)] + full_shapes(pairs)
    kernel = functools.partial(spread_kernel, layer, len(pairs))
    res = exchange_call(kernel, args, outs, [], next(ids), "spread")
    return res[0], res[1], res[2:]


class Pair:
    def __init__(self, lines, src, dst):
        s, c, z = here()
        if len(src.shape) == 4:
            src = src.at[:, 1 - lax.rem(c, 2)]
        self.copy = lines.put(src, dst, sibling_of(s, c, z))

    def finish(self):
        self.copy.wait()


def pair_shapes(arrays):
    return [sds((a.shape[0], *a.shape[2:]) if a.ndim == 4 else a.shape, BF16) for a in arrays]


def turn_kernel(layer, count, pairs, *refs):
    (x_ref,), own_w, got_w, sent, (o_ref,), full, taken, (send, recv) = split_refs(
        refs, 1, count, count, pairs, 1, count, pairs, 2
    )
    s, c, z = here()
    lines = Lines(send, recv)
    peers = [(s, flip(c, delta), z) for delta in (4, 8, 12)]
    greet(peers + ([sibling_of(s, c, z)] if count or pairs else []) + (z_peers() if count else []))
    copies = [lines.put(x_ref.at[peer[1] // 4], o_ref.at[c // 4], peer) for peer in peers]
    gathers = [Gather(lines, layer, *three) for three in zip(own_w, got_w, full)]
    moved = [Pair(lines, src, dst) for src, dst in zip(sent, taken)]
    lines.keep(x_ref.at[c // 4], o_ref.at[c // 4]).wait()
    for copy in copies:
        copy.wait()
    for gather in gathers:
        gather.forward()
    for work in gathers + moved:
        work.finish()


def turn(x, layer=0, pairs=(), acts=()):
    args = [x] + [own for own, _ in pairs] + [got for _, got in pairs] + list(acts)
    outs = [sds((4, GW, ROWS), BF16)] + full_shapes(pairs) + pair_shapes(acts)
    kernel = functools.partial(turn_kernel, layer, len(pairs), len(acts))
    res = exchange_call(kernel, args, outs, [], next(ids), "turn")
    return res[0], res[1 : 1 + len(pairs)], res[1 + len(pairs) :]


def pair_kernel(count, *refs):
    sent, taken, (send, recv) = split_refs(refs, count, count, 2)
    lines = Lines(send, recv)
    greet([sibling_of(*here())])
    for work in [Pair(lines, src, dst) for src, dst in zip(sent, taken)]:
        work.finish()


def pair(acts):
    kernel = functools.partial(pair_kernel, len(acts))
    return exchange_call(kernel, acts, pair_shapes(acts), [], next(ids), "pair")


def scatter_kernel(count, *refs):
    combs, got, (send, recv) = split_refs(refs, count, count, 2)
    lines = Lines(send, recv)
    greet(z_peers())
    for work in [Scatter(lines, *two) for two in zip(combs, got)]:
        work.finish()


def scatter(combs):
    kernel = functools.partial(scatter_kernel, len(combs))
    return exchange_call(kernel, combs, scatter_shapes(combs), [], next(ids), "scatter")


def return_kernel(count, *refs):
    (dq_ref, dkv_ref), combs, (dqo_ref, sums_ref), got, (send, recv, mine, theirs, total) = split_refs(
        refs, 2, count, 2, count, 5
    )
    s, c, z = here()
    lines = Lines(send, recv)
    core = lax.rem(c, 2)
    sibling = sibling_of(s, c, z)
    peers = {delta: (s, flip(c, delta), z) for delta in range(2, CTX, 2)}
    greet([sibling, *peers.values(), *(z_peers() if count else [])])
    passed = [lines.put(dkv_ref.at[2 * i + 1 - core], theirs.at[i], sibling) for i in range(8)]
    loads = [lines.keep(dkv_ref.at[2 * i + core], mine.at[i]) for i in range(8)]
    sends = [
        lines.put(dq_ref.at[peers[delta][1] // 4], dqo_ref.at[c // 4], peers[delta]) for delta in (4, 8, 12)
    ]
    scatters = [Scatter(lines, *two) for two in zip(combs, got)]
    kept = [lines.keep(dq_ref.at[c // 4], dqo_ref.at[c // 4])]
    for i in range(8):
        loads[i].wait()
        passed[i].wait()
        total[i] = (mine[i].astype(F32) + theirs[i].astype(F32)).astype(BF16)
    for delta in (14, 10, 12, 8, 6, 4, 2):
        sends.append(lines.put(total.at[peers[delta][1] // 2], sums_ref.at[c // 2], peers[delta]))
    kept.append(lines.keep(total.at[c // 2], sums_ref.at[c // 2]))
    for copy in kept + sends:
        copy.wait()
    for work in scatters:
        work.finish()


def give_back(dq, dkv, combs):
    block = pltpu.VMEM((8, 2 * GW, ROWS), BF16)
    outs = [sds((4, GW, ROWS), BF16), sds((8, 2 * GW, ROWS), BF16)] + scatter_shapes(combs)
    kernel = functools.partial(return_kernel, len(combs))
    res = exchange_call(kernel, [dq, dkv, *combs], outs, [block] * 3, next(ids), "give_back")
    return res[0], res[1], res[2:]


QUARTER = SUM_ROWS // 4


def finish_kernel(*refs):
    layers = split_refs(refs[:8], 4, 4)
    fin, send, recv, load, terms, own_sum, far_sum, parts, red = refs[8:]
    s, c, z = here()
    lines = Lines(send, recv)
    core = lax.rem(c, 2)
    sibling = sibling_of(s, c, z)
    near = {delta: (s, flip(c, delta), z) for delta in range(2, CTX, 2)}
    far = {delta: (1 - s, flip(c, delta), z) for delta in range(0, CTX, 2)}
    greet([sibling, *near.values(), *far.values()])

    def fill(target, layer):
        comb_m, got_m, comb_q, got_q = layer
        for comb, got, at, rows in ((comb_m, got_m, 0, MLP_ROWS), (comb_q, got_q, MLP_ROWS, QKV_ROWS)):
            copies = [pltpu.make_async_copy(comb.at[z], terms.at[0, pl.ds(at, rows)], load.at[0])]
            copies += [
                pltpu.make_async_copy(got.at[i], terms.at[i + 1, pl.ds(at, rows)], load.at[i + 1])
                for i in range(3)
            ]
            for copy in copies:
                copy.start()
            for copy in copies:
                copy.wait()
        for at in range(0, SUM_ROWS, 128):
            rows = slice(at, at + 128)
            both = terms[0, rows].astype(F32) + terms[1, rows].astype(F32)
            both += terms[2, rows].astype(F32) + terms[3, rows].astype(F32)
            target[rows] = both.astype(BF16)

    @pl.when(s == 0)
    def _():
        fill(far_sum, layers[1])

    @pl.when(s == 1)
    def _():
        fill(far_sum, layers[0])

    def block(at):
        rows = pl.ds(pl.multiple_of(lax.rem(at // 2, 4) * QUARTER, 16), QUARTER)
        return rows, pl.ds(pl.multiple_of(at // 8 * (D // 2), 128), D // 2)

    sends = [lines.put(far_sum.at[block(peer[1])], parts.at[8 + c // 2], peer) for peer in far.values()]

    @pl.when(s == 0)
    def _():
        fill(own_sum, layers[0])

    @pl.when(s == 1)
    def _():
        fill(own_sum, layers[1])

    sends += [lines.put(own_sum.at[block(peer[1])], parts.at[c // 2], peer) for peer in near.values()]
    lines.keep(own_sum.at[block(c)], parts.at[c // 2]).wait()
    for copy in sends:
        copy.wait()
    for at in range(0, QUARTER, 112):
        rows = slice(at, at + 112)
        total = parts[0, rows].astype(F32)
        for i in range(1, 16):
            total += parts[i, rows].astype(F32)
        red[rows] = total.astype(BF16)
    target = fin.at[core]
    kept = lines.keep(red, target.at[block(c)])
    passed = [lines.put(red, target.at[block(c)], sibling)]
    order = [14, 10, 12, 8, 6, 4, 2]
    shown = {delta: lines.put(red, target.at[block(c)], near[delta]) for delta in order}
    for delta in reversed(order):
        shown[delta].wait_recv()
        piece = target.at[block(flip(c, delta))]
        passed.append(lines.put(piece, piece, sibling))
    kept.wait()
    for copy in shown.values():
        copy.wait_send()
    for copy in passed:
        copy.wait()


def finish(zero, one):
    scratch = [
        DMA((4,)),
        pltpu.VMEM((4, SUM_ROWS, D), BF16),
        pltpu.VMEM((SUM_ROWS, D), BF16),
        pltpu.VMEM((SUM_ROWS, D), BF16),
        pltpu.VMEM((16, QUARTER, D // 2), BF16),
        pltpu.VMEM((QUARTER, D // 2), BF16),
    ]
    return exchange_call(
        finish_kernel, [*zero, *one], sds((2, SUM_ROWS, D), BF16), scratch, next(ids), "finish"
    )


def rope_tables():
    positions = (lax.axis_index("ctx") * ROWS + lax.iota(jnp.int32, ROWS)).astype(F32)
    frequency = 1.0 / 160000.0 ** (jnp.arange(HEAD_DIM // 2, dtype=F32) * 2.0 / HEAD_DIM)
    angles = frequency[:, None] * positions[None, :]
    return jnp.cos(angles), jnp.sin(angles)


def forward_layer(layer, x, gains, w_qkv, shards, tables):
    qkv, normed = compute_call(
        qkv_kernel,
        (x, gains[0], w_qkv, *tables),
        (sds((4, 3 * GW, ROWS), BF16), sds((D, ROWS), BF16)),
        name="norm_qkv",
    )
    q, kv, (w_up,) = spread(qkv, layer, [shards[2]])
    low, wide, totals = compute_call(
        attend_kernel,
        (q, kv),
        (sds((4, GW, ROWS), BF16), sds((4, GW, ROWS), F32), sds((GH, 8, 512), F32)),
        [pltpu.VMEM((2048, 512), F32)],
        name="attend",
    )
    ot, (w_out, w_down), _ = turn(low, layer, [shards[1], shards[3]])
    ot = ot.reshape(D, ROWS)
    w_out, w_up, w_down = w_out.reshape(D, D), w_up.reshape(D, 2 * FF), w_down.reshape(FF, D)
    out, hidden, gate_up, normed_two, product = compute_call(
        mlp_kernel,
        (ot, x, gains[1], w_out, w_up, w_down),
        (sds((ROWS, D), BF16), sds((ROWS, D), F32), sds((ROWS, 2 * FF), F32),
         sds((D, ROWS), BF16), sds((FF, ROWS), BF16)),
        name="mlp",
    )
    return out, (w_out, w_up, w_down), (x, normed, q, kv, wide, totals, ot, hidden, gate_up, normed_two, product)


def by_core(a):
    return a.reshape(4, 2, -1, ROWS)


def interleave(own, other):
    return [a for both in zip(own, other) for a in both]


def backward_layer(grad, stored, gains, w_qkv, weights, tables, before=()):
    w_out, w_up, w_down = weights
    x, normed, q, kv, wide, totals, ot, hidden, gate_up, normed_two, product = stored
    d_ot, grad_hidden, gg, branch, d_gain_two = compute_call(
        mlp_back_kernel,
        (grad, hidden, gate_up, gains[1], w_out, w_up, w_down),
        (sds((D, ROWS), BF16), sds((ROWS, D), F32), sds((ROWS, 2 * FF), BF16),
         sds((ROWS, D), BF16), sds((1, D), F32)),
        name="mlp_back",
    )
    acts = [by_core(normed_two), by_core(product), by_core(ot), gg, grad, branch]
    d_o, _, taken = turn(d_ot.reshape(4, GW, ROWS), acts=[*acts, *before[:2]])
    dq, dkv = compute_call(
        attend_back_kernel,
        (q, kv, wide, totals, d_o),
        (sds((4, GW, ROWS), BF16), sds((CTX, 2 * GW, ROWS), BF16)),
        name="attend_back",
    )
    combs = [
        compute_call(
            mlp_weights_kernel, interleave(acts, taken), sds((4, MLP_ROWS, D), BF16), name="mlp_weights"
        )
    ]
    if before:
        combs.append(qkv_weights(before, taken[len(acts) :]))
    dq, dkv, got = give_back(dq, dkv, combs)
    grad_x, gp, d_gain_one = compute_call(
        qkv_back_kernel,
        (dq, dkv, x, gains[0], w_qkv, *tables, grad_hidden),
        (sds((ROWS, D), BF16), sds((ROWS, 3 * D), BF16), sds((1, D), F32)),
        [pltpu.VMEM((3 * D, ROWS), F32)],
        name="qkv_back",
    )
    return grad_x, (by_core(normed), gp, d_gain_one, d_gain_two), combs, got


def qkv_weights(left, taken):
    return compute_call(
        qkv_weights_kernel,
        (*interleave(left[:2], taken), *left[2:]),
        sds((4, QKV_ROWS, D), BF16),
        name="qkv_weights",
    )


def swap_layers(zero, one):
    first = lax.axis_index("section") == 0
    other = lax.ppermute(jnp.where(first, one, zero), "section", [(0, 1), (1, 0)])
    kept = jnp.where(first, zero, one)
    return jnp.stack([jnp.where(first, kept, other), jnp.where(first, other, kept)])[None, :, None]


def local(inputs, cotangent, attn_gain, qkv_weight, out_weight, mlp_gain, up_weight, down_weight):
    first = lax.axis_index("section") == 0
    x = jnp.where(first, inputs[0, 0], inputs[1, 0])
    cot = jnp.where(first, cotangent[0, 0], cotangent[1, 0])
    own = [qkv_weight[0], out_weight[0], up_weight[0], down_weight[0]]
    gain = jnp.pad(jnp.concatenate([attn_gain, mlp_gain], axis=0), ((0, 14), (0, 64)))
    got, w_zero, gains = start(own, gain)
    shards = list(zip(own, got))
    gains = [
        [gains[layer, :, row, :192].reshape(1, D) for row in range(2)] for layer in range(2)
    ]
    tables = rope_tables()
    w_zero = w_zero.reshape(D, 3 * D)
    mid, weights_zero, stored_zero = forward_layer(0, x, gains[0], w_zero, shards, tables)
    (w_one,) = gather(1, [shards[0]])
    w_one = w_one.reshape(D, 3 * D)
    end, weights_one, stored_one = forward_layer(1, mid, gains[1], w_one, shards, tables)
    grad_mid, left_one, combs_one, got_one = backward_layer(
        cot, stored_one, gains[1], w_one, weights_one, tables
    )
    grad_start, left_zero, combs, got = backward_layer(
        grad_mid, stored_zero, gains[0], w_zero, weights_zero, tables, left_one
    )
    activations = swap_layers(mid, end)
    input_grads = swap_layers(grad_start, grad_mid)
    comb_last = qkv_weights(left_zero, pair(list(left_zero[:2])))
    (got_last,) = scatter([comb_last])
    fin = finish(
        [combs[0], got[0], comb_last, got_last], [combs_one[0], got_one[0], combs[1], got[1]]
    ).astype(F32)

    def columns(at):
        return fin[:, at : at + 288].reshape(2, 3, 96, D).transpose(0, 2, 1, 3).reshape(192, 3 * D)

    gain_at = MLP_ROWS + 288
    gain_sums = lax.dynamic_slice_in_dim(
        fin[0, gain_at : gain_at + 2] + fin[1, gain_at : gain_at + 2], lax.axis_index("wshard") * 192, 192, 1
    )
    return (
        activations,
        input_grads,
        gain_sums[0:1],
        columns(MLP_ROWS)[None],
        fin[:, 288:384].reshape(1, 192, D),
        gain_sums[1:2],
        columns(0)[None],
        fin[:, 384:528].reshape(1, 288, D),
    )


def solution(mesh):
    global ids
    ids = iter(range(1, 64))
    placed = (
        P(None, "wshard", "ctx", None),
        P(None, "wshard", "ctx", None),
        P("section", "wshard"),
        P("section", "wshard", None),
        P("section", "wshard", None),
        P("section", "wshard"),
        P("section", "wshard", None),
        P("section", "wshard", None),
    )
    return jax.shard_map(
        local,
        mesh=mesh,
        in_specs=placed,
        out_specs=(
            P("section", None, "wshard", "ctx", None),
            P("section", None, "wshard", "ctx", None),
            P("section", "wshard"),
            P("section", "wshard", None),
            P("section", "wshard", None),
            P("section", "wshard"),
            P("section", "wshard", None),
            P("section", "wshard", None),
        ),
        check_vma=False,
    )
```

```python
import functools

import jax
import jax.numpy as jnp
from jax import lax
from jax.experimental import pallas as pl
from jax.experimental.pallas import tpu as pltpu
from jax.sharding import PartitionSpec as P

D = 768
HEADS = 12
HEAD_DIM = 64
FF = 1152
ROWS = 128
GROUPS = 4
GH = HEADS // GROUPS
GW = GH * HEAD_DIM
CTX = 16
SCALE = HEAD_DIM ** (-0.5)
F32 = jnp.float32
BF16 = jnp.bfloat16
MESH = pl.DeviceIdType.MESH
DMA = pltpu.SemaphoreType.DMA
ANY = pl.BlockSpec(memory_space=pl.ANY)
VM = pl.BlockSpec(memory_space=pltpu.VMEM)
VMEM_LIMIT = 56 * 1024 * 1024


def dot(a, b):
    return jnp.dot(a, b, preferred_element_type=F32)


def dot_nt(a, b):
    return lax.dot_general(a, b, (((1,), (1,)), ((), ())), preferred_element_type=F32)


def sds(shape, dtype):
    return jax.ShapeDtypeStruct(shape, dtype)


def compute_call(kernel, args, outs, scratch=(), name=None, far=0):
    return pl.pallas_call(
        kernel,
        out_shape=outs,
        in_specs=[VM] * (len(args) - far) + [ANY] * far,
        out_specs=jax.tree.map(lambda _: VM, outs),
        scratch_shapes=list(scratch),
        compiler_params=pltpu.CompilerParams(vmem_limit_bytes=VMEM_LIMIT),
        name=name,
    )(*args)


def fetch(src, dst, sem):
    copy = pltpu.make_async_copy(src, dst, sem)
    copy.start()
    return copy


def turned_low(x):
    return x.astype(F32).T.astype(BF16)


def norm_parts(source):
    centered = source - jnp.mean(source, axis=-1, keepdims=True)
    variance = jnp.mean(centered * centered, axis=-1, keepdims=True)
    rstd = lax.rsqrt(variance + 1e-05)
    return centered * rstd, rstd


def norm_back(grad, normalized, rstd, gain):
    inner = grad * gain
    mean_one = jnp.mean(inner, axis=-1, keepdims=True)
    mean_two = jnp.mean(inner * normalized, axis=-1, keepdims=True)
    grad_gain = jnp.sum(grad * normalized, axis=0, keepdims=True)
    return rstd * (inner - mean_one - normalized * mean_two), grad_gain


def split_refs(refs, *counts):
    refs = list(refs)
    out = []
    for count in counts:
        out.append(refs[:count])
        refs = refs[count:]
    return out


def qkv_kernel(layer, x_ref, gain_ref, cos_ref, sin_ref, w_all, qkv_ref, normed_ref, w_ref, sem):
    load = fetch(w_all.at[layer], w_ref, sem)
    normalized, _ = norm_parts(x_ref[...].astype(F32))
    normed = (normalized * gain_ref[...].astype(F32)).astype(BF16)
    normed_ref[...] = turned_low(normed)
    load.wait()
    cos = cos_ref[...]
    sin = sin_ref[...]
    for part in range(3):
        for block in range(3):
            at = part * D + block * 256
            turned = dot(normed, w_ref[:, at : at + 256]).T
            for head_at in range(4):
                head = block * 4 + head_at
                one = turned[head_at * 64 : head_at * 64 + 32]
                two = turned[head_at * 64 + 32 : head_at * 64 + 64]
                if part < 2:
                    one, two = one * cos - two * sin, two * cos + one * sin
                if part == 0:
                    one, two = one * SCALE, two * SCALE
                row = part * GW + (head % GH) * HEAD_DIM
                qkv_ref[head // GH, row : row + 32, :] = one.astype(BF16)
                qkv_ref[head // GH, row + 32 : row + 64, :] = two.astype(BF16)


CHUNK = 256
CHUNKS = 2048 // CHUNK
PAIR = CHUNK // ROWS


def attend_kernel(q_ref, kv_ref, low_ref, wide_ref, totals_ref, s_ref):
    @pl.loop(0, GH)
    def _(h):
        at = pl.multiple_of(h * HEAD_DIM, HEAD_DIM)
        value_at = pl.multiple_of(h * HEAD_DIM + GW, HEAD_DIM)
        qt = jnp.concatenate([q_ref[i, pl.ds(at, HEAD_DIM), :] for i in range(4)], axis=1)
        top = jnp.full((8, 512), -jnp.inf, F32)
        for c in range(CHUNKS):
            keys = jnp.concatenate(
                [kv_ref[c * PAIR + i, pl.ds(at, HEAD_DIM), :].T for i in range(PAIR)], axis=0
            )
            scores = dot(keys, qt)
            s_ref[c * CHUNK : (c + 1) * CHUNK, :] = scores
            top = jnp.maximum(top, jnp.max(scores.reshape(CHUNK // 8, 8, 512), axis=0))
        top = jnp.max(top, axis=0, keepdims=True)
        total = jnp.zeros((8, 512), F32)
        acc = jnp.zeros((HEAD_DIM, 512), F32)
        for c in range(CHUNKS):
            p = jnp.exp(s_ref[c * CHUNK : (c + 1) * CHUNK, :] - top)
            total = total + jnp.sum(p.reshape(CHUNK // 8, 8, 512), axis=0)
            values = jnp.concatenate(
                [kv_ref[c * PAIR + i, pl.ds(value_at, HEAD_DIM), :] for i in range(PAIR)], axis=1
            )
            acc = acc + dot(values, p.astype(BF16))
        total = jnp.sum(total, axis=0, keepdims=True)
        out = acc / total
        totals_ref[h] = jnp.broadcast_to(top + jnp.log(total), (8, 512))
        for i in range(4):
            piece = out[:, i * ROWS : (i + 1) * ROWS]
            wide_ref[i, pl.ds(at, HEAD_DIM), :] = piece
            low_ref[i, pl.ds(at, HEAD_DIM), :] = piece.astype(BF16)


def attend_back_kernel(q_ref, kv_ref, wide_ref, totals_ref, do_ref, dq_ref, dkv_ref):
    @pl.loop(0, GH)
    def _(h):
        at = pl.multiple_of(h * HEAD_DIM, HEAD_DIM)
        value_at = pl.multiple_of(h * HEAD_DIM + GW, HEAD_DIM)
        out_at = pl.multiple_of(h * ROWS, ROWS)
        qt = jnp.concatenate([q_ref[i, pl.ds(at, HEAD_DIM), :] for i in range(4)], axis=1)
        dot_t = jnp.concatenate([do_ref[i, pl.ds(at, HEAD_DIM), :] for i in range(4)], axis=1)
        wide = jnp.concatenate([wide_ref[i, pl.ds(at, HEAD_DIM), :] for i in range(4)], axis=1)
        delta = jnp.sum(wide * dot_t.astype(F32), axis=0, keepdims=True)
        totals = totals_ref[h, 0:1, :]
        zero = jnp.zeros((512, HEAD_DIM), BF16)
        sides = jnp.concatenate(
            [
                jnp.concatenate([qt.T, zero], axis=1),
                jnp.concatenate([zero, dot_t.T], axis=1),
            ],
            axis=0,
        )

        def step(c, acc):
            keys_t = [kv_ref[c * PAIR + i, pl.ds(at, HEAD_DIM), :] for i in range(PAIR)]
            values_t = [kv_ref[c * PAIR + i, pl.ds(value_at, HEAD_DIM), :] for i in range(PAIR)]
            keys = jnp.concatenate([k.T for k in keys_t], axis=0)
            values = jnp.concatenate([v.T for v in values_t], axis=0)
            p = jnp.exp(dot(keys, qt) - totals)
            ds = (p * (dot(values, dot_t) - delta)).astype(BF16)
            both = jnp.concatenate([ds, p.astype(BF16)], axis=1)
            grads = dot(both, sides).astype(BF16)
            for i in range(PAIR):
                dkv_ref[c * PAIR + i, pl.ds(out_at, ROWS), :] = grads[i * ROWS : (i + 1) * ROWS]
            return acc + dot(jnp.concatenate(keys_t, axis=1), ds)

        acc = lax.fori_loop(0, CHUNKS, step, jnp.zeros((HEAD_DIM, 512), F32)) * SCALE
        for i in range(4):
            dq_ref[i, pl.ds(at, HEAD_DIM), :] = acc[:, i * ROWS : (i + 1) * ROWS].astype(BF16)


def mlp_kernel(
    layer, ot_ref, x_ref, gain_ref, wo_all, wu_all, wd_all,
    out_ref, hidden_ref, gate_up_ref, normed_ref, product_ref, wo_ref, wu_ref, wd_ref, sem,
):
    loads = [
        fetch(src.at[layer], dst, sem.at[i])
        for i, (src, dst) in enumerate([(wo_all, wo_ref), (wu_all, wu_ref), (wd_all, wd_ref)])
    ]
    attended = turned_low(ot_ref[...])
    loads[0].wait()
    hidden = x_ref[...].astype(F32) + dot(attended, wo_ref[...])
    hidden_ref[...] = hidden
    normalized, _ = norm_parts(hidden)
    normed = (normalized * gain_ref[...].astype(F32)).astype(BF16)
    normed_ref[...] = turned_low(normed)
    loads[1].wait()
    gate_up = dot(normed, wu_ref[...])
    gate_up_ref[...] = gate_up
    gate = gate_up[:, :FF]
    phi = 0.5 * (1.0 + lax.erf(gate * 0.5**0.5))
    product = (gate * phi * gate_up[:, FF:]).astype(BF16)
    product_ref[...] = turned_low(product)
    loads[2].wait()
    out_ref[...] = (hidden + dot(product, wd_ref[...])).astype(BF16)


def mlp_back_kernel(
    layer, g_ref, hidden_ref, gate_up_ref, gain_ref, wo_all, wu_all, wd_all,
    dot_ref, grad_hidden_ref, gg_ref, branch_ref, d_gain_ref, wo_ref, wu_ref, wd_ref, sem,
):
    loads = [
        fetch(src.at[layer], dst, sem.at[i])
        for i, (src, dst) in enumerate([(wd_all, wd_ref), (wu_all, wu_ref), (wo_all, wo_ref)])
    ]
    grad = g_ref[...]
    loads[0].wait()
    grad_product = dot_nt(grad, wd_ref[...])
    gate = gate_up_ref[:, :FF]
    up = gate_up_ref[:, FF:]
    phi = 0.5 * (1.0 + lax.erf(gate * 0.5**0.5))
    density = jnp.exp(-0.5 * gate * gate) * 0.3989422804014327
    grad_gate = (grad_product * up * (phi + gate * density)).astype(BF16)
    grad_up = (grad_product * gate * phi).astype(BF16)
    gg_ref[:, :FF] = grad_gate
    gg_ref[:, FF:] = grad_up
    loads[1].wait()
    grad_normed = dot_nt(grad_gate, wu_ref[:, :FF]) + dot_nt(grad_up, wu_ref[:, FF:])
    normalized, rstd = norm_parts(hidden_ref[...])
    part, d_gain = norm_back(grad_normed, normalized, rstd, gain_ref[...].astype(F32))
    d_gain_ref[...] = d_gain
    grad_hidden = grad.astype(F32) + part
    grad_hidden_ref[...] = grad_hidden
    branch = grad_hidden.astype(BF16)
    branch_ref[...] = branch
    loads[2].wait()
    dot_ref[...] = dot_nt(branch, wo_ref[...]).T.astype(BF16)


def qkv_back_kernel(
    layer, dq_ref, dkv_ref, x_ref, gain_ref, cos_ref, sin_ref, grad_hidden_ref, gain_two_ref, w_all,
    grad_x_ref, gp_out_ref, gains_ref, gp_ref, w_ref, sem,
):
    load = fetch(w_all.at[layer], w_ref, sem)
    cos = cos_ref[...]
    sin = sin_ref[...]

    def back(one, two):
        return one * cos + two * sin, two * cos - one * sin

    for head in range(HEADS):
        group, inner = head // GH, head % GH
        at = inner * HEAD_DIM
        one = dq_ref[group, at : at + 32, :].astype(F32)
        two = dq_ref[group, at + 32 : at + 64, :].astype(F32)
        gq = back(one, two)
        rows = slice(inner * ROWS, (inner + 1) * ROWS)
        kv = (dkv_ref[2 * group, rows, :].astype(F32) + dkv_ref[2 * group + 1, rows, :].astype(F32)).T
        gk = back(kv[:32], kv[32:64])
        base = head * HEAD_DIM
        gp_ref[base : base + 32, :] = gq[0]
        gp_ref[base + 32 : base + 64, :] = gq[1]
        gp_ref[D + base : D + base + 32, :] = gk[0]
        gp_ref[D + base + 32 : D + base + 64, :] = gk[1]
        gp_ref[2 * D + base : 2 * D + base + 64, :] = kv[64:]
    load.wait()
    grad_normed = jnp.zeros((ROWS, D), F32)
    for block in range(9):
        cols = slice(block * 256, (block + 1) * 256)
        gp = gp_ref[cols, :].T.astype(BF16)
        gp_out_ref[:, cols] = gp
        grad_normed = grad_normed + dot_nt(gp, w_ref[:, cols])
    normalized, rstd = norm_parts(x_ref[...].astype(F32))
    part, d_gain = norm_back(grad_normed, normalized, rstd, gain_ref[...].astype(F32))
    gains_ref[...] = jnp.concatenate(
        [d_gain, gain_two_ref[...], jnp.zeros((14, D), F32)], axis=0
    ).astype(BF16)
    grad_x_ref[...] = (grad_hidden_ref[...] + part).astype(BF16)


MLP_ROWS = 576
QKV_ROWS = 320
SUM_ROWS = MLP_ROWS + QKV_ROWS


def load_rows(sems, own, rest, left, right):
    section = lax.axis_index("section")
    core = lax.rem(lax.axis_index("ctx"), 2)

    def lanes(i):
        return left.at[:, :, pl.ds(i * ROWS, ROWS)]

    def rows(i):
        return right.at[pl.ds(i * ROWS, ROWS)]

    for layer, (a, g) in enumerate(own):

        @pl.when(section == layer)
        def _():
            fetch(a.at[:, core], lanes(0), sems.at[0])
            fetch(g, rows(0), sems.at[1])

    (a_sib, a_far, a_both), (g_sib, g_far, g_both) = rest
    copies = [
        fetch(a_sib, lanes(1), sems.at[2]),
        fetch(a_far.at[:, core], lanes(2), sems.at[3]),
        fetch(a_both, lanes(3), sems.at[4]),
        fetch(g_sib, rows(1), sems.at[5]),
        fetch(g_far, rows(2), sems.at[6]),
        fetch(g_both, rows(3), sems.at[7]),
    ]
    copies.append(pltpu.make_async_copy(a_sib, lanes(0), sems.at[0]))
    copies.append(pltpu.make_async_copy(g_sib, rows(0), sems.at[1]))
    return copies


def weight_product(out_ref, at, left, right):
    height = left.shape[1]

    @pl.loop(0, 4)
    def _(shard):
        for block in range(right.shape[1] // D):
            row = at + block * height
            both = dot(left[shard], right[:, block * D : (block + 1) * D])
            out_ref[shard, row : row + height, :] = both.astype(BF16)


def mlp_weights_kernel(*refs):
    zero, one, lefts, rights, (out_ref,), scratch, (sems,) = split_refs(refs, 6, 6, 9, 9, 1, 6, 1)
    copies = []
    for i in range(3):
        own = [(layer[i], layer[i + 3]) for layer in (zero, one)]
        rest = lefts[i::3], rights[i::3]
        copies.append(load_rows(sems.at[i], own, rest, scratch[2 * i], scratch[2 * i + 1]))
    for i, at in ((0, 0), (2, 288), (1, 384)):
        for copy in copies[i]:
            copy.wait()
        weight_product(out_ref, at, scratch[2 * i], scratch[2 * i + 1])
    out_ref[:, 528:, :] = jnp.zeros((4, 48, D), BF16)


def qkv_weights_kernel(*refs):
    gain_far, zero, one, lefts, rights, (out_ref,), (left, right, gain, sems) = split_refs(
        refs, 1, 3, 3, 3, 3, 1, 4
    )
    copies = load_rows(sems, [(a, g) for a, g, _ in (zero, one)], (lefts, rights), left, right)
    section = lax.axis_index("section")
    for layer, (_, _, own) in enumerate((zero, one)):

        @pl.when(section == layer)
        def _():
            fetch(own, gain, sems.at[8]).wait()

    gains = (gain[...].astype(F32) + gain_far[0][...].astype(F32)).astype(BF16)
    for shard in range(4):
        out_ref[shard, 288:304, :] = gains
        out_ref[shard, 304:, :] = jnp.zeros((16, D), BF16)
    for copy in copies:
        copy.wait()
    weight_product(out_ref, 0, left, right)


def assemble_kernel(fin_ref, up_ref, out_ref, down_ref, qkv_ref, gains_ref):
    for half in range(2):
        rows = slice(half * 96, half * 96 + 96)
        for block in range(3):
            cols = slice(block * D, (block + 1) * D)
            up_ref[rows, cols] = fin_ref[half, block * 96 : block * 96 + 96, :].astype(F32)
            at = MLP_ROWS + block * 96
            qkv_ref[rows, cols] = fin_ref[half, at : at + 96, :].astype(F32)
        out_ref[rows, :] = fin_ref[half, 288:384, :].astype(F32)
        down_ref[half * 144 : half * 144 + 144, :] = fin_ref[half, 384:528, :].astype(F32)
    gain_rows = slice(MLP_ROWS + 288, MLP_ROWS + 304)
    gains_ref[...] = fin_ref[0, gain_rows, :].astype(F32) + fin_ref[1, gain_rows, :].astype(F32)


def here():
    return lax.axis_index("section"), lax.axis_index("ctx"), lax.axis_index("wshard")


def flip(index, delta):
    for bit in (1, 2, 4, 8):
        if delta & bit:
            index = index + bit - 2 * bit * lax.rem(index // bit, 2)
    return index


def greet(peers):
    barrier = pltpu.get_barrier_semaphore()
    for peer in peers:
        pl.semaphore_signal(barrier, inc=1, device_id=peer, device_id_type=MESH)
    pl.semaphore_wait(barrier, len(peers))


def remote(src, dst, send, recv, peer):
    return pltpu.make_async_remote_copy(
        src_ref=src, dst_ref=dst, send_sem=send, recv_sem=recv, device_id=peer, device_id_type=MESH
    )


class Lines:
    count = 112

    def __init__(self, send, recv):
        self.send, self.recv, self.used, self.waits = send, recv, 0, []

    def make(self, src, dst, peer):
        at = self.used
        self.used += 1
        return remote(src, dst, self.send.at[at], self.recv.at[at], peer)

    def put(self, src, dst, peer):
        copy = self.make(src, dst, peer)
        copy.start()
        return copy

    def keep(self, src, dst):
        at = self.used
        self.used += 1
        copy = pltpu.make_async_copy(src, dst, self.send.at[at])
        copy.start()
        return copy


SEMS = [DMA((Lines.count,)), DMA((Lines.count,))]
ids = iter(range(1, 64))


def exchange_call(kernel, args, outs, scratch, collective_id, name):
    return pl.pallas_call(
        kernel,
        out_shape=outs,
        in_specs=[ANY] * len(args),
        out_specs=jax.tree.map(lambda _: ANY, outs),
        scratch_shapes=SEMS + list(scratch),
        compiler_params=pltpu.CompilerParams(
            collective_id=collective_id, has_side_effects=True, vmem_limit_bytes=VMEM_LIMIT
        ),
        name=name,
    )(*args)


def sibling_of(s, c, z):
    return (s, flip(c, 1), z)


def z_peers():
    s, c, z = here()
    return [(s, c, lax.rem(z + r, 4)) for r in (1, 3, 2)]


def beside_peers():
    s, c, z = here()
    return [(1 - s, c, z), (1 - s, flip(c, 8), z)]


class Gather:
    def __init__(self, lines, own, full):
        s, c, z = here()
        rows, cols = full.shape[2] // 2, full.shape[3] // 2
        self.rows = pl.ds(pl.multiple_of(lax.rem(c, 2) * rows, 16), rows)
        self.cols = [
            pl.ds(pl.multiple_of(side * cols, 128), cols) for side in (c // 8, 1 - c // 8)
        ]
        self.halves = [pl.ds(0, cols), pl.ds(cols, cols)]
        self.lines, self.full = lines, full
        self.sibling = sibling_of(s, c, z)
        after, before, _ = z_peers()
        self.step = []
        for cut, order in ((0, (after, before)), (1, (after, before))):
            where = full.at[s, z, self.rows, self.halves[cut]]
            piece = own.at[self.rows, self.halves[cut]]
            self.step.append([lines.put(piece, where, peer) for peer in order])
        self.peers = (after, before)
        self.aside = [self.beside(own.at[self.rows, self.cols[0]], z)]
        whole = full.at[s, z, self.rows]
        self.passed = [lines.put(own.at[self.rows], whole, self.sibling)]
        self.kept = lines.keep(own.at[self.rows], whole)
        self.sent = []

    def beside(self, src, z):
        s, _, _ = here()
        where = self.full.at[s, z, self.rows, self.cols[0]]
        return [self.lines.put(src, where, peer) for peer in beside_peers()]

    def from_neighbours(self):
        s, _, z = here()
        self.sources = [lax.rem(z + 3, 4), lax.rem(z + 1, 4)]
        self.second = []
        for side in (0, 1):
            self.step[side][side].wait_recv()
            block = self.full.at[s, self.sources[side], self.rows, self.halves[side]]
            self.second.append(self.lines.put(block, block, self.peers[side]))
        for side in (0, 1):
            self.step[1 - side][side].wait_recv()
            self.onward(self.sources[side])

    def onward(self, z):
        s, _, _ = here()
        block = self.full.at[s, z, self.rows]
        self.passed.append(self.lines.put(block, block, self.sibling))
        self.aside.append(self.beside(block.at[:, self.cols[0]], z))

    def from_opposite(self):
        _, _, z = here()
        for copy in self.second:
            copy.wait_recv()
        self.onward(lax.rem(z + 2, 4))

    def from_beside(self):
        s, _, z = here()
        for copies, source in zip(self.aside, (z, *self.sources, lax.rem(z + 2, 4))):
            for i, copy in enumerate(copies):
                copy.wait_recv()
                block = self.full.at[1 - s, source, self.rows, self.cols[i]]
                self.passed.append(self.lines.put(block, block, self.sibling))

    def finish(self):
        self.kept.wait()
        for copies in (*self.step, *self.aside, self.second):
            for copy in copies:
                copy.wait_send()
        for copy in self.passed:
            copy.wait()


def run_gathers(gathers):
    for gather in gathers:
        gather.from_neighbours()
    for gather in gathers:
        gather.from_opposite()
    for gather in gathers:
        gather.from_beside()
    for gather in gathers:
        gather.finish()


def full_shapes(weights):
    return [sds((2, 4, *w.shape), BF16) for w in weights]


def gather_peers():
    return [sibling_of(*here()), *z_peers()[:2], *beside_peers()]


class Scatter:
    def __init__(self, lines, comb, got):
        s, c, z = here()
        self.copies = [
            lines.put(comb.at[peer[2]], got.at[i], peer) for i, peer in enumerate(z_peers())
        ]

    def finish(self):
        for copy in self.copies:
            copy.wait()


def scatter_shapes(combs):
    return [sds((3, *comb.shape[1:]), BF16) for comb in combs]


def start_kernel(*refs):
    own, gain, full, gains, send, recv = refs
    s, c, z = here()
    lines = Lines(send, recv)
    across = [(1 - s, c, lax.rem(z + r, 4)) for r in (1, 3, 2)]
    greet([*gather_peers(), z_peers()[2], *across])
    gather = Gather(lines, own, full)
    copies = [
        lines.put(gain, gains.at[s, z], peer) for peer in (*z_peers(), beside_peers()[0], *across)
    ]
    kept = lines.keep(gain, gains.at[s, z])
    run_gathers([gather])
    kept.wait()
    for copy in copies:
        copy.wait()


def start(weight, gain):
    outs = (*full_shapes([weight]), sds((2, 4, *gain.shape), BF16))
    return exchange_call(start_kernel, (weight, gain), outs, [], next(ids), "start")


def spread_kernel(count, *refs):
    (qkv_ref,), own_w, (q_ref, kv_ref), full, (send, recv) = split_refs(refs, 1, count, 2, count, 2)
    s, c, z = here()
    lines = Lines(send, recv)
    sibling = sibling_of(s, c, z)
    peers = {delta: (s, flip(c, delta), z) for delta in range(2, CTX, 2)}
    greet([sibling, *peers.values(), *(gather_peers()[1:] if count else [])])
    kv_rows = pl.ds(GW, 2 * GW)
    q_rows = pl.ds(0, GW)
    order = [14, 10, 12, 8, 6, 4, 2]
    kv_sends, q_sends = {}, []
    for delta in order:
        peer = peers[delta]
        kv_sends[delta] = lines.put(qkv_ref.at[peer[1] // 4, kv_rows], kv_ref.at[c], peer)
        if delta % 4 == 0:
            q_sends.append(lines.put(qkv_ref.at[peer[1] // 4, q_rows], q_ref.at[c // 4], peer))
    gathers = [Gather(lines, *two) for two in zip(own_w, full)]
    passed = [lines.put(qkv_ref.at[c // 4, kv_rows], kv_ref.at[c], sibling)]
    kept = [
        lines.keep(qkv_ref.at[c // 4, kv_rows], kv_ref.at[c]),
        lines.keep(qkv_ref.at[c // 4, q_rows], q_ref.at[c // 4]),
    ]
    for delta in reversed(order):
        kv_sends[delta].wait_recv()
        block = kv_ref.at[flip(c, delta)]
        passed.append(lines.put(block, block, sibling))
    for copy in kept:
        copy.wait()
    for copy in q_sends:
        copy.wait()
    for copy in kv_sends.values():
        copy.wait_send()
    for copy in passed:
        copy.wait()
    run_gathers(gathers)


def spread(qkv, weights):
    outs = [sds((4, GW, ROWS), BF16), sds((CTX, 2 * GW, ROWS), BF16)] + full_shapes(weights)
    kernel = functools.partial(spread_kernel, len(weights))
    res = exchange_call(kernel, [qkv, *weights], outs, [], next(ids), "spread")
    return res[0], res[1], res[2:]


class Meet:
    def __init__(self, lines, zero, one, sib, far, both):
        s, c, z = here()
        self.core = core = lax.rem(c, 2)
        self.lines, self.far, self.both = lines, far, both
        self.sibling = sibling_of(s, c, z)
        peer = (1 - s, flip(c, 8) * core + c * (1 - core), z)
        first = lines.used
        for layer, (near, other) in enumerate(((zero, one), (one, zero))):
            lines.used = first

            @pl.when(s == layer)
            def _():
                self.apart = lines.put(other, far, peer)
                if sib is not None:
                    self.close = lines.put(self.half(near), sib, self.sibling)

        lines.used = first
        self.apart = lines.make(zero, far, peer)
        if sib is not None:
            self.close = lines.make(sib, sib, self.sibling)

    def half(self, ref):
        return ref.at[:, 1 - self.core] if len(ref.shape) == 4 else ref

    def forward(self):
        self.apart.wait_recv()
        if self.both is not None:
            self.passed = self.lines.put(self.half(self.far), self.both, self.sibling)

    def finish(self):
        self.apart.wait_send()
        if self.both is not None:
            self.close.wait()
            self.passed.wait()


def meet_peers():
    return [sibling_of(*here()), *beside_peers()]


def half_shape(a):
    return sds((a.shape[0], *a.shape[2:]) if a.ndim == 4 else a.shape, BF16)


def meet_shapes(zero):
    return [shape(a) for shape in (half_shape, lambda a: sds(a.shape, BF16), half_shape) for a in zero]


class Show:
    def __init__(self, lines, zero, one, out):
        s, c, z = here()
        first = lines.used
        for layer, (near, other) in enumerate(((zero, one), (one, zero))):
            lines.used = first

            @pl.when(s == layer)
            def _():
                lines.put(other, out.at[s], (1 - s, c, z))
                lines.keep(near, out.at[s])

        lines.used = first
        self.copy = lines.make(zero, out.at[s], (1 - s, c, z))
        self.kept = pltpu.make_async_copy(zero, out.at[s], lines.send.at[lines.used])
        lines.used += 1

    def finish(self):
        self.copy.wait()
        self.kept.wait()


def turn_kernel(count, acts, shows, *refs):
    (x_ref,), own_w, zero, one, shown, (o_ref,), full, taken, outs, (send, recv) = split_refs(
        refs, 1, count, acts, acts, 2 * shows, 1, count, 3 * acts, shows, 2
    )
    s, c, z = here()
    lines = Lines(send, recv)
    peers = [(s, flip(c, delta), z) for delta in (4, 8, 12)]
    greet(peers + (gather_peers() if count else meet_peers() if acts else []))
    copies = [lines.put(x_ref.at[peer[1] // 4], o_ref.at[c // 4], peer) for peer in peers]
    gathers = [Gather(lines, *two) for two in zip(own_w, full)]
    meets = [Meet(lines, *five) for five in zip(zero, one, *split_refs(taken, acts, acts, acts))]
    shown = [Show(lines, *shown, out) for out in outs]
    lines.keep(x_ref.at[c // 4], o_ref.at[c // 4]).wait()
    for copy in copies:
        copy.wait()
    for meet in meets:
        meet.forward()
    run_gathers(gathers)
    for work in meets + shown:
        work.finish()


def turn(x, weights=(), zero=(), one=(), show=()):
    args = [x, *weights, *zero, *one, *show]
    counts = len(weights), len(zero), len(show) // 2
    outs = [sds((4, GW, ROWS), BF16)] + full_shapes(weights) + meet_shapes(zero)
    outs += [sds((2, *a.shape), BF16) for a in show[::2]]
    res = exchange_call(functools.partial(turn_kernel, *counts), args, outs, [], next(ids), "turn")
    return res[0], *split_refs(res[1:], counts[0], 3 * counts[1], counts[2])


def meet_kernel(*refs):
    zero, one, taken, (out,), (send, recv) = split_refs(refs, 3, 3, 4, 1, 2)
    lines = Lines(send, recv)
    greet(meet_peers())
    work = [
        Meet(lines, zero[0], one[0], *taken[:3]),
        Meet(lines, zero[1], one[1], None, taken[3], None),
    ]
    shown = Show(lines, zero[2], one[2], out)
    for meet in work:
        meet.forward()
    for meet in (*work, shown):
        meet.finish()


def meet(zero, one):
    outs = meet_shapes(zero[:1]) + [sds(zero[1].shape, BF16), sds((2, *zero[2].shape), BF16)]
    return exchange_call(meet_kernel, (*zero, *one), outs, [], next(ids), "meet")


def scatter_kernel(count, *refs):
    combs, got, (send, recv) = split_refs(refs, count, count, 2)
    lines = Lines(send, recv)
    greet(z_peers())
    for work in [Scatter(lines, *two) for two in zip(combs, got)]:
        work.finish()


def scatter(combs):
    kernel = functools.partial(scatter_kernel, len(combs))
    return exchange_call(kernel, combs, scatter_shapes(combs), [], next(ids), "scatter")


def return_kernel(count, *refs):
    (dq_ref, dkv_ref), combs, (dqo_ref, sums_ref), got, (send, recv, mine, theirs, total) = split_refs(
        refs, 2, count, 2, count, 5
    )
    s, c, z = here()
    lines = Lines(send, recv)
    core = lax.rem(c, 2)
    sibling = sibling_of(s, c, z)
    peers = {delta: (s, flip(c, delta), z) for delta in range(2, CTX, 2)}
    greet([sibling, *peers.values(), *(z_peers() if count else [])])
    passed = [lines.put(dkv_ref.at[2 * i + 1 - core], theirs.at[i], sibling) for i in range(8)]
    loads = [lines.keep(dkv_ref.at[2 * i + core], mine.at[i]) for i in range(8)]
    sends = [
        lines.put(dq_ref.at[peers[delta][1] // 4], dqo_ref.at[c // 4], peers[delta]) for delta in (4, 8, 12)
    ]
    scatters = [Scatter(lines, *two) for two in zip(combs, got)]
    kept = [lines.keep(dq_ref.at[c // 4], dqo_ref.at[c // 4])]
    for i in range(8):
        loads[i].wait()
        passed[i].wait()
        total[i] = (mine[i].astype(F32) + theirs[i].astype(F32)).astype(BF16)
    for delta in (14, 10, 12, 8, 6, 4, 2):
        sends.append(lines.put(total.at[peers[delta][1] // 2], sums_ref.at[c // 2], peers[delta]))
    kept.append(lines.keep(total.at[c // 2], sums_ref.at[c // 2]))
    for copy in kept + sends:
        copy.wait()
    for work in scatters:
        work.finish()


def give_back(dq, dkv, combs):
    block = pltpu.VMEM((8, 2 * GW, ROWS), BF16)
    outs = [sds((4, GW, ROWS), BF16), sds((8, 2 * GW, ROWS), BF16)] + scatter_shapes(combs)
    kernel = functools.partial(return_kernel, len(combs))
    res = exchange_call(kernel, [dq, dkv, *combs], outs, [block] * 3, next(ids), "give_back")
    return res[0], res[1], res[2:]


QUARTER = SUM_ROWS // 4


def finish_kernel(comb_m, got_m, comb_q, got_q, fin, send, recv, load, terms, own_sum, parts, red):
    s, c, z = here()
    lines = Lines(send, recv)
    core = lax.rem(c, 2)
    sibling = sibling_of(s, c, z)
    near = {delta: (s, flip(c, delta), z) for delta in range(2, CTX, 2)}
    loads = []
    for part, (comb, got, at, rows) in enumerate(
        ((comb_m, got_m, 0, MLP_ROWS), (comb_q, got_q, MLP_ROWS, QKV_ROWS))
    ):
        rows = pl.ds(at, rows)
        loads.append(fetch(comb.at[z], terms.at[0, rows], load.at[4 * part]))
        loads += [fetch(got.at[i], terms.at[i + 1, rows], load.at[4 * part + i + 1]) for i in range(3)]
    greet([sibling, *near.values()])
    for copy in loads:
        copy.wait()
    for at in range(0, SUM_ROWS, 128):
        rows = slice(at, at + 128)
        both = terms[0, rows].astype(F32) + terms[1, rows].astype(F32)
        both += terms[2, rows].astype(F32) + terms[3, rows].astype(F32)
        own_sum[rows] = both.astype(BF16)

    def block(at):
        rows = pl.ds(pl.multiple_of(lax.rem(at // 2, 4) * QUARTER, 16), QUARTER)
        return rows, pl.ds(pl.multiple_of(at // 8 * (D // 2), 128), D // 2)

    order = [14, 10, 12, 8, 6, 4, 2]
    sends = [lines.put(own_sum.at[block(near[delta][1])], parts.at[c // 2], near[delta]) for delta in order]
    lines.keep(own_sum.at[block(c)], parts.at[c // 2]).wait()
    for copy in sends:
        copy.wait()
    for at in range(0, QUARTER, 112):
        rows = slice(at, at + 112)
        total = parts[0, rows].astype(F32)
        for i in range(1, 8):
            total += parts[i, rows].astype(F32)
        red[rows] = total.astype(BF16)
    target = fin.at[core]
    kept = lines.keep(red, target.at[block(c)])
    passed = [lines.put(red, target.at[block(c)], sibling)]
    shown = {delta: lines.put(red, target.at[block(c)], near[delta]) for delta in order}
    for delta in reversed(order):
        shown[delta].wait_recv()
        piece = target.at[block(flip(c, delta))]
        passed.append(lines.put(piece, piece, sibling))
    kept.wait()
    for copy in shown.values():
        copy.wait_send()
    for copy in passed:
        copy.wait()


def finish(*args):
    scratch = [
        DMA((8,)),
        pltpu.VMEM((4, SUM_ROWS, D), BF16),
        pltpu.VMEM((SUM_ROWS, D), BF16),
        pltpu.VMEM((8, QUARTER, D // 2), BF16),
        pltpu.VMEM((QUARTER, D // 2), BF16),
    ]
    return exchange_call(
        finish_kernel, args, sds((2, SUM_ROWS, D), BF16), scratch, next(ids), "finish"
    )


def rope_tables():
    positions = (lax.axis_index("ctx") * ROWS + lax.iota(jnp.int32, ROWS)).astype(F32)
    frequency = 1.0 / 160000.0 ** (jnp.arange(HEAD_DIM // 2, dtype=F32) * 2.0 / HEAD_DIM)
    angles = frequency[:, None] * positions[None, :]
    return jnp.cos(angles), jnp.sin(angles)


def weight_scratch(*shapes):
    return [pltpu.VMEM(shape, BF16) for shape in shapes]


def forward_layer(layer, x, gains, w_qkv, late, tables):
    qkv, normed = compute_call(
        functools.partial(qkv_kernel, layer),
        (x, gains[0], *tables, w_qkv),
        (sds((4, 3 * GW, ROWS), BF16), sds((D, ROWS), BF16)),
        [*weight_scratch((D, 3 * D)), DMA],
        name="norm_qkv",
        far=1,
    )
    q, kv, w_up = spread(qkv, late[1:2] if layer == 0 else [])
    low, wide, totals = compute_call(
        attend_kernel,
        (q, kv),
        (sds((4, GW, ROWS), BF16), sds((4, GW, ROWS), F32), sds((GH, 8, 512), F32)),
        [pltpu.VMEM((2048, 512), F32)],
        name="attend",
    )
    ot, w_rest, _, _ = turn(low, late[::2] if layer == 0 else [])
    if layer == 0:
        late = [w.reshape(2, -1, w.shape[-1]) for w in (w_rest[0], w_up[0], w_rest[1])]
    ot = ot.reshape(D, ROWS)
    out, hidden, gate_up, normed_two, product = compute_call(
        functools.partial(mlp_kernel, layer),
        (ot, x, gains[1], *late),
        (sds((ROWS, D), BF16), sds((ROWS, D), F32), sds((ROWS, 2 * FF), F32),
         sds((D, ROWS), BF16), sds((FF, ROWS), BF16)),
        [*weight_scratch((D, D), (D, 2 * FF), (FF, D)), DMA((3,))],
        name="mlp",
        far=3,
    )
    lefts = [by_core(a) for a in (normed_two, product, ot, normed)]
    return out, late, lefts, (x, q, kv, wide, totals, hidden, gate_up)


def by_core(a):
    return a.reshape(4, 2, -1, ROWS)


def mlp_back(layer, grad, stored, gains, late):
    hidden, gate_up = stored[5:]
    return compute_call(
        functools.partial(mlp_back_kernel, layer),
        (grad, hidden, gate_up, gains[1], *late),
        (sds((D, ROWS), BF16), sds((ROWS, D), F32), sds((ROWS, 2 * FF), BF16),
         sds((ROWS, D), BF16), sds((1, D), F32)),
        [*weight_scratch((D, D), (D, 2 * FF), (FF, D)), DMA((3,))],
        name="mlp_back",
        far=3,
    )


def attend_back(d_o, stored):
    _, q, kv, wide, totals = stored[:5]
    return compute_call(
        attend_back_kernel,
        (q, kv, wide, totals, d_o),
        (sds((4, GW, ROWS), BF16), sds((CTX, 2 * GW, ROWS), BF16)),
        name="attend_back",
    )


def qkv_back(layer, dq, dkv, stored, gains, tables, grad_hidden, d_gain_two, w_qkv):
    return compute_call(
        functools.partial(qkv_back_kernel, layer),
        (dq, dkv, stored[0], gains[0], *tables, grad_hidden, d_gain_two, w_qkv),
        (sds((ROWS, D), BF16), sds((ROWS, 3 * D), BF16), sds((16, D), BF16)),
        [pltpu.VMEM((3 * D, ROWS), F32), *weight_scratch((D, 3 * D)), DMA],
        name="qkv_back",
        far=1,
    )


def local(inputs, cotangent, attn_gain, qkv_weight, out_weight, mlp_gain, up_weight, down_weight):
    first = lax.axis_index("section") == 0
    x = jnp.where(first, inputs[0, 0], inputs[1, 0])
    cot = jnp.where(first, cotangent[0, 0], cotangent[1, 0])
    gain = jnp.pad(jnp.concatenate([attn_gain, mlp_gain], axis=0), ((0, 14), (0, 64)))
    w_qkv, gains = start(qkv_weight[0], gain)
    w_qkv = w_qkv.reshape(2, D, 3 * D)
    gains = [
        [gains[layer, :, row, :192].reshape(1, D) for row in range(2)] for layer in range(2)
    ]
    tables = rope_tables()
    late = [out_weight[0], up_weight[0], down_weight[0]]
    mid, late, left_zero, kept_zero = forward_layer(0, x, gains[0], w_qkv, late, tables)
    end, _, left_one, kept_one = forward_layer(1, mid, gains[1], w_qkv, late, tables)

    d_ot, grad_hidden, gg_one, branch_one, d_gain = mlp_back(1, cot, kept_one, gains[1], late)
    d_o, _, lefts, (activations,) = turn(
        d_ot.reshape(4, GW, ROWS), zero=left_zero, one=left_one, show=(mid, end)
    )
    dq, dkv = attend_back(d_o, kept_one)
    dq, dkv, _ = give_back(dq, dkv, [])
    grad_mid, gp_one, gains_one = qkv_back(
        1, dq, dkv, kept_one, gains[1], tables, grad_hidden, d_gain, w_qkv
    )

    d_ot, grad_hidden, gg_zero, branch_zero, d_gain = mlp_back(0, grad_mid, kept_zero, gains[0], late)
    rights_zero, rights_one = [gg_zero, grad_mid, branch_zero], [gg_one, cot, branch_one]
    d_o, _, rights, _ = turn(d_ot.reshape(4, GW, ROWS), zero=rights_zero, one=rights_one)
    mlp_lefts = [lefts[4 * i + j] for i in range(3) for j in range(3)]
    heights = (96, 144, 96)
    comb_mlp = compute_call(
        mlp_weights_kernel,
        (*left_zero[:3], *rights_zero, *left_one[:3], *rights_one, *mlp_lefts, *rights),
        sds((4, MLP_ROWS, D), BF16),
        [
            pltpu.VMEM(shape, BF16)
            for height, right in zip(heights, rights_zero)
            for shape in ((4, height, 4 * ROWS), (4 * ROWS, right.shape[1]))
        ]
        + [DMA((3, 8))],
        name="mlp_weights",
        far=30,
    )
    dq, dkv = attend_back(d_o, kept_zero)
    dq, dkv, (got_mlp,) = give_back(dq, dkv, [comb_mlp])
    grad_start, gp_zero, gains_zero = qkv_back(
        0, dq, dkv, kept_zero, gains[0], tables, grad_hidden, d_gain, w_qkv
    )
    *gp_rest, gains_far, input_grads = meet(
        (gp_zero, gains_zero, grad_start), (gp_one, gains_one, grad_mid)
    )
    comb_qkv = compute_call(
        qkv_weights_kernel,
        (gains_far, left_zero[3], gp_zero, gains_zero, left_one[3], gp_one, gains_one,
         *lefts[3::4], *gp_rest),
        sds((4, QKV_ROWS, D), BF16),
        [*weight_scratch((4, 96, 4 * ROWS), (4 * ROWS, 3 * D), (16, D)), DMA((9,))],
        name="qkv_weights",
        far=12,
    )
    (got_qkv,) = scatter([comb_qkv])
    fin = finish(comb_mlp, got_mlp, comb_qkv, got_qkv)
    grad_up, grad_out, grad_down, grad_qkv, gain_sums = compute_call(
        assemble_kernel,
        (fin,),
        [sds(shape, F32) for shape in ((192, 3 * D), (192, D), (288, D), (192, 3 * D), (16, D))],
        name="assemble",
    )
    gain_sums = lax.dynamic_slice_in_dim(gain_sums[:2], lax.axis_index("wshard") * 192, 192, 1)
    return (
        activations[None, :, None],
        input_grads[None, :, None],
        gain_sums[0:1],
        grad_qkv[None],
        grad_out[None],
        gain_sums[1:2],
        grad_up[None],
        grad_down[None],
    )


def solution(mesh):
    global ids
    ids = iter(range(1, 64))
    placed = (
        P(None, "wshard", "ctx", None),
        P(None, "wshard", "ctx", None),
        P("section", "wshard"),
        P("section", "wshard", None),
        P("section", "wshard", None),
        P("section", "wshard"),
        P("section", "wshard", None),
        P("section", "wshard", None),
    )
    return jax.shard_map(
        local,
        mesh=mesh,
        in_specs=placed,
        out_specs=(
            P("section", None, "wshard", "ctx", None),
            P("section", None, "wshard", "ctx", None),
            P("section", "wshard"),
            P("section", "wshard", None),
            P("section", "wshard", None),
            P("section", "wshard"),
            P("section", "wshard", None),
            P("section", "wshard", None),
        ),
        check_vma=False,
    )
```

```python
import functools

import jax
import jax.numpy as jnp
from jax import lax
from jax.experimental import pallas as pl
from jax.experimental.pallas import tpu as pltpu
from jax.sharding import PartitionSpec as P

D = 768
HEADS = 12
HEAD_DIM = 64
FF = 1152
ROWS = 128
GROUPS = 4
GH = HEADS // GROUPS
GW = GH * HEAD_DIM
CTX = 16
SCALE = HEAD_DIM ** (-0.5)
F32 = jnp.float32
BF16 = jnp.bfloat16
MESH = pl.DeviceIdType.MESH
DMA = pltpu.SemaphoreType.DMA
ANY = pl.BlockSpec(memory_space=pl.ANY)
VM = pl.BlockSpec(memory_space=pltpu.VMEM)
VMEM_LIMIT = 56 * 1024 * 1024


def dot(a, b):
    return jnp.dot(a, b, preferred_element_type=F32)


def dot_nt(a, b):
    return lax.dot_general(a, b, (((1,), (1,)), ((), ())), preferred_element_type=F32)


def sds(shape, dtype):
    return jax.ShapeDtypeStruct(shape, dtype)


def compute_call(kernel, args, outs, scratch=(), name=None, far=0):
    return pl.pallas_call(
        kernel,
        out_shape=outs,
        in_specs=[VM] * (len(args) - far) + [ANY] * far,
        out_specs=jax.tree.map(lambda _: VM, outs),
        scratch_shapes=list(scratch),
        compiler_params=pltpu.CompilerParams(vmem_limit_bytes=VMEM_LIMIT),
        name=name,
    )(*args)


def fetch(src, dst, sem):
    copy = pltpu.make_async_copy(src, dst, sem)
    copy.start()
    return copy


def turned_low(x):
    return x.astype(F32).T.astype(BF16)


def norm_parts(source):
    centered = source - jnp.mean(source, axis=-1, keepdims=True)
    variance = jnp.mean(centered * centered, axis=-1, keepdims=True)
    rstd = lax.rsqrt(variance + 1e-05)
    return centered * rstd, rstd


def norm_back(grad, normalized, rstd, gain):
    inner = grad * gain
    mean_one = jnp.mean(inner, axis=-1, keepdims=True)
    mean_two = jnp.mean(inner * normalized, axis=-1, keepdims=True)
    grad_gain = jnp.sum(grad * normalized, axis=0, keepdims=True)
    return rstd * (inner - mean_one - normalized * mean_two), grad_gain


def split_refs(refs, *counts):
    refs = list(refs)
    out = []
    for count in counts:
        out.append(refs[:count])
        refs = refs[count:]
    return out


def project(x_ref, gain, cos_ref, sin_ref, w_ref, loaded, qkv_ref, normed_ref):
    normalized, _ = norm_parts(x_ref[...].astype(F32))
    normed = (normalized * gain).astype(BF16)
    normed_ref[...] = turned_low(normed)
    loaded()
    cos = cos_ref[...]
    sin = sin_ref[...]
    for part in range(3):
        for block in range(3):
            at = part * D + block * 256
            turned = dot(normed, w_ref[:, at : at + 256]).T
            for head_at in range(4):
                head = block * 4 + head_at
                one = turned[head_at * 64 : head_at * 64 + 32]
                two = turned[head_at * 64 + 32 : head_at * 64 + 64]
                if part < 2:
                    one, two = one * cos - two * sin, two * cos + one * sin
                if part == 0:
                    one, two = one * SCALE, two * SCALE
                row = part * GW + (head % GH) * HEAD_DIM
                qkv_ref[head // GH, row : row + 32, :] = one.astype(BF16)
                qkv_ref[head // GH, row + 32 : row + 64, :] = two.astype(BF16)


CHUNK = 256
CHUNKS = 2048 // CHUNK
PAIR = CHUNK // ROWS


def attend(q_ref, kv_ref, low_ref, wide_ref, totals_ref, s_ref):
    @pl.loop(0, GH)
    def _(h):
        at = pl.multiple_of(h * HEAD_DIM, HEAD_DIM)
        value_at = pl.multiple_of(h * HEAD_DIM + GW, HEAD_DIM)
        qt = jnp.concatenate([q_ref[i, pl.ds(at, HEAD_DIM), :] for i in range(4)], axis=1)
        top = jnp.full((8, 512), -jnp.inf, F32)
        for c in range(CHUNKS):
            keys = jnp.concatenate(
                [kv_ref[c * PAIR + i, pl.ds(at, HEAD_DIM), :].T for i in range(PAIR)], axis=0
            )
            scores = dot(keys, qt)
            s_ref[c * CHUNK : (c + 1) * CHUNK, :] = scores
            top = jnp.maximum(top, jnp.max(scores.reshape(CHUNK // 8, 8, 512), axis=0))
        top = jnp.max(top, axis=0, keepdims=True)
        total = jnp.zeros((8, 512), F32)
        acc = jnp.zeros((HEAD_DIM, 512), F32)
        for c in range(CHUNKS):
            p = jnp.exp(s_ref[c * CHUNK : (c + 1) * CHUNK, :] - top)
            total = total + jnp.sum(p.reshape(CHUNK // 8, 8, 512), axis=0)
            values = jnp.concatenate(
                [kv_ref[c * PAIR + i, pl.ds(value_at, HEAD_DIM), :] for i in range(PAIR)], axis=1
            )
            acc = acc + dot(values, p.astype(BF16))
        total = jnp.sum(total, axis=0, keepdims=True)
        out = acc / total
        totals_ref[h] = jnp.broadcast_to(top + jnp.log(total), (8, 512))
        for i in range(4):
            piece = out[:, i * ROWS : (i + 1) * ROWS]
            wide_ref[i, pl.ds(at, HEAD_DIM), :] = piece
            low_ref[i, pl.ds(at, HEAD_DIM), :] = piece.astype(BF16)


def attend_back_kernel(q_ref, kv_ref, wide_ref, totals_ref, do_ref, dq_ref, dkv_ref):
    @pl.loop(0, GH)
    def _(h):
        at = pl.multiple_of(h * HEAD_DIM, HEAD_DIM)
        value_at = pl.multiple_of(h * HEAD_DIM + GW, HEAD_DIM)
        out_at = pl.multiple_of(h * ROWS, ROWS)
        qt = jnp.concatenate([q_ref[i, pl.ds(at, HEAD_DIM), :] for i in range(4)], axis=1)
        dot_t = jnp.concatenate([do_ref[i, pl.ds(at, HEAD_DIM), :] for i in range(4)], axis=1)
        wide = jnp.concatenate([wide_ref[i, pl.ds(at, HEAD_DIM), :] for i in range(4)], axis=1)
        delta = jnp.sum(wide * dot_t.astype(F32), axis=0, keepdims=True)
        totals = totals_ref[h, 0:1, :]
        zero = jnp.zeros((512, HEAD_DIM), BF16)
        sides = jnp.concatenate(
            [
                jnp.concatenate([qt.T, zero], axis=1),
                jnp.concatenate([zero, dot_t.T], axis=1),
            ],
            axis=0,
        )

        def step(c, acc):
            keys_t = [kv_ref[c * PAIR + i, pl.ds(at, HEAD_DIM), :] for i in range(PAIR)]
            values_t = [kv_ref[c * PAIR + i, pl.ds(value_at, HEAD_DIM), :] for i in range(PAIR)]
            keys = jnp.concatenate([k.T for k in keys_t], axis=0)
            values = jnp.concatenate([v.T for v in values_t], axis=0)
            p = jnp.exp(dot(keys, qt) - totals)
            ds = (p * (dot(values, dot_t) - delta)).astype(BF16)
            both = jnp.concatenate([ds, p.astype(BF16)], axis=1)
            grads = dot(both, sides).astype(BF16)
            for i in range(PAIR):
                dkv_ref[c * PAIR + i, pl.ds(out_at, ROWS), :] = grads[i * ROWS : (i + 1) * ROWS]
            return acc + dot(jnp.concatenate(keys_t, axis=1), ds)

        acc = lax.fori_loop(0, CHUNKS, step, jnp.zeros((HEAD_DIM, 512), F32)) * SCALE
        for i in range(4):
            dq_ref[i, pl.ds(at, HEAD_DIM), :] = acc[:, i * ROWS : (i + 1) * ROWS].astype(BF16)


def mlp(
    ot_ref, x_ref, gain, wo_ref, wu_ref, wd_ref, loaded,
    out_ref, hidden_ref, gate_up_ref, normed_ref, product_ref,
):
    attended = turned_low(ot_ref[...].reshape(D, ROWS))
    loaded(0)
    hidden = x_ref[...].astype(F32) + dot(attended, wo_ref[...])
    hidden_ref[...] = hidden
    normalized, _ = norm_parts(hidden)
    normed = (normalized * gain).astype(BF16)
    normed_ref[...] = turned_low(normed)
    loaded(1)
    gate_up = dot(normed, wu_ref[...])
    gate_up_ref[...] = gate_up
    gate = gate_up[:, :FF]
    phi = 0.5 * (1.0 + lax.erf(gate * 0.5**0.5))
    product = (gate * phi * gate_up[:, FF:]).astype(BF16)
    product_ref[...] = turned_low(product)
    loaded(2)
    out_ref[...] = (hidden + dot(product, wd_ref[...])).astype(BF16)


def mlp_back_kernel(
    layer, g_ref, hidden_ref, gate_up_ref, gain_ref, wo_all, wu_all, wd_all,
    dot_ref, grad_hidden_ref, gg_ref, branch_ref, d_gain_ref, wo_ref, wu_ref, wd_ref, sem,
):
    loads = [
        fetch(src.at[layer], dst, sem.at[i])
        for i, (src, dst) in enumerate([(wd_all, wd_ref), (wu_all, wu_ref), (wo_all, wo_ref)])
    ]
    grad = g_ref[...]
    loads[0].wait()
    grad_product = dot_nt(grad, wd_ref[...])
    gate = gate_up_ref[:, :FF]
    up = gate_up_ref[:, FF:]
    phi = 0.5 * (1.0 + lax.erf(gate * 0.5**0.5))
    density = jnp.exp(-0.5 * gate * gate) * 0.3989422804014327
    grad_gate = (grad_product * up * (phi + gate * density)).astype(BF16)
    grad_up = (grad_product * gate * phi).astype(BF16)
    gg_ref[:, :FF] = grad_gate
    gg_ref[:, FF:] = grad_up
    loads[1].wait()
    grad_normed = dot_nt(grad_gate, wu_ref[:, :FF]) + dot_nt(grad_up, wu_ref[:, FF:])
    normalized, rstd = norm_parts(hidden_ref[...])
    part, d_gain = norm_back(grad_normed, normalized, rstd, gain_ref[...].astype(F32))
    d_gain_ref[...] = d_gain
    grad_hidden = grad.astype(F32) + part
    grad_hidden_ref[...] = grad_hidden
    branch = grad_hidden.astype(BF16)
    branch_ref[...] = branch
    loads[2].wait()
    dot_ref[...] = dot_nt(branch, wo_ref[...]).T.astype(BF16)


def qkv_back_kernel(
    layer, dq_ref, dkv_ref, x_ref, gain_ref, cos_ref, sin_ref, grad_hidden_ref, gain_two_ref, w_all,
    grad_x_ref, gp_out_ref, gains_ref, gp_ref, w_ref, sem,
):
    load = fetch(w_all.at[layer], w_ref, sem)
    cos = cos_ref[...]
    sin = sin_ref[...]

    def back(one, two):
        return one * cos + two * sin, two * cos - one * sin

    for head in range(HEADS):
        group, inner = head // GH, head % GH
        at = inner * HEAD_DIM
        one = dq_ref[group, at : at + 32, :].astype(F32)
        two = dq_ref[group, at + 32 : at + 64, :].astype(F32)
        gq = back(one, two)
        rows = slice(inner * ROWS, (inner + 1) * ROWS)
        kv = (dkv_ref[2 * group, rows, :].astype(F32) + dkv_ref[2 * group + 1, rows, :].astype(F32)).T
        gk = back(kv[:32], kv[32:64])
        base = head * HEAD_DIM
        gp_ref[base : base + 32, :] = gq[0]
        gp_ref[base + 32 : base + 64, :] = gq[1]
        gp_ref[D + base : D + base + 32, :] = gk[0]
        gp_ref[D + base + 32 : D + base + 64, :] = gk[1]
        gp_ref[2 * D + base : 2 * D + base + 64, :] = kv[64:]
    load.wait()
    grad_normed = jnp.zeros((ROWS, D), F32)
    for block in range(9):
        cols = slice(block * 256, (block + 1) * 256)
        gp = gp_ref[cols, :].T.astype(BF16)
        gp_out_ref[:, cols] = gp
        grad_normed = grad_normed + dot_nt(gp, w_ref[:, cols])
    normalized, rstd = norm_parts(x_ref[...].astype(F32))
    part, d_gain = norm_back(grad_normed, normalized, rstd, gain_ref[...].astype(F32))
    gains_ref[...] = jnp.concatenate(
        [d_gain, gain_two_ref[...], jnp.zeros((14, D), F32)], axis=0
    ).astype(BF16)
    grad_x_ref[...] = (grad_hidden_ref[...] + part).astype(BF16)


MLP_ROWS = 576
QKV_ROWS = 320
SUM_ROWS = MLP_ROWS + QKV_ROWS


def load_rows(sems, own, rest, left, right):
    section = lax.axis_index("section")
    core = lax.rem(lax.axis_index("ctx"), 2)

    def lanes(i):
        return left.at[:, :, pl.ds(i * ROWS, ROWS)]

    def rows(i):
        return right.at[pl.ds(i * ROWS, ROWS)]

    for layer, (a, g) in enumerate(own):

        @pl.when(section == layer)
        def _():
            fetch(a.at[:, core], lanes(0), sems.at[0])
            fetch(g, rows(0), sems.at[1])

    (a_sib, a_far, a_both), (g_sib, g_far, g_both) = rest
    copies = [
        fetch(a_sib, lanes(1), sems.at[2]),
        fetch(a_far.at[:, core], lanes(2), sems.at[3]),
        fetch(a_both, lanes(3), sems.at[4]),
        fetch(g_sib, rows(1), sems.at[5]),
        fetch(g_far, rows(2), sems.at[6]),
        fetch(g_both, rows(3), sems.at[7]),
    ]
    copies.append(pltpu.make_async_copy(a_sib, lanes(0), sems.at[0]))
    copies.append(pltpu.make_async_copy(g_sib, rows(0), sems.at[1]))
    return copies


def weight_product(out_ref, at, left, right):
    height = left.shape[1]

    @pl.loop(0, 4)
    def _(shard):
        for block in range(right.shape[1] // D):
            row = at + block * height
            both = dot(left[shard], right[:, block * D : (block + 1) * D])
            out_ref[shard, row : row + height, :] = both.astype(BF16)


def mlp_weights_kernel(*refs):
    zero, one, lefts, rights, (out_ref,), scratch, (sems,) = split_refs(refs, 6, 6, 9, 9, 1, 6, 1)
    copies = []
    for i in range(3):
        own = [(layer[i], layer[i + 3]) for layer in (zero, one)]
        rest = lefts[i::3], rights[i::3]
        copies.append(load_rows(sems.at[i], own, rest, scratch[2 * i], scratch[2 * i + 1]))
    for i, at in ((0, 0), (2, 288), (1, 384)):
        for copy in copies[i]:
            copy.wait()
        weight_product(out_ref, at, scratch[2 * i], scratch[2 * i + 1])
    out_ref[:, 528:, :] = jnp.zeros((4, 48, D), BF16)


def qkv_weights_kernel(*refs):
    gain_far, zero, one, lefts, rights, (out_ref,), (left, right, gain, sems) = split_refs(
        refs, 1, 3, 3, 3, 3, 1, 4
    )
    copies = load_rows(sems, [(a, g) for a, g, _ in (zero, one)], (lefts, rights), left, right)
    section = lax.axis_index("section")
    for layer, (_, _, own) in enumerate((zero, one)):

        @pl.when(section == layer)
        def _():
            fetch(own, gain, sems.at[8]).wait()

    gains = (gain[...].astype(F32) + gain_far[0][...].astype(F32)).astype(BF16)
    for shard in range(4):
        out_ref[shard, 288:304, :] = gains
        out_ref[shard, 304:, :] = jnp.zeros((16, D), BF16)
    for copy in copies:
        copy.wait()
    weight_product(out_ref, 0, left, right)


def assemble_kernel(fin_ref, up_ref, out_ref, down_ref, qkv_ref, gains_ref):
    for half in range(2):
        rows = slice(half * 96, half * 96 + 96)
        for block in range(3):
            cols = slice(block * D, (block + 1) * D)
            up_ref[rows, cols] = fin_ref[half, block * 96 : block * 96 + 96, :].astype(F32)
            at = MLP_ROWS + block * 96
            qkv_ref[rows, cols] = fin_ref[half, at : at + 96, :].astype(F32)
        out_ref[rows, :] = fin_ref[half, 288:384, :].astype(F32)
        down_ref[half * 144 : half * 144 + 144, :] = fin_ref[half, 384:528, :].astype(F32)
    gain_rows = slice(MLP_ROWS + 288, MLP_ROWS + 304)
    gains_ref[...] = fin_ref[0, gain_rows, :].astype(F32) + fin_ref[1, gain_rows, :].astype(F32)


def here():
    return lax.axis_index("section"), lax.axis_index("ctx"), lax.axis_index("wshard")


def flip(index, delta):
    for bit in (1, 2, 4, 8):
        if delta & bit:
            index = index + bit - 2 * bit * lax.rem(index // bit, 2)
    return index


def greet(peers):
    barrier = pltpu.get_barrier_semaphore()
    for peer in peers:
        pl.semaphore_signal(barrier, inc=1, device_id=peer, device_id_type=MESH)
    pl.semaphore_wait(barrier, len(peers))


def remote(src, dst, send, recv, peer):
    return pltpu.make_async_remote_copy(
        src_ref=src, dst_ref=dst, send_sem=send, recv_sem=recv, device_id=peer, device_id_type=MESH
    )


class Lines:
    count = 112

    def __init__(self, send, recv):
        self.send, self.recv, self.used, self.waits = send, recv, 0, []

    def make(self, src, dst, peer):
        at = self.used
        self.used += 1
        return remote(src, dst, self.send.at[at], self.recv.at[at], peer)

    def put(self, src, dst, peer):
        copy = self.make(src, dst, peer)
        copy.start()
        return copy

    def keep(self, src, dst):
        at = self.used
        self.used += 1
        copy = pltpu.make_async_copy(src, dst, self.send.at[at])
        copy.start()
        return copy


SEMS = [DMA((Lines.count,)), DMA((Lines.count,))]
ids = iter(range(1, 64))


def exchange_call(kernel, args, outs, scratch, collective_id, name):
    return pl.pallas_call(
        kernel,
        out_shape=outs,
        in_specs=[ANY] * len(args),
        out_specs=jax.tree.map(lambda _: ANY, outs),
        scratch_shapes=SEMS + list(scratch),
        compiler_params=pltpu.CompilerParams(
            collective_id=collective_id, has_side_effects=True, vmem_limit_bytes=VMEM_LIMIT
        ),
        name=name,
    )(*args)


def sibling_of(s, c, z):
    return (s, flip(c, 1), z)


def z_peers():
    s, c, z = here()
    return [(s, c, lax.rem(z + r, 4)) for r in (1, 3, 2)]


def beside_peers():
    s, c, z = here()
    return [(1 - s, c, z), (1 - s, flip(c, 8), z)]


class Gather:
    def __init__(self, lines, own, full):
        s, c, z = here()
        rows, cols = full.shape[2] // 2, full.shape[3] // 2
        self.rows = pl.ds(pl.multiple_of(lax.rem(c, 2) * rows, 16), rows)
        self.cols = [
            pl.ds(pl.multiple_of(side * cols, 128), cols) for side in (c // 8, 1 - c // 8)
        ]
        self.halves = [pl.ds(0, cols), pl.ds(cols, cols)]
        self.lines, self.full = lines, full
        self.sibling = sibling_of(s, c, z)
        after, before, _ = z_peers()
        self.step = []
        for cut, order in ((0, (after, before)), (1, (after, before))):
            where = full.at[s, z, self.rows, self.halves[cut]]
            piece = own.at[self.rows, self.halves[cut]]
            self.step.append([lines.put(piece, where, peer) for peer in order])
        self.peers = (after, before)
        self.aside = [self.beside(own.at[self.rows, self.cols[0]], z)]
        whole = full.at[s, z, self.rows]
        self.passed = [lines.put(own.at[self.rows], whole, self.sibling)]
        self.kept = lines.keep(own.at[self.rows], whole)
        self.sent = []

    def beside(self, src, z):
        s, _, _ = here()
        where = self.full.at[s, z, self.rows, self.cols[0]]
        return [self.lines.put(src, where, peer) for peer in beside_peers()]

    def from_neighbours(self):
        s, _, z = here()
        self.sources = [lax.rem(z + 3, 4), lax.rem(z + 1, 4)]
        self.second = []
        for side in (0, 1):
            self.step[side][side].wait_recv()
            block = self.full.at[s, self.sources[side], self.rows, self.halves[side]]
            self.second.append(self.lines.put(block, block, self.peers[side]))
        for side in (0, 1):
            self.step[1 - side][side].wait_recv()
            self.onward(self.sources[side])

    def onward(self, z):
        s, _, _ = here()
        block = self.full.at[s, z, self.rows]
        self.passed.append(self.lines.put(block, block, self.sibling))
        self.aside.append(self.beside(block.at[:, self.cols[0]], z))

    def from_opposite(self):
        _, _, z = here()
        for copy in self.second:
            copy.wait_recv()
        self.onward(lax.rem(z + 2, 4))

    def from_beside(self):
        s, _, z = here()
        for copies, source in zip(self.aside, (z, *self.sources, lax.rem(z + 2, 4))):
            for i, copy in enumerate(copies):
                copy.wait_recv()
                block = self.full.at[1 - s, source, self.rows, self.cols[i]]
                self.passed.append(self.lines.put(block, block, self.sibling))

    def finish(self):
        self.kept.wait()
        for copies in (*self.step, *self.aside, self.second):
            for copy in copies:
                copy.wait_send()
        for copy in self.passed:
            copy.wait()


def run_gathers(gathers):
    for gather in gathers:
        gather.from_neighbours()
    for gather in gathers:
        gather.from_opposite()
    for gather in gathers:
        gather.from_beside()
    for gather in gathers:
        gather.finish()


def full_shapes(weights):
    return [sds((2, 4, *w.shape), BF16) for w in weights]


def gather_peers():
    return [sibling_of(*here()), *z_peers()[:2], *beside_peers()]


class Scatter:
    def __init__(self, lines, comb, got):
        s, c, z = here()
        self.copies = [
            lines.put(comb.at[peer[2]], got.at[i], peer) for i, peer in enumerate(z_peers())
        ]

    def finish(self):
        for copy in self.copies:
            copy.wait()


def scatter_shapes(combs):
    return [sds((3, *comb.shape[1:]), BF16) for comb in combs]


def shard_loads(full, layer, dst, sems):
    rows = full.shape[2]
    return [
        pltpu.make_async_copy(full.at[layer, i], dst.at[pl.ds(i * rows, rows)], sems.at[i])
        for i in range(4)
    ]


class Spread:
    order = [14, 10, 12, 8, 6, 4, 2]

    def __init__(self, lines, qkv_ref, q_ref, kv_ref):
        s, c, z = here()
        self.lines, self.kv_ref = lines, kv_ref
        self.sibling = sibling_of(s, c, z)
        kv_rows = pl.ds(GW, 2 * GW)
        q_rows = pl.ds(0, GW)
        self.kv_sends, self.q_sends = {}, []
        for delta in self.order:
            peer = (s, flip(c, delta), z)
            self.kv_sends[delta] = lines.put(qkv_ref.at[peer[1] // 4, kv_rows], kv_ref.at[c], peer)
            if delta % 4 == 0:
                self.q_sends.append(lines.put(qkv_ref.at[peer[1] // 4, q_rows], q_ref.at[c // 4], peer))
        self.passed = [lines.put(qkv_ref.at[c // 4, kv_rows], kv_ref.at[c], self.sibling)]
        self.kept = [
            lines.keep(qkv_ref.at[c // 4, kv_rows], kv_ref.at[c]),
            lines.keep(qkv_ref.at[c // 4, q_rows], q_ref.at[c // 4]),
        ]

    def finish(self):
        _, c, _ = here()
        for delta in reversed(self.order):
            self.kv_sends[delta].wait_recv()
            block = self.kv_ref.at[flip(c, delta)]
            self.passed.append(self.lines.put(block, block, self.sibling))
        for copy in self.kept + self.q_sends + self.passed:
            copy.wait()
        for copy in self.kv_sends.values():
            copy.wait_send()


class Turn:
    def __init__(self, lines, x_ref, o_ref):
        s, c, z = here()
        peers = [(s, flip(c, delta), z) for delta in (4, 8, 12)]
        self.copies = [lines.put(x_ref.at[peer[1] // 4], o_ref.at[c // 4], peer) for peer in peers]
        self.copies.append(lines.keep(x_ref.at[c // 4], o_ref.at[c // 4]))

    def finish(self):
        for copy in self.copies:
            copy.wait()


def forward_kernel(*refs):
    (cos, sin, inputs, gain), own, per_layer, full, (gains,), scratch = split_refs(refs, 4, 4, 22, 4, 1, 14)
    x_s, w_q, w_o, w_u, w_d, qkv_s, low_s, s_ref, got_gain, load_sem, in_sem, send, recv, gain_s = scratch
    s, c, z = here()
    lines = Lines(send, recv)
    x_load = fetch(inputs.at[s, 0], x_s, in_sem.at[0])
    across = [(1 - s, c, lax.rem(z + r, 4)) for r in (1, 3, 2)]
    ctx_peers = [(s, flip(c, delta), z) for delta in range(2, CTX, 2)]
    greet([*gather_peers(), z_peers()[2], *across, *ctx_peers])

    first = Gather(lines, own[0], full[0])
    gain_copies = [
        lines.put(gain, got_gain.at[s, z], peer) for peer in (*z_peers(), beside_peers()[0], *across)
    ]
    gain_copies.append(lines.keep(gain, got_gain.at[s, z]))
    run_gathers([first])
    rest = [Gather(lines, own[i], full[i]) for i in (2, 1, 3)]

    targets = (w_q, w_o, w_u, w_d)
    loads = [
        [shard_loads(full[i], layer, targets[i], load_sem.at[layer, i]) for i in range(4)]
        for layer in range(2)
    ]

    def begin(layer, which):
        for i in which:
            for copy in loads[layer][i]:
                copy.start()

    def loaded(layer, i):
        for copy in loads[layer][i]:
            copy.wait()

    begin(0, [0])
    for copy in gain_copies:
        copy.wait()
    for layer in range(2):
        total = got_gain[layer, 0].astype(F32) + got_gain[layer, 1].astype(F32)
        gain_s[layer] = total + got_gain[layer, 2].astype(F32) + got_gain[layer, 3].astype(F32)
    gains[...] = gain_s[...]
    x_load.wait()
    source = x_s
    for layer in range(2):
        q, kv, wide, totals, ot, out, hidden, gate_up, normed_two, product, normed = per_layer[layer::2]
        project(
            source, gain_s[layer, 0:1, :], cos, sin, w_q, lambda: loaded(layer, 0), qkv_s.at[layer], normed
        )
        if layer == 0:
            begin(1, [0])
        spread = Spread(lines, qkv_s.at[layer], q, kv)
        spread.finish()
        if layer == 0:
            for gather in rest:
                gather.from_neighbours()
        attend(q, kv, low_s.at[layer], wide, totals, s_ref)
        if layer == 0:
            for gather in rest:
                gather.from_opposite()
        turn = Turn(lines, low_s.at[layer], ot)
        turn.finish()
        if layer == 0:
            for gather in rest:
                gather.from_beside()
            for gather in rest:
                gather.finish()
            begin(0, [1, 2, 3])
        mlp(
            ot, source, gain_s[layer, 1:2, :], w_o, w_u, w_d, lambda i: loaded(layer, i + 1),
            out, hidden, gate_up, normed_two, product,
        )
        if layer == 0:
            begin(1, [1, 2, 3])
        source = out


LAYER_SHAPES = (
    sds((4, GW, ROWS), BF16),
    sds((CTX, 2 * GW, ROWS), BF16),
    sds((4, GW, ROWS), F32),
    sds((GH, 8, 512), F32),
    sds((4, GW, ROWS), BF16),
    sds((ROWS, D), BF16),
    sds((ROWS, D), F32),
    sds((ROWS, 2 * FF), F32),
    sds((D, ROWS), BF16),
    sds((FF, ROWS), BF16),
    sds((D, ROWS), BF16),
)


def forward(inputs, gain, weights, tables):
    per_layer = [shape for shape in LAYER_SHAPES for _ in range(2)]
    full = full_shapes(weights)
    scratch = [
        pltpu.VMEM((ROWS, D), BF16),
        *[pltpu.VMEM((4 * w.shape[0], w.shape[1]), BF16) for w in weights],
        pltpu.VMEM((2, 4, 3 * GW, ROWS), BF16),
        pltpu.VMEM((2, 4, GW, ROWS), BF16),
        pltpu.VMEM((2048, 512), F32),
        pltpu.VMEM((2, 4, 16, D), BF16),
        DMA((2, 4, 4)),
        DMA((1,)),
        DMA((192,)),
        DMA((192,)),
        pltpu.VMEM((2, 16, D), F32),
    ]
    res = pl.pallas_call(
        forward_kernel,
        out_shape=[*per_layer, *full, sds((2, 16, D), F32)],
        in_specs=[VM, VM, ANY, ANY] + [ANY] * 4,
        out_specs=[VM] * 22 + [ANY] * 4 + [VM],
        scratch_shapes=scratch,
        compiler_params=pltpu.CompilerParams(
            collective_id=next(ids), has_side_effects=True, vmem_limit_bytes=VMEM_LIMIT
        ),
        name="forward",
    )(*tables, inputs, gain, *weights)
    layers = [res[layer:22:2] for layer in range(2)]
    return layers, res[22:26], res[26]


class Meet:
    def __init__(self, lines, zero, one, sib, far, both):
        s, c, z = here()
        self.core = core = lax.rem(c, 2)
        self.lines, self.far, self.both = lines, far, both
        self.sibling = sibling_of(s, c, z)
        peer = (1 - s, flip(c, 8) * core + c * (1 - core), z)
        first = lines.used
        for layer, (near, other) in enumerate(((zero, one), (one, zero))):
            lines.used = first

            @pl.when(s == layer)
            def _():
                self.apart = lines.put(other, far, peer)
                if sib is not None:
                    self.close = lines.put(self.half(near), sib, self.sibling)

        lines.used = first
        self.apart = lines.make(zero, far, peer)
        if sib is not None:
            self.close = lines.make(sib, sib, self.sibling)

    def half(self, ref):
        return ref.at[:, 1 - self.core] if len(ref.shape) == 4 else ref

    def forward(self):
        self.apart.wait_recv()
        if self.both is not None:
            self.passed = self.lines.put(self.half(self.far), self.both, self.sibling)

    def finish(self):
        self.apart.wait_send()
        if self.both is not None:
            self.close.wait()
            self.passed.wait()


def meet_peers():
    return [sibling_of(*here()), *beside_peers()]


def half_shape(a):
    return sds((a.shape[0], *a.shape[2:]) if a.ndim == 4 else a.shape, BF16)


def meet_shapes(zero):
    return [shape(a) for shape in (half_shape, lambda a: sds(a.shape, BF16), half_shape) for a in zero]


class Show:
    def __init__(self, lines, zero, one, out):
        s, c, z = here()
        first = lines.used
        for layer, (near, other) in enumerate(((zero, one), (one, zero))):
            lines.used = first

            @pl.when(s == layer)
            def _():
                lines.put(other, out.at[s], (1 - s, c, z))
                lines.keep(near, out.at[s])

        lines.used = first
        self.copy = lines.make(zero, out.at[s], (1 - s, c, z))
        self.kept = pltpu.make_async_copy(zero, out.at[s], lines.send.at[lines.used])
        lines.used += 1

    def finish(self):
        self.copy.wait()
        self.kept.wait()


def turn_kernel(acts, shows, *refs):
    (x_ref,), zero, one, shown, (o_ref,), taken, outs, (send, recv) = split_refs(
        refs, 1, acts, acts, 2 * shows, 1, 3 * acts, shows, 2
    )
    s, c, z = here()
    lines = Lines(send, recv)
    greet([(s, flip(c, delta), z) for delta in (4, 8, 12)] + meet_peers())
    turn = Turn(lines, x_ref, o_ref)
    meets = [Meet(lines, *five) for five in zip(zero, one, *split_refs(taken, acts, acts, acts))]
    shown = [Show(lines, *shown, out) for out in outs]
    turn.finish()
    for meet in meets:
        meet.forward()
    for work in meets + shown:
        work.finish()


def turn(x, zero=(), one=(), show=()):
    args = [x, *zero, *one, *show]
    counts = len(zero), len(show) // 2
    outs = [sds((4, GW, ROWS), BF16)] + meet_shapes(zero)
    outs += [sds((2, *a.shape), BF16) for a in show[::2]]
    res = exchange_call(functools.partial(turn_kernel, *counts), args, outs, [], next(ids), "turn")
    return res[0], *split_refs(res[1:], 3 * counts[0], counts[1])


def meet_kernel(*refs):
    zero, one, taken, (out,), (send, recv) = split_refs(refs, 3, 3, 4, 1, 2)
    lines = Lines(send, recv)
    greet(meet_peers())
    work = [
        Meet(lines, zero[0], one[0], *taken[:3]),
        Meet(lines, zero[1], one[1], None, taken[3], None),
    ]
    shown = Show(lines, zero[2], one[2], out)
    for meet in work:
        meet.forward()
    for meet in (*work, shown):
        meet.finish()


def meet(zero, one):
    outs = meet_shapes(zero[:1]) + [sds(zero[1].shape, BF16), sds((2, *zero[2].shape), BF16)]
    return exchange_call(meet_kernel, (*zero, *one), outs, [], next(ids), "meet")


def scatter_kernel(count, *refs):
    combs, got, (send, recv) = split_refs(refs, count, count, 2)
    lines = Lines(send, recv)
    greet(z_peers())
    for work in [Scatter(lines, *two) for two in zip(combs, got)]:
        work.finish()


def scatter(combs):
    kernel = functools.partial(scatter_kernel, len(combs))
    return exchange_call(kernel, combs, scatter_shapes(combs), [], next(ids), "scatter")


def return_kernel(count, *refs):
    (dq_ref, dkv_ref), combs, (dqo_ref, sums_ref), got, (send, recv, mine, theirs, total) = split_refs(
        refs, 2, count, 2, count, 5
    )
    s, c, z = here()
    lines = Lines(send, recv)
    core = lax.rem(c, 2)
    sibling = sibling_of(s, c, z)
    peers = {delta: (s, flip(c, delta), z) for delta in range(2, CTX, 2)}
    greet([sibling, *peers.values(), *(z_peers() if count else [])])
    passed = [lines.put(dkv_ref.at[2 * i + 1 - core], theirs.at[i], sibling) for i in range(8)]
    loads = [lines.keep(dkv_ref.at[2 * i + core], mine.at[i]) for i in range(8)]
    sends = [
        lines.put(dq_ref.at[peers[delta][1] // 4], dqo_ref.at[c // 4], peers[delta]) for delta in (4, 8, 12)
    ]
    scatters = [Scatter(lines, *two) for two in zip(combs, got)]
    kept = [lines.keep(dq_ref.at[c // 4], dqo_ref.at[c // 4])]
    for i in range(8):
        loads[i].wait()
        passed[i].wait()
        total[i] = (mine[i].astype(F32) + theirs[i].astype(F32)).astype(BF16)
    for delta in (14, 10, 12, 8, 6, 4, 2):
        sends.append(lines.put(total.at[peers[delta][1] // 2], sums_ref.at[c // 2], peers[delta]))
    kept.append(lines.keep(total.at[c // 2], sums_ref.at[c // 2]))
    for copy in kept + sends:
        copy.wait()
    for work in scatters:
        work.finish()


def give_back(dq, dkv, combs):
    block = pltpu.VMEM((8, 2 * GW, ROWS), BF16)
    outs = [sds((4, GW, ROWS), BF16), sds((8, 2 * GW, ROWS), BF16)] + scatter_shapes(combs)
    kernel = functools.partial(return_kernel, len(combs))
    res = exchange_call(kernel, [dq, dkv, *combs], outs, [block] * 3, next(ids), "give_back")
    return res[0], res[1], res[2:]


QUARTER = SUM_ROWS // 4


def finish_kernel(comb_m, got_m, comb_q, got_q, fin, send, recv, load, terms, own_sum, parts, red):
    s, c, z = here()
    lines = Lines(send, recv)
    core = lax.rem(c, 2)
    sibling = sibling_of(s, c, z)
    near = {delta: (s, flip(c, delta), z) for delta in range(2, CTX, 2)}
    loads = []
    for part, (comb, got, at, rows) in enumerate(
        ((comb_m, got_m, 0, MLP_ROWS), (comb_q, got_q, MLP_ROWS, QKV_ROWS))
    ):
        rows = pl.ds(at, rows)
        loads.append(fetch(comb.at[z], terms.at[0, rows], load.at[4 * part]))
        loads += [fetch(got.at[i], terms.at[i + 1, rows], load.at[4 * part + i + 1]) for i in range(3)]
    greet([sibling, *near.values()])
    for copy in loads:
        copy.wait()
    for at in range(0, SUM_ROWS, 128):
        rows = slice(at, at + 128)
        both = terms[0, rows].astype(F32) + terms[1, rows].astype(F32)
        both += terms[2, rows].astype(F32) + terms[3, rows].astype(F32)
        own_sum[rows] = both.astype(BF16)

    def block(at):
        rows = pl.ds(pl.multiple_of(lax.rem(at // 2, 4) * QUARTER, 16), QUARTER)
        return rows, pl.ds(pl.multiple_of(at // 8 * (D // 2), 128), D // 2)

    order = [14, 10, 12, 8, 6, 4, 2]
    sends = [lines.put(own_sum.at[block(near[delta][1])], parts.at[c // 2], near[delta]) for delta in order]
    lines.keep(own_sum.at[block(c)], parts.at[c // 2]).wait()
    for copy in sends:
        copy.wait()
    for at in range(0, QUARTER, 112):
        rows = slice(at, at + 112)
        total = parts[0, rows].astype(F32)
        for i in range(1, 8):
            total += parts[i, rows].astype(F32)
        red[rows] = total.astype(BF16)
    target = fin.at[core]
    kept = lines.keep(red, target.at[block(c)])
    passed = [lines.put(red, target.at[block(c)], sibling)]
    shown = {delta: lines.put(red, target.at[block(c)], near[delta]) for delta in order}
    for delta in reversed(order):
        shown[delta].wait_recv()
        piece = target.at[block(flip(c, delta))]
        passed.append(lines.put(piece, piece, sibling))
    kept.wait()
    for copy in shown.values():
        copy.wait_send()
    for copy in passed:
        copy.wait()


def finish(*args):
    scratch = [
        DMA((8,)),
        pltpu.VMEM((4, SUM_ROWS, D), BF16),
        pltpu.VMEM((SUM_ROWS, D), BF16),
        pltpu.VMEM((8, QUARTER, D // 2), BF16),
        pltpu.VMEM((QUARTER, D // 2), BF16),
    ]
    return exchange_call(
        finish_kernel, args, sds((2, SUM_ROWS, D), BF16), scratch, next(ids), "finish"
    )


def rope_tables():
    positions = (lax.axis_index("ctx") * ROWS + lax.iota(jnp.int32, ROWS)).astype(F32)
    frequency = 1.0 / 160000.0 ** (jnp.arange(HEAD_DIM // 2, dtype=F32) * 2.0 / HEAD_DIM)
    angles = frequency[:, None] * positions[None, :]
    return jnp.cos(angles), jnp.sin(angles)


def weight_scratch(*shapes):
    return [pltpu.VMEM(shape, BF16) for shape in shapes]


def by_core(a):
    return a.reshape(4, 2, -1, ROWS)


def mlp_back(layer, grad, stored, gains, late):
    hidden, gate_up = stored[5:]
    return compute_call(
        functools.partial(mlp_back_kernel, layer),
        (grad, hidden, gate_up, gains[1], *late),
        (sds((D, ROWS), BF16), sds((ROWS, D), F32), sds((ROWS, 2 * FF), BF16),
         sds((ROWS, D), BF16), sds((1, D), F32)),
        [*weight_scratch((D, D), (D, 2 * FF), (FF, D)), DMA((3,))],
        name="mlp_back",
        far=3,
    )


def attend_back(d_o, stored):
    _, q, kv, wide, totals = stored[:5]
    return compute_call(
        attend_back_kernel,
        (q, kv, wide, totals, d_o),
        (sds((4, GW, ROWS), BF16), sds((CTX, 2 * GW, ROWS), BF16)),
        name="attend_back",
    )


def qkv_back(layer, dq, dkv, stored, gains, tables, grad_hidden, d_gain_two, w_qkv):
    return compute_call(
        functools.partial(qkv_back_kernel, layer),
        (dq, dkv, stored[0], gains[0], *tables, grad_hidden, d_gain_two, w_qkv),
        (sds((ROWS, D), BF16), sds((ROWS, 3 * D), BF16), sds((16, D), BF16)),
        [pltpu.VMEM((3 * D, ROWS), F32), *weight_scratch((D, 3 * D)), DMA],
        name="qkv_back",
        far=1,
    )


def local(inputs, cotangent, attn_gain, qkv_weight, out_weight, mlp_gain, up_weight, down_weight):
    first = lax.axis_index("section") == 0
    z = lax.axis_index("wshard")
    cot = jnp.where(first, cotangent[0, 0], cotangent[1, 0])
    gain = jnp.concatenate([attn_gain, mlp_gain], axis=0)
    lanes = lax.broadcasted_iota(jnp.int32, (2, 4, 192), 1) == z
    gain = jnp.where(lanes, gain[:, None, :], jnp.zeros((), BF16)).reshape(2, D)
    gain = jnp.pad(gain, ((0, 14), (0, 0)))
    x = jnp.where(first, inputs[0, 0], inputs[1, 0])
    tables = rope_tables()
    layers, full, gains = forward(
        inputs, gain, [w[0] for w in (qkv_weight, out_weight, up_weight, down_weight)], tables
    )
    full = [w.reshape(2, -1, w.shape[-1]) for w in full]
    w_qkv, late = full[0], full[1:]
    gains = [[gains[layer, row : row + 1] for row in range(2)] for layer in range(2)]
    kept, lefts_all = [], []
    for source, layer in zip((x, layers[0][5]), layers):
        q, kv, wide, totals, ot, out, hidden, gate_up, normed_two, product, normed = layer
        kept.append((source, q, kv, wide, totals, hidden, gate_up))
        lefts_all.append([by_core(a) for a in (normed_two, product, ot, normed)])
    (kept_zero, kept_one), (left_zero, left_one) = kept, lefts_all
    mid, end = layers[0][5], layers[1][5]

    d_ot, grad_hidden, gg_one, branch_one, d_gain = mlp_back(1, cot, kept_one, gains[1], late)
    d_o, lefts, (activations,) = turn(
        d_ot.reshape(4, GW, ROWS), zero=left_zero, one=left_one, show=(mid, end)
    )
    dq, dkv = attend_back(d_o, kept_one)
    dq, dkv, _ = give_back(dq, dkv, [])
    grad_mid, gp_one, gains_one = qkv_back(
        1, dq, dkv, kept_one, gains[1], tables, grad_hidden, d_gain, w_qkv
    )

    d_ot, grad_hidden, gg_zero, branch_zero, d_gain = mlp_back(0, grad_mid, kept_zero, gains[0], late)
    rights_zero, rights_one = [gg_zero, grad_mid, branch_zero], [gg_one, cot, branch_one]
    d_o, rights, _ = turn(d_ot.reshape(4, GW, ROWS), zero=rights_zero, one=rights_one)
    mlp_lefts = [lefts[4 * i + j] for i in range(3) for j in range(3)]
    heights = (96, 144, 96)
    comb_mlp = compute_call(
        mlp_weights_kernel,
        (*left_zero[:3], *rights_zero, *left_one[:3], *rights_one, *mlp_lefts, *rights),
        sds((4, MLP_ROWS, D), BF16),
        [
            pltpu.VMEM(shape, BF16)
            for height, right in zip(heights, rights_zero)
            for shape in ((4, height, 4 * ROWS), (4 * ROWS, right.shape[1]))
        ]
        + [DMA((3, 8))],
        name="mlp_weights",
        far=30,
    )
    dq, dkv = attend_back(d_o, kept_zero)
    dq, dkv, (got_mlp,) = give_back(dq, dkv, [comb_mlp])
    grad_start, gp_zero, gains_zero = qkv_back(
        0, dq, dkv, kept_zero, gains[0], tables, grad_hidden, d_gain, w_qkv
    )
    *gp_rest, gains_far, input_grads = meet(
        (gp_zero, gains_zero, grad_start), (gp_one, gains_one, grad_mid)
    )
    comb_qkv = compute_call(
        qkv_weights_kernel,
        (gains_far, left_zero[3], gp_zero, gains_zero, left_one[3], gp_one, gains_one,
         *lefts[3::4], *gp_rest),
        sds((4, QKV_ROWS, D), BF16),
        [*weight_scratch((4, 96, 4 * ROWS), (4 * ROWS, 3 * D), (16, D)), DMA((9,))],
        name="qkv_weights",
        far=12,
    )
    (got_qkv,) = scatter([comb_qkv])
    fin = finish(comb_mlp, got_mlp, comb_qkv, got_qkv)
    grad_up, grad_out, grad_down, grad_qkv, gain_sums = compute_call(
        assemble_kernel,
        (fin,),
        [sds(shape, F32) for shape in ((192, 3 * D), (192, D), (288, D), (192, 3 * D), (16, D))],
        name="assemble",
    )
    gain_sums = lax.dynamic_slice_in_dim(gain_sums[:2], lax.axis_index("wshard") * 192, 192, 1)
    return (
        activations[None, :, None],
        input_grads[None, :, None],
        gain_sums[0:1],
        grad_qkv[None],
        grad_out[None],
        gain_sums[1:2],
        grad_up[None],
        grad_down[None],
    )


def solution(mesh):
    global ids
    ids = iter(range(1, 64))
    placed = (
        P(None, "wshard", "ctx", None),
        P(None, "wshard", "ctx", None),
        P("section", "wshard"),
        P("section", "wshard", None),
        P("section", "wshard", None),
        P("section", "wshard"),
        P("section", "wshard", None),
        P("section", "wshard", None),
    )
    return jax.shard_map(
        local,
        mesh=mesh,
        in_specs=placed,
        out_specs=(
            P("section", None, "wshard", "ctx", None),
            P("section", None, "wshard", "ctx", None),
            P("section", "wshard"),
            P("section", "wshard", None),
            P("section", "wshard", None),
            P("section", "wshard"),
            P("section", "wshard", None),
            P("section", "wshard", None),
        ),
        check_vma=False,
    )
```

```python
import functools

import jax
import jax.numpy as jnp
from jax import lax
from jax.experimental import pallas as pl
from jax.experimental.pallas import tpu as pltpu
from jax.sharding import PartitionSpec as P

D = 768
HEADS = 12
HEAD_DIM = 64
FF = 1152
ROWS = 128
GROUPS = 4
GH = HEADS // GROUPS
GW = GH * HEAD_DIM
CTX = 16
SCALE = HEAD_DIM ** (-0.5)
F32 = jnp.float32
BF16 = jnp.bfloat16
MESH = pl.DeviceIdType.MESH
DMA = pltpu.SemaphoreType.DMA
ANY = pl.BlockSpec(memory_space=pl.ANY)
VM = pl.BlockSpec(memory_space=pltpu.VMEM)
VMEM_LIMIT = 60 * 1024 * 1024


def dot(a, b):
    return jnp.dot(a, b, preferred_element_type=F32)


def dot_nt(a, b):
    return lax.dot_general(a, b, (((1,), (1,)), ((), ())), preferred_element_type=F32)


def sds(shape, dtype):
    return jax.ShapeDtypeStruct(shape, dtype)


def compute_call(kernel, args, outs, name):
    return pl.pallas_call(
        kernel,
        out_shape=outs,
        in_specs=[VM] * len(args),
        out_specs=jax.tree.map(lambda _: VM, outs),
        compiler_params=pltpu.CompilerParams(vmem_limit_bytes=VMEM_LIMIT),
        name=name,
    )(*args)


def fetch(src, dst, sem):
    copy = pltpu.make_async_copy(src, dst, sem)
    copy.start()
    return copy


def turned_low(x):
    return x.astype(F32).T.astype(BF16)


def norm_parts(source):
    centered = source - jnp.mean(source, axis=-1, keepdims=True)
    variance = jnp.mean(centered * centered, axis=-1, keepdims=True)
    rstd = lax.rsqrt(variance + 1e-05)
    return centered * rstd, rstd


def norm_back(grad, normalized, rstd, gain):
    inner = grad * gain
    mean_one = jnp.mean(inner, axis=-1, keepdims=True)
    mean_two = jnp.mean(inner * normalized, axis=-1, keepdims=True)
    grad_gain = jnp.sum(grad * normalized, axis=0, keepdims=True)
    return rstd * (inner - mean_one - normalized * mean_two), grad_gain


def split_refs(refs, *counts):
    refs = list(refs)
    out = []
    for count in counts:
        out.append(refs[:count])
        refs = refs[count:]
    return out


def project(x_ref, gain, cos_ref, sin_ref, w_ref, loaded, qkv_ref, normed_ref):
    normalized, _ = norm_parts(x_ref[...].astype(F32))
    normed = (normalized * gain).astype(BF16)
    normed_ref[...] = turned_low(normed)
    loaded()
    cos = cos_ref[...]
    sin = sin_ref[...]
    for part in range(3):
        for block in range(3):
            at = part * D + block * 256
            turned = dot(normed, w_ref[:, at : at + 256]).T
            for head_at in range(4):
                head = block * 4 + head_at
                one = turned[head_at * 64 : head_at * 64 + 32]
                two = turned[head_at * 64 + 32 : head_at * 64 + 64]
                if part < 2:
                    one, two = one * cos - two * sin, two * cos + one * sin
                if part == 0:
                    one, two = one * SCALE, two * SCALE
                row = part * GW + (head % GH) * HEAD_DIM
                qkv_ref[head // GH, row : row + 32, :] = one.astype(BF16)
                qkv_ref[head // GH, row + 32 : row + 64, :] = two.astype(BF16)


CHUNK = 256
CHUNKS = 2048 // CHUNK
PAIR = CHUNK // ROWS


def attend(q_ref, kv_ref, low_ref, wide_ref, totals_ref, s_ref):
    @pl.loop(0, GH)
    def _(h):
        at = pl.multiple_of(h * HEAD_DIM, HEAD_DIM)
        value_at = pl.multiple_of(h * HEAD_DIM + GW, HEAD_DIM)
        qt = jnp.concatenate([q_ref[i, pl.ds(at, HEAD_DIM), :] for i in range(4)], axis=1)
        top = jnp.full((8, 512), -jnp.inf, F32)
        for c in range(CHUNKS):
            keys = jnp.concatenate(
                [kv_ref[c * PAIR + i, pl.ds(at, HEAD_DIM), :].T for i in range(PAIR)], axis=0
            )
            scores = dot(keys, qt)
            s_ref[c * CHUNK : (c + 1) * CHUNK, :] = scores
            top = jnp.maximum(top, jnp.max(scores.reshape(CHUNK // 8, 8, 512), axis=0))
        top = jnp.max(top, axis=0, keepdims=True)
        total = jnp.zeros((8, 512), F32)
        acc = jnp.zeros((HEAD_DIM, 512), F32)
        for c in range(CHUNKS):
            p = jnp.exp(s_ref[c * CHUNK : (c + 1) * CHUNK, :] - top)
            total = total + jnp.sum(p.reshape(CHUNK // 8, 8, 512), axis=0)
            values = jnp.concatenate(
                [kv_ref[c * PAIR + i, pl.ds(value_at, HEAD_DIM), :] for i in range(PAIR)], axis=1
            )
            acc = acc + dot(values, p.astype(BF16))
        total = jnp.sum(total, axis=0, keepdims=True)
        out = acc / total
        totals_ref[h] = jnp.broadcast_to(top + jnp.log(total), (8, 512))
        for i in range(4):
            piece = out[:, i * ROWS : (i + 1) * ROWS]
            wide_ref[i, pl.ds(at, HEAD_DIM), :] = piece
            low_ref[i, pl.ds(at, HEAD_DIM), :] = piece.astype(BF16)


def attend_back(start, stop, q_ref, kv_ref, wide_ref, totals_ref, do_ref, dq_ref, dkv_ref):
    @pl.loop(start, stop)
    def _(h):
        at = pl.multiple_of(h * HEAD_DIM, HEAD_DIM)
        value_at = pl.multiple_of(h * HEAD_DIM + GW, HEAD_DIM)
        out_at = pl.multiple_of(h * ROWS, ROWS)
        qt = jnp.concatenate([q_ref[i, pl.ds(at, HEAD_DIM), :] for i in range(4)], axis=1)
        dot_t = jnp.concatenate([do_ref[i, pl.ds(at, HEAD_DIM), :] for i in range(4)], axis=1)
        wide = jnp.concatenate([wide_ref[i, pl.ds(at, HEAD_DIM), :] for i in range(4)], axis=1)
        delta = jnp.sum(wide * dot_t.astype(F32), axis=0, keepdims=True)
        totals = totals_ref[h, 0:1, :]
        zero = jnp.zeros((512, HEAD_DIM), BF16)
        sides = jnp.concatenate(
            [
                jnp.concatenate([qt.T, zero], axis=1),
                jnp.concatenate([zero, dot_t.T], axis=1),
            ],
            axis=0,
        )

        def step(c, acc):
            keys_t = [kv_ref[c * PAIR + i, pl.ds(at, HEAD_DIM), :] for i in range(PAIR)]
            values_t = [kv_ref[c * PAIR + i, pl.ds(value_at, HEAD_DIM), :] for i in range(PAIR)]
            keys = jnp.concatenate([k.T for k in keys_t], axis=0)
            values = jnp.concatenate([v.T for v in values_t], axis=0)
            p = jnp.exp(dot(keys, qt) - totals)
            ds = (p * (dot(values, dot_t) - delta)).astype(BF16)
            both = jnp.concatenate([ds, p.astype(BF16)], axis=1)
            grads = dot(both, sides).astype(BF16)
            for i in range(PAIR):
                dkv_ref[c * PAIR + i, pl.ds(out_at, ROWS), :] = grads[i * ROWS : (i + 1) * ROWS]
            return acc + dot(jnp.concatenate(keys_t, axis=1), ds)

        acc = lax.fori_loop(0, CHUNKS, step, jnp.zeros((HEAD_DIM, 512), F32)) * SCALE
        for i in range(4):
            dq_ref[i, pl.ds(at, HEAD_DIM), :] = acc[:, i * ROWS : (i + 1) * ROWS].astype(BF16)


def mlp(
    ot_ref, x_ref, gain, wo_ref, wu_ref, wd_ref, loaded,
    out_ref, hidden_ref, gate_up_ref, normed_ref, product_ref,
):
    attended = turned_low(ot_ref[...].reshape(D, ROWS))
    loaded(0)
    hidden = x_ref[...].astype(F32) + dot(attended, wo_ref[...])
    hidden_ref[...] = hidden
    normalized, _ = norm_parts(hidden)
    normed = (normalized * gain).astype(BF16)
    normed_ref[...] = turned_low(normed)
    loaded(1)
    gate_up = dot(normed, wu_ref[...])
    gate_up_ref[...] = gate_up
    gate = gate_up[:, :FF]
    phi = 0.5 * (1.0 + lax.erf(gate * 0.5**0.5))
    product = (gate * phi * gate_up[:, FF:]).astype(BF16)
    product_ref[...] = turned_low(product)
    loaded(2)
    out_ref[...] = (hidden + dot(product, wd_ref[...])).astype(BF16)


def mlp_back(
    grad_ref, hidden_ref, gate_up_ref, gain, wo_ref, wu_ref, wd_ref, loaded,
    dot_ref, grad_hidden_ref, gg_ref, branch_ref, d_gain_ref,
):
    grad = grad_ref[...]
    loaded(2)
    grad_product = dot_nt(grad, wd_ref[...])
    gate = gate_up_ref[:, :FF]
    up = gate_up_ref[:, FF:]
    phi = 0.5 * (1.0 + lax.erf(gate * 0.5**0.5))
    density = jnp.exp(-0.5 * gate * gate) * 0.3989422804014327
    grad_gate = (grad_product * up * (phi + gate * density)).astype(BF16)
    grad_up = (grad_product * gate * phi).astype(BF16)
    gg_ref[:, :FF] = grad_gate
    gg_ref[:, FF:] = grad_up
    loaded(1)
    grad_normed = dot_nt(grad_gate, wu_ref[:, :FF]) + dot_nt(grad_up, wu_ref[:, FF:])
    normalized, rstd = norm_parts(hidden_ref[...])
    part, d_gain = norm_back(grad_normed, normalized, rstd, gain)
    d_gain_ref[...] = d_gain
    grad_hidden = grad.astype(F32) + part
    grad_hidden_ref[...] = grad_hidden
    branch = grad_hidden.astype(BF16)
    branch_ref[...] = branch
    loaded(0)
    turned = dot_nt(branch, wo_ref[...]).T.astype(BF16)
    for group in range(GROUPS):
        dot_ref[group] = turned[group * GW : (group + 1) * GW]


def qkv_back(
    dq_ref, dkv_ref, x_ref, gain, cos_ref, sin_ref, grad_hidden_ref, gain_two_ref, w_ref, loaded,
    grad_x_refs, gp_out_ref, gains_ref, gp_ref,
):
    cos = cos_ref[...]
    sin = sin_ref[...]

    def back(one, two):
        return one * cos + two * sin, two * cos - one * sin

    for head in range(HEADS):
        group, inner = head // GH, head % GH
        at = inner * HEAD_DIM
        one = dq_ref[group, at : at + 32, :].astype(F32)
        two = dq_ref[group, at + 32 : at + 64, :].astype(F32)
        gq = back(one, two)
        rows = slice(inner * ROWS, (inner + 1) * ROWS)
        kv = (dkv_ref[2 * group, rows, :].astype(F32) + dkv_ref[2 * group + 1, rows, :].astype(F32)).T
        gk = back(kv[:32], kv[32:64])
        base = head * HEAD_DIM
        gp_ref[base : base + 32, :] = gq[0]
        gp_ref[base + 32 : base + 64, :] = gq[1]
        gp_ref[D + base : D + base + 32, :] = gk[0]
        gp_ref[D + base + 32 : D + base + 64, :] = gk[1]
        gp_ref[2 * D + base : 2 * D + base + 64, :] = kv[64:]
    loaded()
    grad_normed = jnp.zeros((ROWS, D), F32)
    for block in range(9):
        cols = slice(block * 256, (block + 1) * 256)
        gp = gp_ref[cols, :].T.astype(BF16)
        gp_out_ref[:, cols] = gp
        grad_normed = grad_normed + dot_nt(gp, w_ref[:, cols])
    normalized, rstd = norm_parts(x_ref[...].astype(F32))
    part, d_gain = norm_back(grad_normed, normalized, rstd, gain)
    gains_ref[...] = jnp.concatenate(
        [d_gain, gain_two_ref[...], jnp.zeros((14, D), F32)], axis=0
    ).astype(BF16)
    for ref in grad_x_refs:
        ref[...] = (grad_hidden_ref[...] + part).astype(BF16)


MLP_ROWS = 576
QKV_ROWS = 320
SUM_ROWS = MLP_ROWS + QKV_ROWS


def weight_product(out_ref, at, left, lefts, right, rights):
    section = lax.axis_index("section")
    core = lax.rem(lax.axis_index("ctx"), 2)
    (a_sib, a_far, a_both), (g_sib, g_far, g_both) = lefts, rights
    height = a_sib.shape[1]
    for block in range(g_sib.shape[1] // D):
        cols = slice(block * D, (block + 1) * D)
        g = [right[section, :, cols], g_sib[:, cols], g_far[:, cols], g_both[:, cols]]
        g = jnp.concatenate(g, axis=0)
        for shard in range(4):
            a = [left[section, shard, core], a_sib[shard], a_far[shard, core], a_both[shard]]
            row = at + block * height
            both = dot(jnp.concatenate(a, axis=1), g)
            out_ref[shard, row : row + height, :] = both.astype(BF16)


def assemble_kernel(mlp_ref, qkv_in_ref, up_ref, out_ref, down_ref, qkv_ref, gains_ref):
    for half in range(2):
        rows = slice(half * 96, half * 96 + 96)
        for block in range(3):
            cols = slice(block * D, (block + 1) * D)
            at = slice(block * 96, block * 96 + 96)
            up_ref[rows, cols] = mlp_ref[half, at, :].astype(F32)
            qkv_ref[rows, cols] = qkv_in_ref[half, at, :].astype(F32)
        out_ref[rows, :] = mlp_ref[half, 288:384, :].astype(F32)
        down_ref[half * 144 : half * 144 + 144, :] = mlp_ref[half, 384:528, :].astype(F32)
    gains_ref[...] = qkv_in_ref[0, 288:304, :].astype(F32) + qkv_in_ref[1, 288:304, :].astype(F32)


def here():
    return lax.axis_index("section"), lax.axis_index("ctx"), lax.axis_index("wshard")


def flip(index, delta):
    for bit in (1, 2, 4, 8):
        if delta & bit:
            index = index + bit - 2 * bit * lax.rem(index // bit, 2)
    return index


def greet(peers):
    barrier = pltpu.get_barrier_semaphore()
    for peer in peers:
        pl.semaphore_signal(barrier, inc=1, device_id=peer, device_id_type=MESH)
    pl.semaphore_wait(barrier, len(peers))


def remote(src, dst, send, recv, peer):
    return pltpu.make_async_remote_copy(
        src_ref=src, dst_ref=dst, send_sem=send, recv_sem=recv, device_id=peer, device_id_type=MESH
    )


class Lines:
    count = 192

    def __init__(self, send, recv):
        self.send, self.recv, self.used, self.waits = send, recv, 0, []

    def make(self, src, dst, peer):
        at = self.used
        self.used += 1
        assert at < self.count
        return remote(src, dst, self.send.at[at], self.recv.at[at], peer)

    def put(self, src, dst, peer):
        copy = self.make(src, dst, peer)
        copy.start()
        return copy

    def keep(self, src, dst):
        at = self.used
        self.used += 1
        assert at < self.count
        copy = pltpu.make_async_copy(src, dst, self.send.at[at])
        copy.start()
        return copy


ids = iter(range(1, 64))


def sibling_of(s, c, z):
    return (s, flip(c, 1), z)


def z_peers():
    s, c, z = here()
    return [(s, c, lax.rem(z + r, 4)) for r in (1, 3, 2)]


def beside_peers():
    s, c, z = here()
    return [(1 - s, c, z), (1 - s, flip(c, 8), z)]


class Gather:
    def __init__(self, lines, own, full):
        s, c, z = here()
        rows, cols = full.shape[2] // 2, full.shape[3] // 2
        self.rows = pl.ds(pl.multiple_of(lax.rem(c, 2) * rows, 16), rows)
        self.cols = [
            pl.ds(pl.multiple_of(side * cols, 128), cols) for side in (c // 8, 1 - c // 8)
        ]
        self.halves = [pl.ds(0, cols), pl.ds(cols, cols)]
        self.lines, self.full = lines, full
        self.sibling = sibling_of(s, c, z)
        after, before, _ = z_peers()
        self.step = []
        for cut, order in ((0, (after, before)), (1, (after, before))):
            where = full.at[s, z, self.rows, self.halves[cut]]
            piece = own.at[self.rows, self.halves[cut]]
            self.step.append([lines.put(piece, where, peer) for peer in order])
        self.peers = (after, before)
        self.aside = [self.beside(own.at[self.rows, self.cols[0]], z)]
        whole = full.at[s, z, self.rows]
        self.passed = [lines.put(own.at[self.rows], whole, self.sibling)]
        self.kept = lines.keep(own.at[self.rows], whole)
        self.sent = []

    def beside(self, src, z):
        s, _, _ = here()
        where = self.full.at[s, z, self.rows, self.cols[0]]
        return [self.lines.put(src, where, peer) for peer in beside_peers()]

    def from_neighbours(self):
        s, _, z = here()
        self.sources = [lax.rem(z + 3, 4), lax.rem(z + 1, 4)]
        self.second = []
        for side in (0, 1):
            self.step[side][side].wait_recv()
            block = self.full.at[s, self.sources[side], self.rows, self.halves[side]]
            self.second.append(self.lines.put(block, block, self.peers[side]))
        for side in (0, 1):
            self.step[1 - side][side].wait_recv()
            self.onward(self.sources[side])

    def onward(self, z):
        s, _, _ = here()
        block = self.full.at[s, z, self.rows]
        self.passed.append(self.lines.put(block, block, self.sibling))
        self.aside.append(self.beside(block.at[:, self.cols[0]], z))

    def from_opposite(self):
        _, _, z = here()
        for copy in self.second:
            copy.wait_recv()
        self.onward(lax.rem(z + 2, 4))

    def from_beside(self):
        s, _, z = here()
        for copies, source in zip(self.aside, (z, *self.sources, lax.rem(z + 2, 4))):
            for i, copy in enumerate(copies):
                copy.wait_recv()
                block = self.full.at[1 - s, source, self.rows, self.cols[i]]
                self.passed.append(self.lines.put(block, block, self.sibling))

    def finish(self):
        self.kept.wait()
        for copies in (*self.step, *self.aside, self.second):
            for copy in copies:
                copy.wait_send()
        for copy in self.passed:
            copy.wait()


def run_gathers(gathers):
    for gather in gathers:
        gather.from_neighbours()
    for gather in gathers:
        gather.from_opposite()
    for gather in gathers:
        gather.from_beside()
    for gather in gathers:
        gather.finish()


def full_shapes(weights):
    return [sds((2, 4, *w.shape), BF16) for w in weights]


def gather_peers():
    return [sibling_of(*here()), *z_peers()[:2], *beside_peers()]


def shard_loads(full, layer, dst, sems):
    rows = full.shape[2]
    return [
        pltpu.make_async_copy(full.at[layer, i], dst.at[pl.ds(i * rows, rows)], sems.at[i])
        for i in range(4)
    ]


class Spread:
    order = [14, 10, 12, 8, 6, 4, 2]

    def __init__(self, lines, qkv_ref, q_ref, kv_ref):
        s, c, z = here()
        self.lines, self.kv_ref = lines, kv_ref
        self.sibling = sibling_of(s, c, z)
        kv_rows = pl.ds(GW, 2 * GW)
        q_rows = pl.ds(0, GW)
        self.kv_sends, self.q_sends = {}, []
        for delta in self.order:
            peer = (s, flip(c, delta), z)
            self.kv_sends[delta] = lines.put(qkv_ref.at[peer[1] // 4, kv_rows], kv_ref.at[c], peer)
            if delta % 4 == 0:
                self.q_sends.append(lines.put(qkv_ref.at[peer[1] // 4, q_rows], q_ref.at[c // 4], peer))
        self.passed = [lines.put(qkv_ref.at[c // 4, kv_rows], kv_ref.at[c], self.sibling)]
        self.kept = [
            lines.keep(qkv_ref.at[c // 4, kv_rows], kv_ref.at[c]),
            lines.keep(qkv_ref.at[c // 4, q_rows], q_ref.at[c // 4]),
        ]

    def finish(self):
        _, c, _ = here()
        for delta in reversed(self.order):
            self.kv_sends[delta].wait_recv()
            block = self.kv_ref.at[flip(c, delta)]
            self.passed.append(self.lines.put(block, block, self.sibling))
        for copy in self.kept + self.q_sends + self.passed:
            copy.wait()
        for copy in self.kv_sends.values():
            copy.wait_send()


class Turn:
    def __init__(self, lines, x_ref, o_ref):
        s, c, z = here()
        peers = [(s, flip(c, delta), z) for delta in (4, 8, 12)]
        self.copies = [lines.put(x_ref.at[peer[1] // 4], o_ref.at[c // 4], peer) for peer in peers]
        self.copies.append(lines.keep(x_ref.at[c // 4], o_ref.at[c // 4]))

    def finish(self):
        for copy in self.copies:
            copy.wait()


def forward_kernel(*refs):
    (cos, sin, inputs, gain), own, per_layer, full, (gains,), scratch = split_refs(refs, 4, 4, 11, 4, 1, 14)
    x_s, w_q, w_o, w_u, w_d, qkv_s, low_s, s_ref, got_gain, load_sem, in_sem, send, recv, gain_s = scratch
    s, c, z = here()
    lines = Lines(send, recv)
    x_load = fetch(inputs.at[s, 0], x_s, in_sem.at[0])
    across = [(1 - s, c, lax.rem(z + r, 4)) for r in (1, 3, 2)]
    ctx_peers = [(s, flip(c, delta), z) for delta in range(2, CTX, 2)]
    greet([*gather_peers(), z_peers()[2], *across, *ctx_peers])

    first = Gather(lines, own[0], full[0])
    gain_copies = [
        lines.put(gain, got_gain.at[s, z], peer) for peer in (*z_peers(), beside_peers()[0], *across)
    ]
    gain_copies.append(lines.keep(gain, got_gain.at[s, z]))
    run_gathers([first])
    rest = [Gather(lines, own[i], full[i]) for i in (2, 1, 3)]

    targets = (w_q, w_o, w_u, w_d)
    loads = [
        [shard_loads(full[i], layer, targets[i], load_sem.at[layer, i]) for i in range(4)]
        for layer in range(2)
    ]

    def begin(layer, which):
        for i in which:
            for copy in loads[layer][i]:
                copy.start()

    def loaded(layer, i):
        for copy in loads[layer][i]:
            copy.wait()

    begin(0, [0])
    for copy in gain_copies:
        copy.wait()
    for layer in range(2):
        total = got_gain[layer, 0].astype(F32) + got_gain[layer, 1].astype(F32)
        gain_s[layer] = total + got_gain[layer, 2].astype(F32) + got_gain[layer, 3].astype(F32)
    gains[...] = gain_s[...]
    x_load.wait()
    source = x_s
    for layer in range(2):
        q, kv, wide, totals, ot, out, hidden, gate_up, normed_two, product, normed = [
            ref.at[layer] for ref in per_layer
        ]
        project(
            source, gain_s[layer, 0:1, :], cos, sin, w_q, lambda: loaded(layer, 0), qkv_s.at[layer], normed
        )
        if layer == 0:
            begin(1, [0])
        spread = Spread(lines, qkv_s.at[layer], q, kv)
        spread.finish()
        if layer == 0:
            for gather in rest:
                gather.from_neighbours()
        attend(q, kv, low_s.at[layer], wide, totals, s_ref)
        if layer == 0:
            for gather in rest:
                gather.from_opposite()
        turn = Turn(lines, low_s.at[layer], ot)
        turn.finish()
        if layer == 0:
            for gather in rest:
                gather.from_beside()
            for gather in rest:
                gather.finish()
            begin(0, [1, 2, 3])
        mlp(
            ot, source, gain_s[layer, 1:2, :], w_o, w_u, w_d, lambda i: loaded(layer, i + 1),
            out, hidden, gate_up, normed_two, product,
        )
        if layer == 0:
            begin(1, [1, 2, 3])
        source = out


LAYER_SHAPES = (
    sds((4, GW, ROWS), BF16),
    sds((CTX, 2 * GW, ROWS), BF16),
    sds((4, GW, ROWS), F32),
    sds((GH, 8, 512), F32),
    sds((4, GW, ROWS), BF16),
    sds((ROWS, D), BF16),
    sds((ROWS, D), F32),
    sds((ROWS, 2 * FF), F32),
    sds((D, ROWS), BF16),
    sds((FF, ROWS), BF16),
    sds((D, ROWS), BF16),
)


def forward(inputs, gain, weights, tables):
    per_layer = [sds((2, *a.shape), a.dtype) for a in LAYER_SHAPES]
    full = full_shapes(weights)
    scratch = [
        pltpu.VMEM((ROWS, D), BF16),
        *[pltpu.VMEM((4 * w.shape[0], w.shape[1]), BF16) for w in weights],
        pltpu.VMEM((2, 4, 3 * GW, ROWS), BF16),
        pltpu.VMEM((2, 4, GW, ROWS), BF16),
        pltpu.VMEM((2048, 512), F32),
        pltpu.VMEM((2, 4, 16, D), BF16),
        DMA((2, 4, 4)),
        DMA((1,)),
        DMA((Lines.count,)),
        DMA((Lines.count,)),
        pltpu.VMEM((2, 16, D), F32),
    ]
    res = pl.pallas_call(
        forward_kernel,
        out_shape=[*per_layer, *full, sds((2, 16, D), F32)],
        in_specs=[VM, VM, ANY, ANY] + [ANY] * 4,
        out_specs=[VM] * 11 + [ANY] * 4 + [VM],
        scratch_shapes=scratch,
        compiler_params=pltpu.CompilerParams(
            collective_id=next(ids), has_side_effects=True, vmem_limit_bytes=VMEM_LIMIT
        ),
        name="forward",
    )(*tables, inputs, gain, *weights)
    return res[:11], res[11:15], res[15]


class Meet:
    def __init__(self, lines, layers, sib, far, both):
        s, c, z = here()
        self.core = core = lax.rem(c, 2)
        self.lines, self.far, self.both = lines, far, both
        self.sibling = sibling_of(s, c, z)
        peer = (1 - s, flip(c, 8) * core + c * (1 - core), z)
        self.apart = lines.put(layers.at[1 - s], far, peer)
        if sib is not None:
            self.close = lines.put(self.half(layers.at[s]), sib, self.sibling)

    def half(self, ref):
        return ref.at[:, 1 - self.core] if len(ref.shape) == 4 else ref

    def forward(self):
        self.apart.wait_recv()
        if self.both is not None:
            self.passed = self.lines.put(self.half(self.far), self.both, self.sibling)

    def finish(self):
        self.apart.wait_send()
        if self.both is not None:
            self.close.wait()
            self.passed.wait()


def meet_buffers(shape):
    half = (shape[0], *shape[2:]) if len(shape) == 4 else shape
    return [pltpu.VMEM(each, BF16) for each in (half, shape, half)]


class Show:
    def __init__(self, lines, layers, out):
        s, c, z = here()
        self.copy = lines.put(layers.at[1 - s], out.at[s], (1 - s, c, z))
        self.kept = lines.keep(layers.at[s], out.at[s])

    def finish(self):
        self.copy.wait()
        self.kept.wait()


class GiveBack:
    order = [14, 10, 12, 8, 6, 4, 2, 0]

    def __init__(self, lines, dq_ref, dkv_ref, dqo_ref, theirs):
        s, c, z = here()
        self.lines, self.dkv, self.theirs = lines, dkv_ref, theirs
        sibling = sibling_of(s, c, z)
        self.passed = {
            delta: lines.put(dkv_ref.at[flip(flip(c, 1), delta)], theirs.at[delta // 2], sibling)
            for delta in self.order
        }
        self.turn = Turn(lines, dq_ref, dqo_ref)

    def finish(self, total, sums):
        s, c, z = here()
        sends = []
        for delta in self.order:
            self.passed[delta].wait_recv()
            at = delta // 2
            both = self.dkv[flip(c, delta)].astype(F32) + self.theirs[at].astype(F32)
            total[at] = both.astype(BF16)
            if delta:
                peer = (s, flip(c, delta), z)
                sends.append(self.lines.put(total.at[at], sums.at[c // 2], peer))
            else:
                sends.append(self.lines.keep(total.at[at], sums.at[c // 2]))
        for copy in self.passed.values():
            copy.wait_send()
        for copy in sends:
            copy.wait()
        self.turn.finish()


class Reduce:
    order = [14, 10, 12, 8, 6, 4, 2]

    def __init__(self, lines, comb, got, own_sum, parts, red, fin):
        self.lines, self.comb, self.got, self.own_sum = lines, comb, got, own_sum
        self.parts, self.red, self.fin = parts, red, fin
        self.quarter = comb.shape[1] // 4
        s, c, z = here()
        self.peers = {delta: (s, flip(c, delta), z) for delta in self.order}
        self.sibling = sibling_of(s, c, z)

    def block(self, at):
        rows = pl.ds(pl.multiple_of(lax.rem(at // 2, 4) * self.quarter, 16), self.quarter)
        return rows, pl.ds(pl.multiple_of(at // 8 * (D // 2), 128), D // 2)

    def along(self):
        self.scatter = [
            self.lines.put(self.comb.at[peer[2]], self.got.at[i], peer) for i, peer in enumerate(z_peers())
        ]

    def plane(self):
        _, c, z = here()
        for copy in self.scatter:
            copy.wait()
        for at in range(0, self.comb.shape[1], 64):
            rows = slice(at, at + 64)
            both = self.comb[z, rows].astype(F32) + self.got[0, rows].astype(F32)
            both += self.got[1, rows].astype(F32) + self.got[2, rows].astype(F32)
            self.own_sum[rows] = both.astype(BF16)
        self.sends = [
            self.lines.put(self.own_sum.at[self.block(peer[1])], self.parts.at[c // 2], peer)
            for peer in self.peers.values()
        ]
        self.sends.append(self.lines.keep(self.own_sum.at[self.block(c)], self.parts.at[c // 2]))

    def spread(self):
        _, c, _ = here()
        for copy in self.sends:
            copy.wait()
        for at in range(0, self.quarter, 16):
            rows = slice(at, at + 16)
            total = self.parts[0, rows].astype(F32)
            for i in range(1, 8):
                total += self.parts[i, rows].astype(F32)
            self.red[rows] = total.astype(BF16)
        self.target = self.fin.at[lax.rem(c, 2)]
        place = self.target.at[self.block(c)]
        self.shown = {delta: self.lines.put(self.red, place, peer) for delta, peer in self.peers.items()}
        self.kept = self.lines.keep(self.red, place)
        self.passed = [self.lines.put(self.red, place, self.sibling)]

    def forward(self):
        _, c, _ = here()
        for delta in reversed(self.order):
            self.shown[delta].wait_recv()
            piece = self.target.at[self.block(flip(c, delta))]
            self.passed.append(self.lines.put(piece, piece, self.sibling))

    def finish(self):
        self.kept.wait()
        for copy in self.shown.values():
            copy.wait_send()
        for copy in self.passed:
            copy.wait()


def reduce_buffers(rows):
    return [
        pltpu.VMEM((4, rows, D), BF16),
        pltpu.VMEM((3, rows, D), BF16),
        pltpu.VMEM((rows, D), BF16),
        pltpu.VMEM((8, rows // 4, D // 2), BF16),
        pltpu.VMEM((rows // 4, D // 2), BF16),
    ]


LEFT_SHAPES = ((4, 2, 96, ROWS), (4, 2, 144, ROWS), (4, 2, 96, ROWS), (4, 2, 96, ROWS))
RIGHT_SHAPES = ((ROWS, 2 * FF), (ROWS, D), (ROWS, D))
HELD_SHAPES = (
    ((2, 4, GW, ROWS), BF16),
    ((2, CTX, 2 * GW, ROWS), BF16),
    ((2, 4, GW, ROWS), F32),
    ((2, GH, 8, 512), F32),
    ((2, ROWS, D), F32),
    ((2, ROWS, 2 * FF), F32),
    ((2, ROWS, D), BF16),
)


def backward_kernel(*refs):
    (
        (cos, sin, gains, cotangent, inputs, outs), full, far_held, lefts,
        (activations, input_grads, fin_m, fin_q), weights, held, left_meets, right_meets, gp_meets,
        reduce_m, reduce_q, scratch,
    ) = split_refs(refs, 6, 4, 6, 4, 4, 4, 7, 12, 9, 3, 5, 5, 21)
    (
        d_ot, d_o, gg, branch, grads, gp, starts, gain_sums, gains_far, grad_hidden, d_gain, gp_f32,
        dq, dkv, dqo, theirs, total, sums, load_sem, held_sem, lines_sem,
    ) = scratch
    s, c, z = here()
    lines = Lines(lines_sem.at[0], lines_sem.at[1])
    w_q, w_o, w_u, w_d = weights
    loads = [
        [
            shard_loads(full[i], layer, weights[i], load_sem.at[layer, i]) for i in range(4)
        ]
        for layer in range(2)
    ]

    def begin(layer, which):
        for i in which:
            for copy in loads[layer][i]:
                copy.start()

    def loaded(layer, i):
        for copy in loads[layer][i]:
            copy.wait()

    cot_load = fetch(cotangent.at[s, 0], grads.at[1], held_sem.at[2, 0])
    q, kv, wide, totals, hidden, gate_up, x = held
    hold = {}
    for layer in (1, 0):
        for i in (5, 4, 0, 1, 2, 3):
            hold[layer, i] = fetch(far_held[i].at[layer], held[i].at[layer], held_sem.at[layer, i])
        begin(1, [3, 2, 1, 0] if layer == 1 else [])
    x_loads = [fetch(inputs.at[s, 0], x.at[0], held_sem.at[0, 6]), fetch(outs.at[0], x.at[1], held_sem.at[1, 6])]
    greet(
        [sibling_of(s, c, z), *z_peers(), *beside_peers()]
        + [(s, flip(c, delta), z) for delta in range(2, CTX, 2)]
    )
    meets = [Meet(lines, left, *left_meets[3 * i : 3 * i + 3]) for i, left in enumerate(lefts)]
    shown = [Show(lines, outs, activations)]
    cot_load.wait()

    def run_mlp_back(layer):
        hold[layer, 5].wait()
        hold[layer, 4].wait()
        mlp_back(
            grads.at[layer], hidden.at[layer], gate_up.at[layer], gains[layer, 1:2, :], w_o, w_u, w_d,
            lambda i: loaded(layer, i + 1),
            d_ot.at[layer], grad_hidden, gg.at[layer], branch.at[layer], d_gain,
        )

    def run_attend_back(layer, start, stop):
        if start == 0:
            for i in range(4):
                hold[layer, i].wait()
        attend_back(
            start, stop, q.at[layer], kv.at[layer], wide.at[layer], totals.at[layer], d_o.at[layer], dq, dkv
        )

    def run_give_back(layer):
        work = GiveBack(lines, dq, dkv, dqo.at[layer], theirs.at[layer])
        work.finish(total, sums.at[layer])

    def run_qkv_back(layer):
        x_loads[layer].wait()
        qkv_back(
            dqo.at[layer], sums.at[layer], x.at[layer], gains[layer, 0:1, :], cos, sin, grad_hidden, d_gain,
            w_q, lambda: loaded(layer, 0),
            [starts.at[1], grads.at[0]] if layer else [starts.at[0]],
            gp.at[layer], gain_sums.at[layer], gp_f32,
        )

    run_mlp_back(1)
    begin(0, [3, 2, 1])
    turn = Turn(lines, d_ot.at[1], d_o.at[1])
    for work in meets:
        work.forward()
    turn.finish()
    run_attend_back(1, 0, GH)
    for work in meets + shown:
        work.finish()
    run_give_back(1)
    run_qkv_back(1)
    begin(0, [0])
    run_mlp_back(0)
    turn = Turn(lines, d_ot.at[0], d_o.at[0])
    rights = (gg, grads, branch)
    meets = [Meet(lines, right, *right_meets[3 * i : 3 * i + 3]) for i, right in enumerate(rights)]
    turn.finish()
    run_attend_back(0, 0, 1)
    for work in meets:
        work.forward()
    run_attend_back(0, 1, 2)
    for work in meets:
        work.finish()
    part_m = Reduce(lines, *reduce_m, fin_m)
    part_q = Reduce(lines, *reduce_q, fin_q)
    comb_m, comb_q = reduce_m[0], reduce_q[0]
    for i, at in ((0, 0), (2, 288), (1, 384)):
        weight_product(
            comb_m, at, lefts[i], left_meets[3 * i : 3 * i + 3],
            (gg, grads, branch)[i], right_meets[3 * i : 3 * i + 3],
        )
    comb_m[:, 528:, :] = jnp.zeros((4, 48, D), BF16)
    part_m.along()
    run_attend_back(0, 2, GH)
    run_give_back(0)
    run_qkv_back(0)
    meets = [
        Meet(lines, gp, *gp_meets),
        Meet(lines, gain_sums, None, gains_far, None),
    ]
    shown = [Show(lines, starts, input_grads)]
    for work in meets:
        work.forward()
    for work in meets:
        work.finish()
    weight_product(comb_q, 0, lefts[3], left_meets[9:], gp, gp_meets)
    gain_rows = (gain_sums[s].astype(F32) + gains_far[...].astype(F32)).astype(BF16)
    for shard in range(4):
        comb_q[shard, 288:304, :] = gain_rows
        comb_q[shard, 304:, :] = jnp.zeros((16, D), BF16)
    part_q.along()
    part_m.plane()
    part_q.plane()
    part_m.spread()
    part_q.spread()
    part_m.forward()
    part_q.forward()
    for work in [part_m, part_q, *shown]:
        work.finish()


def backward(tables, gains, cotangent, inputs, full, stored):
    q, kv, wide, totals, ot, outs, hidden, gate_up, normed_two, product, normed = stored
    lefts = [
        a.reshape(2, *shape) for a, shape in zip((normed_two, product, ot, normed), LEFT_SHAPES)
    ]
    scratch = [
        *[pltpu.VMEM((4 * w.shape[2], w.shape[3]), BF16) for w in full],
        *[pltpu.VMEM(*held) for held in HELD_SHAPES],
        *[buffer for shape in LEFT_SHAPES for buffer in meet_buffers(shape)],
        *[buffer for shape in RIGHT_SHAPES for buffer in meet_buffers(shape)],
        *meet_buffers((ROWS, 3 * D)),
        *reduce_buffers(MLP_ROWS),
        *reduce_buffers(QKV_ROWS),
        pltpu.VMEM((2, 4, GW, ROWS), BF16),
        pltpu.VMEM((2, 4, GW, ROWS), BF16),
        pltpu.VMEM((2, ROWS, 2 * FF), BF16),
        pltpu.VMEM((2, ROWS, D), BF16),
        pltpu.VMEM((2, ROWS, D), BF16),
        pltpu.VMEM((2, ROWS, 3 * D), BF16),
        pltpu.VMEM((2, ROWS, D), BF16),
        pltpu.VMEM((2, 16, D), BF16),
        pltpu.VMEM((16, D), BF16),
        pltpu.VMEM((ROWS, D), F32),
        pltpu.VMEM((1, D), F32),
        pltpu.VMEM((3 * D, ROWS), F32),
        pltpu.VMEM((4, GW, ROWS), BF16),
        pltpu.VMEM((CTX, 2 * GW, ROWS), BF16),
        pltpu.VMEM((2, 4, GW, ROWS), BF16),
        pltpu.VMEM((2, 8, 2 * GW, ROWS), BF16),
        pltpu.VMEM((8, 2 * GW, ROWS), BF16),
        pltpu.VMEM((2, 8, 2 * GW, ROWS), BF16),
        DMA((2, 4, 4)),
        DMA((3, 7)),
        DMA((2, Lines.count)),
    ]
    return pl.pallas_call(
        backward_kernel,
        out_shape=[
            sds((2, ROWS, D), BF16), sds((2, ROWS, D), BF16),
            sds((2, MLP_ROWS, D), BF16), sds((2, QKV_ROWS, D), BF16),
        ],
        in_specs=[VM] * 3 + [ANY] * 3 + [ANY] * 4 + [ANY] * 6 + [VM] * 4,
        out_specs=[ANY, ANY, VM, VM],
        scratch_shapes=scratch,
        compiler_params=pltpu.CompilerParams(
            collective_id=next(ids), has_side_effects=True, vmem_limit_bytes=VMEM_LIMIT
        ),
        name="backward",
    )(*tables, gains, cotangent, inputs, outs, *full, q, kv, wide, totals, hidden, gate_up, *lefts)


def rope_tables():
    positions = (lax.axis_index("ctx") * ROWS + lax.iota(jnp.int32, ROWS)).astype(F32)
    frequency = 1.0 / 160000.0 ** (jnp.arange(HEAD_DIM // 2, dtype=F32) * 2.0 / HEAD_DIM)
    angles = frequency[:, None] * positions[None, :]
    return jnp.cos(angles), jnp.sin(angles)


def local(inputs, cotangent, attn_gain, qkv_weight, out_weight, mlp_gain, up_weight, down_weight):
    z = lax.axis_index("wshard")
    gain = jnp.concatenate([attn_gain, mlp_gain], axis=0)
    lanes = lax.broadcasted_iota(jnp.int32, (2, 4, 192), 1) == z
    gain = jnp.where(lanes, gain[:, None, :], jnp.zeros((), BF16)).reshape(2, D)
    gain = jnp.pad(gain, ((0, 14), (0, 0)))
    tables = rope_tables()
    stored, full, gains = forward(
        inputs, gain, [w[0] for w in (qkv_weight, out_weight, up_weight, down_weight)], tables
    )
    activations, input_grads, fin_m, fin_q = backward(tables, gains, cotangent, inputs, full, stored)
    grad_up, grad_out, grad_down, grad_qkv, gain_sums = compute_call(
        assemble_kernel,
        (fin_m, fin_q),
        [sds(shape, F32) for shape in ((192, 3 * D), (192, D), (288, D), (192, 3 * D), (16, D))],
        name="assemble",
    )
    gain_sums = lax.dynamic_slice_in_dim(gain_sums[:2], z * 192, 192, 1)
    return (
        activations[None, :, None],
        input_grads[None, :, None],
        gain_sums[0:1],
        grad_qkv[None],
        grad_out[None],
        gain_sums[1:2],
        grad_up[None],
        grad_down[None],
    )


def solution(mesh):
    global ids
    ids = iter(range(1, 64))
    placed = (
        P(None, "wshard", "ctx", None),
        P(None, "wshard", "ctx", None),
        P("section", "wshard"),
        P("section", "wshard", None),
        P("section", "wshard", None),
        P("section", "wshard"),
        P("section", "wshard", None),
        P("section", "wshard", None),
    )
    return jax.shard_map(
        local,
        mesh=mesh,
        in_specs=placed,
        out_specs=(
            P("section", None, "wshard", "ctx", None),
            P("section", None, "wshard", "ctx", None),
            P("section", "wshard"),
            P("section", "wshard", None),
            P("section", "wshard", None),
            P("section", "wshard"),
            P("section", "wshard", None),
            P("section", "wshard", None),
        ),
        check_vma=False,
    )
```

```python
import functools

import jax
import jax.numpy as jnp
from jax import lax
from jax.experimental import pallas as pl
from jax.experimental.pallas import tpu as pltpu
from jax.sharding import PartitionSpec as P

D = 768
HEADS = 12
HEAD_DIM = 64
FF = 1152
ROWS = 128
GROUPS = 4
GH = HEADS // GROUPS
GW = GH * HEAD_DIM
CTX = 16
SCALE = HEAD_DIM ** (-0.5)
F32 = jnp.float32
BF16 = jnp.bfloat16
MESH = pl.DeviceIdType.MESH
DMA = pltpu.SemaphoreType.DMA
ANY = pl.BlockSpec(memory_space=pl.ANY)
VM = pl.BlockSpec(memory_space=pltpu.VMEM)
VMEM_LIMIT = 60 * 1024 * 1024


def dot(a, b):
    return jnp.dot(a, b, preferred_element_type=F32)


def dot_nt(a, b):
    return lax.dot_general(a, b, (((1,), (1,)), ((), ())), preferred_element_type=F32)


def sds(shape, dtype):
    return jax.ShapeDtypeStruct(shape, dtype)


def compute_call(kernel, args, outs, name):
    return pl.pallas_call(
        kernel,
        out_shape=outs,
        in_specs=[VM] * len(args),
        out_specs=jax.tree.map(lambda _: VM, outs),
        compiler_params=pltpu.CompilerParams(vmem_limit_bytes=VMEM_LIMIT),
        name=name,
    )(*args)


def fetch(src, dst, sem):
    copy = pltpu.make_async_copy(src, dst, sem)
    copy.start()
    return copy


def turned_low(x):
    return x.astype(F32).T.astype(BF16)


def norm_parts(source):
    centered = source - jnp.mean(source, axis=-1, keepdims=True)
    variance = jnp.mean(centered * centered, axis=-1, keepdims=True)
    rstd = lax.rsqrt(variance + 1e-05)
    return centered * rstd, rstd


def norm_back(grad, normalized, rstd, gain):
    inner = grad * gain
    mean_one = jnp.mean(inner, axis=-1, keepdims=True)
    mean_two = jnp.mean(inner * normalized, axis=-1, keepdims=True)
    grad_gain = jnp.sum(grad * normalized, axis=0, keepdims=True)
    return rstd * (inner - mean_one - normalized * mean_two), grad_gain


def split_refs(refs, *counts):
    refs = list(refs)
    out = []
    for count in counts:
        out.append(refs[:count])
        refs = refs[count:]
    return out


def project(x_ref, gain, cos_ref, sin_ref, w_ref, loaded, qkv_ref, normed_ref):
    normalized, _ = norm_parts(x_ref[...].astype(F32))
    normed = (normalized * gain).astype(BF16)
    normed_ref[...] = turned_low(normed)
    loaded()
    cos = cos_ref[...]
    sin = sin_ref[...]
    for part in range(3):
        for block in range(3):
            at = part * D + block * 256
            turned = dot(normed, w_ref[:, at : at + 256]).T
            for head_at in range(4):
                head = block * 4 + head_at
                one = turned[head_at * 64 : head_at * 64 + 32]
                two = turned[head_at * 64 + 32 : head_at * 64 + 64]
                if part < 2:
                    one, two = one * cos - two * sin, two * cos + one * sin
                if part == 0:
                    one, two = one * SCALE, two * SCALE
                inner = head % GH
                row = inner * HEAD_DIM if part == 0 else GW + (2 * inner + part - 1) * HEAD_DIM
                qkv_ref[head // GH, row : row + 32, :] = one.astype(BF16)
                qkv_ref[head // GH, row + 32 : row + 64, :] = two.astype(BF16)


CHUNK = 256
CHUNKS = 2048 // CHUNK
PAIR = CHUNK // ROWS


def attend(start, stop, q_ref, kv_ref, low_ref, wide_ref, totals_ref, s_ref):
    @pl.loop(start, stop)
    def _(h):
        at = pl.multiple_of(h * HEAD_DIM, HEAD_DIM)
        key_at = pl.multiple_of(h * ROWS, ROWS)
        value_at = pl.multiple_of(h * ROWS + HEAD_DIM, HEAD_DIM)
        qt = jnp.concatenate([q_ref[i, pl.ds(at, HEAD_DIM), :] for i in range(4)], axis=1)
        top = jnp.full((8, 512), -jnp.inf, F32)
        for c in range(CHUNKS):
            keys = jnp.concatenate(
                [kv_ref[c * PAIR + i, pl.ds(key_at, HEAD_DIM), :].T for i in range(PAIR)], axis=0
            )
            scores = dot(keys, qt)
            s_ref[c * CHUNK : (c + 1) * CHUNK, :] = scores
            top = jnp.maximum(top, jnp.max(scores.reshape(CHUNK // 8, 8, 512), axis=0))
        top = jnp.max(top, axis=0, keepdims=True)
        total = jnp.zeros((8, 512), F32)
        acc = jnp.zeros((HEAD_DIM, 512), F32)
        for c in range(CHUNKS):
            p = jnp.exp(s_ref[c * CHUNK : (c + 1) * CHUNK, :] - top)
            total = total + jnp.sum(p.reshape(CHUNK // 8, 8, 512), axis=0)
            values = jnp.concatenate(
                [kv_ref[c * PAIR + i, pl.ds(value_at, HEAD_DIM), :] for i in range(PAIR)], axis=1
            )
            acc = acc + dot(values, p.astype(BF16))
        total = jnp.sum(total, axis=0, keepdims=True)
        out = acc / total
        totals_ref[h] = jnp.broadcast_to(top + jnp.log(total), (8, 512))
        for i in range(4):
            piece = out[:, i * ROWS : (i + 1) * ROWS]
            wide_ref[i, pl.ds(at, HEAD_DIM), :] = piece
            low_ref[i, pl.ds(at, HEAD_DIM), :] = piece.astype(BF16)


def attend_back(start, stop, q_ref, kv_ref, wide_ref, totals_ref, do_ref, dq_ref, dkv_ref):
    @pl.loop(start, stop)
    def _(h):
        at = pl.multiple_of(h * HEAD_DIM, HEAD_DIM)
        key_at = pl.multiple_of(h * ROWS, ROWS)
        value_at = pl.multiple_of(h * ROWS + HEAD_DIM, HEAD_DIM)
        qt = jnp.concatenate([q_ref[i, pl.ds(at, HEAD_DIM), :] for i in range(4)], axis=1)
        dot_t = jnp.concatenate([do_ref[i, pl.ds(at, HEAD_DIM), :] for i in range(4)], axis=1)
        wide = jnp.concatenate([wide_ref[i, pl.ds(at, HEAD_DIM), :] for i in range(4)], axis=1)
        delta = jnp.sum(wide * dot_t.astype(F32), axis=0, keepdims=True)
        totals = totals_ref[h, 0:1, :]
        zero = jnp.zeros((512, HEAD_DIM), BF16)
        sides = jnp.concatenate(
            [
                jnp.concatenate([qt.T, zero], axis=1),
                jnp.concatenate([zero, dot_t.T], axis=1),
            ],
            axis=0,
        )

        def step(c, acc):
            keys_t = [kv_ref[c * PAIR + i, pl.ds(key_at, HEAD_DIM), :] for i in range(PAIR)]
            values_t = [kv_ref[c * PAIR + i, pl.ds(value_at, HEAD_DIM), :] for i in range(PAIR)]
            keys = jnp.concatenate([k.T for k in keys_t], axis=0)
            values = jnp.concatenate([v.T for v in values_t], axis=0)
            p = jnp.exp(dot(keys, qt) - totals)
            ds = (p * (dot(values, dot_t) - delta)).astype(BF16)
            both = jnp.concatenate([ds, p.astype(BF16)], axis=1)
            grads = dot(both, sides).astype(BF16)
            for i in range(PAIR):
                dkv_ref[c * PAIR + i, pl.ds(key_at, ROWS), :] = grads[i * ROWS : (i + 1) * ROWS]
            return acc + dot(jnp.concatenate(keys_t, axis=1), ds)

        acc = lax.fori_loop(0, CHUNKS, step, jnp.zeros((HEAD_DIM, 512), F32)) * SCALE
        for i in range(4):
            dq_ref[i, pl.ds(at, HEAD_DIM), :] = acc[:, i * ROWS : (i + 1) * ROWS].astype(BF16)


def mlp(
    ot_ref, x_ref, gain, wo_ref, wu_ref, wd_ref, loaded,
    out_ref, hidden_ref, gate_up_ref, normed_ref, product_ref,
):
    attended = turned_low(ot_ref[...].reshape(D, ROWS))
    loaded(0)
    hidden = x_ref[...].astype(F32) + dot(attended, wo_ref[...])
    hidden_ref[...] = hidden
    normalized, _ = norm_parts(hidden)
    normed = (normalized * gain).astype(BF16)
    normed_ref[...] = turned_low(normed)
    loaded(1)
    gate_up = dot(normed, wu_ref[...])
    gate_up_ref[...] = gate_up
    gate = gate_up[:, :FF]
    phi = 0.5 * (1.0 + lax.erf(gate * 0.5**0.5))
    product = (gate * phi * gate_up[:, FF:]).astype(BF16)
    product_ref[...] = turned_low(product)
    loaded(2)
    out_ref[...] = (hidden + dot(product, wd_ref[...])).astype(BF16)


def mlp_back(
    grad_ref, hidden_ref, gate_up_ref, gain, wo_ref, wu_ref, wd_ref, loaded,
    dot_ref, grad_hidden_ref, gg_ref, branch_ref, d_gain_ref,
):
    grad = grad_ref[...]
    loaded(2)
    grad_product = dot_nt(grad, wd_ref[...])
    gate = gate_up_ref[:, :FF]
    up = gate_up_ref[:, FF:]
    phi = 0.5 * (1.0 + lax.erf(gate * 0.5**0.5))
    density = jnp.exp(-0.5 * gate * gate) * 0.3989422804014327
    grad_gate = (grad_product * up * (phi + gate * density)).astype(BF16)
    grad_up = (grad_product * gate * phi).astype(BF16)
    gg_ref[:, :FF] = grad_gate
    gg_ref[:, FF:] = grad_up
    loaded(1)
    grad_normed = dot_nt(grad_gate, wu_ref[:, :FF]) + dot_nt(grad_up, wu_ref[:, FF:])
    normalized, rstd = norm_parts(hidden_ref[...])
    part, d_gain = norm_back(grad_normed, normalized, rstd, gain)
    d_gain_ref[...] = d_gain
    grad_hidden = grad.astype(F32) + part
    grad_hidden_ref[...] = grad_hidden
    branch = grad_hidden.astype(BF16)
    branch_ref[...] = branch
    loaded(0)
    turned = dot_nt(branch, wo_ref[...]).T.astype(BF16)
    for group in range(GROUPS):
        dot_ref[group] = turned[group * GW : (group + 1) * GW]


def qkv_back(
    dq_ref, dkv_ref, x_ref, gain, cos_ref, sin_ref, grad_hidden_ref, gain_two_ref, w_ref, loaded, ready,
    grad_x_refs, gp_out_ref, gains_ref, gp_ref,
):
    cos = cos_ref[...]
    sin = sin_ref[...]

    def back(one, two):
        return one * cos + two * sin, two * cos - one * sin

    for head in range(HEADS):
        group, inner = head // GH, head % GH
        at = inner * HEAD_DIM
        one = dq_ref[group, at : at + 32, :].astype(F32)
        two = dq_ref[group, at + 32 : at + 64, :].astype(F32)
        gq = back(one, two)
        rows = slice(inner * ROWS, (inner + 1) * ROWS)
        kv = (dkv_ref[2 * group, rows, :].astype(F32) + dkv_ref[2 * group + 1, rows, :].astype(F32)).T
        gk = back(kv[:32], kv[32:64])
        base = head * HEAD_DIM
        gp_ref[base : base + 32, :] = gq[0]
        gp_ref[base + 32 : base + 64, :] = gq[1]
        gp_ref[D + base : D + base + 32, :] = gk[0]
        gp_ref[D + base + 32 : D + base + 64, :] = gk[1]
        gp_ref[2 * D + base : 2 * D + base + 64, :] = kv[64:]
    for block in range(9):
        cols = slice(block * 256, (block + 1) * 256)
        gp_out_ref[:, cols] = gp_ref[cols, :].T.astype(BF16)
    result = ready()
    loaded()
    grad_normed = jnp.zeros((ROWS, D), F32)
    for block in range(9):
        cols = slice(block * 256, (block + 1) * 256)
        grad_normed = grad_normed + dot_nt(gp_out_ref[:, cols], w_ref[:, cols])
    normalized, rstd = norm_parts(x_ref[...].astype(F32))
    part, d_gain = norm_back(grad_normed, normalized, rstd, gain)
    gains_ref[...] = jnp.concatenate(
        [d_gain, gain_two_ref[...], jnp.zeros((14, D), F32)], axis=0
    ).astype(BF16)
    for ref in grad_x_refs:
        ref[...] = (grad_hidden_ref[...] + part).astype(BF16)
    return result


MLP_ROWS = 576
QKV_ROWS = 320
SUM_ROWS = MLP_ROWS + QKV_ROWS


def weight_product(out_ref, shard, at, left, lefts, right, rights):
    section = lax.axis_index("section")
    core = lax.rem(lax.axis_index("ctx"), 2)
    (a_sib, a_far, a_both), (g_sib, g_far, g_both) = lefts, rights
    height = a_sib.shape[1]
    a = [left[section, shard, core], a_sib[shard], a_far[shard, core], a_both[shard]]
    a = jnp.concatenate(a, axis=1)
    for block in range(g_sib.shape[1] // D):
        cols = slice(block * D, (block + 1) * D)
        g = [right[section, :, cols], g_sib[:, cols], g_far[:, cols], g_both[:, cols]]
        row = at + block * height
        out_ref[shard, row : row + height, :] = dot(a, jnp.concatenate(g, axis=0)).astype(BF16)


def assemble_kernel(
    mlp_ref, qkv_in_ref, act_ref, grad_ref, up_ref, out_ref, down_ref, qkv_ref, one_ref, two_ref, act_out, grad_out
):
    act_out[...] = act_ref[...]
    grad_out[...] = grad_ref[...]
    for half in range(2):
        rows = slice(half * 96, half * 96 + 96)
        for block in range(3):
            cols = slice(block * D, (block + 1) * D)
            at = slice(block * 96, block * 96 + 96)
            up_ref[rows, cols] = mlp_ref[half, at, :].astype(F32)
            qkv_ref[rows, cols] = qkv_in_ref[half, at, :].astype(F32)
        out_ref[rows, :] = mlp_ref[half, 288:384, :].astype(F32)
        down_ref[half * 144 : half * 144 + 144, :] = mlp_ref[half, 384:528, :].astype(F32)
    gains = qkv_in_ref[0, 288:304, :].astype(F32) + qkv_in_ref[1, 288:304, :].astype(F32)
    z = lax.axis_index("wshard")
    mine = gains[:, :192]
    for shard in range(1, 4):
        mine = jnp.where(z == shard, gains[:, shard * 192 : shard * 192 + 192], mine)
    one_ref[...] = mine[0:1]
    two_ref[...] = mine[1:2]


def here():
    return lax.axis_index("section"), lax.axis_index("ctx"), lax.axis_index("wshard")


def flip(index, delta):
    for bit in (1, 2, 4, 8):
        if delta & bit:
            index = index + bit - 2 * bit * lax.rem(index // bit, 2)
    return index


def greet(peers):
    barrier = pltpu.get_barrier_semaphore()
    for peer in peers:
        pl.semaphore_signal(barrier, inc=1, device_id=peer, device_id_type=MESH)
    pl.semaphore_wait(barrier, len(peers))


def remote(src, dst, send, recv, peer):
    return pltpu.make_async_remote_copy(
        src_ref=src, dst_ref=dst, send_sem=send, recv_sem=recv, device_id=peer, device_id_type=MESH
    )


class Lines:
    count = 288

    def __init__(self, send, recv):
        self.send, self.recv, self.used, self.places = send, recv, 0, {}

    def make(self, src, dst, peer):
        at = self.used
        self.used += 1
        assert at < self.count
        copy = remote(src, dst, self.send.at[at], self.recv.at[at], peer)
        self.places[id(copy)] = at
        return copy

    def put(self, src, dst, peer):
        copy = self.make(src, dst, peer)
        copy.start()
        return copy

    def again(self, made, src, dst, peer):
        at = self.places[id(made)]
        remote(src, dst, self.send.at[at], self.recv.at[at], peer).start()

    def keep(self, src, dst):
        at = self.used
        self.used += 1
        assert at < self.count
        copy = pltpu.make_async_copy(src, dst, self.send.at[at])
        copy.start()
        return copy


ids = iter(range(1, 64))


def sibling_of(s, c, z):
    return (s, flip(c, 1), z)


def z_peers():
    s, c, z = here()
    return [(s, c, lax.rem(z + r, 4)) for r in (1, 3, 2)]


def beside_peers():
    s, c, z = here()
    return [(1 - s, c, z), (1 - s, flip(c, 8), z)]


class Gather:
    def __init__(self, lines, own, full):
        s, c, z = here()
        rows, cols = full.shape[2] // 2, full.shape[3] // 2
        self.rows = pl.ds(pl.multiple_of(lax.rem(c, 2) * rows, 16), rows)
        self.halves = [pl.ds(0, cols), pl.ds(cols, cols)]
        self.lines, self.own, self.full = lines, own, full
        self.sibling = sibling_of(s, c, z)
        self.peers = z_peers()[:2]
        at = self.rows, pl.ds(pl.multiple_of(c // 8 * cols, 128), cols)
        self.aside = [lines.put(own.at[at], full.at[(s, z, *at)], peer) for peer in beside_peers()]
        self.kept = lines.keep(own.at[self.rows], full.at[s, z, self.rows])
        self.step, self.second, self.passed = {}, {}, {}

    def ring(self, layer):
        s, _, z = here()
        whole = self.full.at[layer, z, self.rows]
        self.step[layer] = [
            [self.lines.make(block, block, peer) for peer in self.peers]
            for block in (whole.at[:, half] for half in self.halves)
        ]
        self.passed[layer] = [self.lines.make(whole, whole, self.sibling)]

        def start(src):
            for copies, half in zip(self.step[layer], self.halves):
                for copy, peer in zip(copies, self.peers):
                    self.lines.again(copy, src.at[:, half], whole.at[:, half], peer)
            self.lines.again(self.passed[layer][0], src, whole, self.sibling)

        @pl.when(s == layer)
        def _():
            start(self.own.at[self.rows])

        @pl.when(s != layer)
        def _():
            for copy in self.aside:
                copy.wait_recv()
            start(whole)

    def onward(self, layer, z):
        block = self.full.at[layer, z, self.rows]
        self.passed[layer].append(self.lines.put(block, block, self.sibling))

    def neighbours(self, layer):
        _, _, z = here()
        sources = [lax.rem(z + 3, 4), lax.rem(z + 1, 4)]
        self.second[layer] = []
        for side in (0, 1):
            self.step[layer][side][side].wait_recv()
            block = self.full.at[layer, sources[side], self.rows, self.halves[side]]
            self.second[layer].append(self.lines.put(block, block, self.peers[side]))
        for side in (0, 1):
            self.step[layer][1 - side][side].wait_recv()
            self.onward(layer, sources[side])

    def opposite(self, layer):
        _, _, z = here()
        for copy in self.second[layer]:
            copy.wait_recv()
        self.onward(layer, lax.rem(z + 2, 4))

    def finish(self, layer):
        for copies in (*self.step[layer], self.second[layer]):
            for copy in copies:
                copy.wait_send()
        for copy in self.passed[layer]:
            copy.wait()

        @pl.when(lax.axis_index("section") == layer)
        def _():
            self.kept.wait()

    def close(self):
        for copy in self.aside:
            copy.wait_send()


def full_shapes(weights):
    return [sds((2, 4, *w.shape), BF16) for w in weights]


def gather_peers():
    return [sibling_of(*here()), *z_peers()[:2], *beside_peers()]


def shard_loads(full, layer, dst, sems):
    rows = full.shape[2]
    return [
        pltpu.make_async_copy(full.at[layer, i], dst.at[pl.ds(i * rows, rows)], sems.at[i])
        for i in range(4)
    ]


class Spread:
    order = [14, 10, 12, 8, 6, 4, 2]

    def __init__(self, lines, qkv_ref, q_ref, kv_ref):
        s, c, z = here()
        self.lines, self.kv_ref = lines, kv_ref
        self.sibling = sibling_of(s, c, z)
        self.kv_sends, self.whole, self.passed = {}, {}, {}
        for h in range(GH):
            kv_rows, rows = pl.ds(GW + h * ROWS, ROWS), pl.ds(h * ROWS, ROWS)
            q_rows = pl.ds(h * HEAD_DIM, HEAD_DIM)
            self.whole[h] = []
            for delta in self.order:
                peer = (s, flip(c, delta), z)
                group = peer[1] // 4
                block = qkv_ref.at[group, kv_rows]
                self.kv_sends[h, delta] = lines.put(block, kv_ref.at[c, rows], peer)
                if delta % 4 == 0:
                    block = qkv_ref.at[group, q_rows]
                    self.whole[h].append(lines.put(block, q_ref.at[c // 4, q_rows], peer))
            own = qkv_ref.at[c // 4, kv_rows]
            self.passed[h] = [lines.put(own, kv_ref.at[c, rows], self.sibling)]
            self.whole[h] += [
                lines.keep(own, kv_ref.at[c, rows]),
                lines.keep(qkv_ref.at[c // 4, q_rows], q_ref.at[c // 4, q_rows]),
            ]

    def head(self, h):
        _, c, _ = here()
        for delta in reversed(self.order):
            self.kv_sends[h, delta].wait_recv()
            block = self.kv_ref.at[flip(c, delta), pl.ds(h * ROWS, ROWS)]
            self.passed[h].append(self.lines.put(block, block, self.sibling))
        for copy in self.whole[h] + self.passed[h]:
            copy.wait()

    def finish(self):
        for copy in self.kv_sends.values():
            copy.wait_send()


class Turn:
    def __init__(self, lines, x_ref, o_ref):
        self.lines, self.x_ref, self.o_ref, self.copies = lines, x_ref, o_ref, []

    def start(self, at=0, size=GW):
        s, c, z = here()
        rows = pl.ds(at, size)
        for delta in (12, 8, 4):
            peer = (s, flip(c, delta), z)
            src = self.x_ref.at[peer[1] // 4, rows]
            self.copies.append(self.lines.put(src, self.o_ref.at[c // 4, rows], peer))
        self.copies.append(self.lines.keep(self.x_ref.at[c // 4, rows], self.o_ref.at[c // 4, rows]))
        return self

    def head(self, h):
        self.start(h * HEAD_DIM, HEAD_DIM)

    def finish(self):
        for copy in self.copies:
            copy.wait()


def forward_kernel(*refs):
    (cos, sin, inputs, gain), own, per_layer, full, (gains,), scratch = split_refs(refs, 4, 4, 11, 4, 1, 14)
    x_s, w_q, w_o, w_u, w_d, qkv_s, low_s, s_ref, got_gain, load_sem, in_sem, send, recv, gain_s = scratch
    s, c, z = here()
    lines = Lines(send, recv)
    x_load = fetch(inputs.at[s, 0], x_s, in_sem.at[0])
    across = [(1 - s, c, lax.rem(z + r, 4)) for r in (1, 3, 2)]
    ctx_peers = [(s, flip(c, delta), z) for delta in range(2, CTX, 2)]
    greet([*gather_peers(), z_peers()[2], *across, *ctx_peers])

    first = Gather(lines, own[0], full[0])
    first.ring(0)
    gain_copies = [
        lines.put(gain, got_gain.at[s, z], peer) for peer in (*z_peers(), beside_peers()[0], *across)
    ]
    gain_copies.append(lines.keep(gain, got_gain.at[s, z]))
    w_out, w_up, w_down = rest = [Gather(lines, own[i], full[i]) for i in (1, 2, 3)]
    first.neighbours(0)
    first.opposite(0)
    for gather in rest:
        gather.ring(0)
    first.finish(0)

    def progress(layer, stage):
        steps = {
            "spread": [w_out.neighbours],
            "come 0": [w_out.opposite, w_up.neighbours],
            "attend 0": [w_down.neighbours],
            "attend 1": [w_up.opposite],
            "attend 2": [w_down.opposite],
        }
        for step in steps.get(stage, ()):
            step(layer)
        if layer == 0:
            if stage == "attend 0":
                first.ring(1)
            if stage == "turn":
                first.neighbours(1)
            if stage == "mlp":
                first.opposite(1)
                for gather in rest:
                    gather.ring(1)
                first.finish(1)
                begin(1, [0])

    targets = (w_q, w_o, w_u, w_d)
    loads = [
        [shard_loads(full[i], layer, targets[i], load_sem.at[layer, i]) for i in range(4)]
        for layer in range(2)
    ]

    def begin(layer, which):
        for i in which:
            for copy in loads[layer][i]:
                copy.start()

    def loaded(layer, i):
        for copy in loads[layer][i]:
            copy.wait()

    begin(0, [0])
    for copy in gain_copies:
        copy.wait()
    for layer in range(2):
        total = got_gain[layer, 0].astype(F32) + got_gain[layer, 1].astype(F32)
        gain_s[layer] = total + got_gain[layer, 2].astype(F32) + got_gain[layer, 3].astype(F32)
    gains[...] = gain_s[...]
    x_load.wait()
    source = x_s
    for layer in range(2):
        q, kv, wide, totals, ot, out, hidden, gate_up, normed_two, product, normed = [
            ref.at[layer] for ref in per_layer
        ]
        project(
            source, gain_s[layer, 0:1, :], cos, sin, w_q, lambda: loaded(layer, 0), qkv_s.at[layer], normed
        )
        spread = Spread(lines, qkv_s.at[layer], q, kv)
        progress(layer, "spread")
        turn = Turn(lines, low_s.at[layer], ot)
        for h in range(GH):
            spread.head(h)
            progress(layer, f"come {h}")
            attend(h, h + 1, q, kv, low_s.at[layer], wide, totals, s_ref)
            turn.head(h)
            progress(layer, f"attend {h}")
        for gather in rest:
            gather.finish(layer)
        begin(layer, [1, 2, 3])
        spread.finish()
        turn.finish()
        progress(layer, "turn")
        mlp(
            ot, source, gain_s[layer, 1:2, :], w_o, w_u, w_d, lambda i: loaded(layer, i + 1),
            out, hidden, gate_up, normed_two, product,
        )
        progress(layer, "mlp")
        source = out
    for gather in (first, *rest):
        gather.close()


LAYER_SHAPES = (
    sds((4, GW, ROWS), BF16),
    sds((CTX, 2 * GW, ROWS), BF16),
    sds((4, GW, ROWS), F32),
    sds((GH, 8, 512), F32),
    sds((4, GW, ROWS), BF16),
    sds((ROWS, D), BF16),
    sds((ROWS, D), F32),
    sds((ROWS, 2 * FF), F32),
    sds((D, ROWS), BF16),
    sds((FF, ROWS), BF16),
    sds((D, ROWS), BF16),
)


def forward(inputs, gain, weights, tables):
    per_layer = [sds((2, *a.shape), a.dtype) for a in LAYER_SHAPES]
    full = full_shapes(weights)
    scratch = [
        pltpu.VMEM((ROWS, D), BF16),
        *[pltpu.VMEM((4 * w.shape[0], w.shape[1]), BF16) for w in weights],
        pltpu.VMEM((2, 4, 3 * GW, ROWS), BF16),
        pltpu.VMEM((2, 4, GW, ROWS), BF16),
        pltpu.VMEM((2048, 512), F32),
        pltpu.VMEM((2, 4, 16, D), BF16),
        DMA((2, 4, 4)),
        DMA((1,)),
        DMA((Lines.count,)),
        DMA((Lines.count,)),
        pltpu.VMEM((2, 16, D), F32),
    ]
    res = pl.pallas_call(
        forward_kernel,
        out_shape=[*per_layer, *full, sds((2, 16, D), F32)],
        in_specs=[VM, VM, ANY, ANY] + [ANY] * 4,
        out_specs=[VM] * 11 + [ANY] * 4 + [VM],
        scratch_shapes=scratch,
        compiler_params=pltpu.CompilerParams(
            collective_id=next(ids), has_side_effects=True, vmem_limit_bytes=VMEM_LIMIT
        ),
        name="forward",
    )(*tables, inputs, gain, *weights)
    return res[:11], res[11:15], res[15]


class Meet:
    def __init__(self, lines, layers, sib, far, both):
        s, c, z = here()
        self.core = core = lax.rem(c, 2)
        self.lines, self.far, self.both = lines, far, both
        self.sibling = sibling_of(s, c, z)
        peer = (1 - s, flip(c, 8) * core + c * (1 - core), z)
        self.apart = lines.put(layers.at[1 - s], far, peer)
        if sib is not None:
            self.close = lines.put(self.half(layers.at[s]), sib, self.sibling)

    def half(self, ref):
        return ref.at[:, 1 - self.core] if len(ref.shape) == 4 else ref

    def forward(self):
        self.apart.wait_recv()
        if self.both is not None:
            self.passed = self.lines.put(self.half(self.far), self.both, self.sibling)

    def finish(self):
        self.apart.wait_send()
        if self.both is not None:
            self.close.wait()
            self.passed.wait()


def meet_buffers(shape):
    half = (shape[0], *shape[2:]) if len(shape) == 4 else shape
    return [pltpu.VMEM(each, BF16) for each in (half, shape, half)]


class Show:
    def __init__(self, lines, layers, out):
        s, c, z = here()
        self.copy = lines.put(layers.at[1 - s], out.at[s], (1 - s, c, z))
        self.kept = lines.keep(layers.at[s], out.at[s])

    def finish(self):
        self.copy.wait()
        self.kept.wait()


class GiveBack:
    order = [14, 10, 12, 8, 6, 4, 2, 0]

    def __init__(self, lines, dq_ref, dkv_ref, dqo_ref, theirs, total, sums):
        self.lines, self.dkv, self.theirs, self.total, self.sums = lines, dkv_ref, theirs, total, sums
        self.turn = Turn(lines, dq_ref, dqo_ref)
        self.passed, self.sends = {}, []

    def head(self, h):
        s, c, z = here()
        rows = pl.ds(h * ROWS, ROWS)
        sibling = sibling_of(s, c, z)
        for delta in self.order:
            src = self.dkv.at[flip(flip(c, 1), delta), rows]
            self.passed[h, delta] = self.lines.put(src, self.theirs.at[delta // 2, rows], sibling)
        self.turn.head(h)

    def add(self, h):
        s, c, z = here()
        rows = slice(h * ROWS, (h + 1) * ROWS)
        for delta in self.order:
            self.passed[h, delta].wait_recv()
            at = delta // 2
            both = self.dkv[flip(c, delta), rows].astype(F32) + self.theirs[at, rows].astype(F32)
            self.total[at, rows] = both.astype(BF16)
            src, dst = self.total.at[at, rows], self.sums.at[c // 2, rows]
            if delta:
                self.sends.append(self.lines.put(src, dst, (s, flip(c, delta), z)))
            else:
                self.sends.append(self.lines.keep(src, dst))

    def finish(self):
        for copy in self.passed.values():
            copy.wait_send()
        for copy in self.sends:
            copy.wait()
        self.turn.finish()


class Reduce:
    order = [14, 10, 12, 8, 6, 4, 2]

    def __init__(self, lines, comb, fin, start, stop, along_z, got, own_sum, parts, red):
        self.lines, self.along_z, self.start = lines, along_z, start
        self.comb = comb.at[:, pl.ds(start, stop - start)]
        self.fin = fin.at[:, pl.ds(start, stop - start)]
        self.got, self.own_sum, self.parts, self.red = got, own_sum, parts, red
        self.rows = stop - start
        self.quarter = self.rows // 4
        s, c, z = here()
        self.peers = {delta: (s, flip(c, delta), z) for delta in self.order}
        self.sibling = sibling_of(s, c, z)
        self.scatter, self.sends = {}, []

    def strip(self, at):
        return pl.ds(pl.multiple_of(lax.rem(at // 2, 4) * self.quarter, 16), self.quarter)

    def side(self, at):
        return pl.ds(pl.multiple_of(at // 8 * (D // 2), 128), D // 2)

    def block(self, at):
        return self.strip(at), self.side(at)

    def along(self, shard, i):
        s, c, z = here()
        if self.along_z and i < 3:
            self.scatter[i] = self.lines.put(self.comb.at[shard], self.got.at[i], z_peers()[i])
        if not self.along_z:
            for j, delta in enumerate((4, 2, 6)):
                peer = (s, flip(c, delta), z)
                src = self.comb.at[shard, self.strip(peer[1])]
                self.scatter[i, j] = self.lines.put(src, self.got.at[j, shard], peer)

    def plane(self):
        s, c, z = here()
        for copy in self.scatter.values():
            copy.wait()
        if self.along_z:
            for at in range(0, self.rows, 64):
                rows = slice(at, at + 64)
                both = self.comb[z, rows].astype(F32) + self.got[0, rows].astype(F32)
                both += self.got[1, rows].astype(F32) + self.got[2, rows].astype(F32)
                self.own_sum[rows] = both.astype(BF16)
            for peer in self.peers.values():
                src = self.own_sum.at[self.block(peer[1])]
                self.sends.append(self.lines.put(src, self.parts.at[c // 2], peer))
            self.sends.append(self.lines.keep(self.own_sum.at[self.block(c)], self.parts.at[c // 2]))
            return
        for shard in range(4):
            both = self.comb[shard, self.strip(c)].astype(F32) + self.got[0, shard].astype(F32)
            both += self.got[1, shard].astype(F32) + self.got[2, shard].astype(F32)
            self.own_sum[shard] = both.astype(BF16)
        slot = c // 8 * 4 + z
        for far in (0, 8):
            for r in (2, 1, 3, 0):
                peer = (s, flip(c, far), lax.rem(z + r, 4))
                src = self.own_sum.at[peer[2], :, self.side(peer[1])]
                if far or r:
                    self.sends.append(self.lines.put(src, self.parts.at[slot], peer))
                else:
                    self.sends.append(self.lines.keep(src, self.parts.at[slot]))

    def spread(self):
        _, c, _ = here()
        for copy in self.sends:
            copy.wait()
        for at in range(0, self.quarter, 16):
            rows = slice(at, at + 16)
            total = self.parts[0, rows].astype(F32)
            for i in range(1, 8):
                total += self.parts[i, rows].astype(F32)
            self.red[rows] = total.astype(BF16)
        self.target = self.fin.at[lax.rem(c, 2)]
        place = self.target.at[self.block(c)]
        self.shown = {delta: self.lines.put(self.red, place, peer) for delta, peer in self.peers.items()}
        self.kept = self.lines.keep(self.red, place)
        self.passed = [self.lines.put(self.red, place, self.sibling)]

    def forward(self):
        _, c, _ = here()
        for delta in reversed(self.order):
            self.shown[delta].wait_recv()
            piece = self.target.at[self.block(flip(c, delta))]
            self.passed.append(self.lines.put(piece, piece, self.sibling))

    def finish(self):
        self.kept.wait()
        for copy in self.shown.values():
            copy.wait_send()
        for copy in self.passed:
            copy.wait()


def reduce_buffers(start, stop, along_z):
    rows = stop - start
    return [
        pltpu.VMEM((3, rows, D) if along_z else (3, 4, rows // 4, D), BF16),
        pltpu.VMEM((rows, D) if along_z else (4, rows // 4, D), BF16),
        pltpu.VMEM((8, rows // 4, D // 2), BF16),
        pltpu.VMEM((rows // 4, D // 2), BF16),
    ]


CUTS_M = ((0, 512, True), (512, MLP_ROWS, False))
CUTS_Q = ((0, 192, True), (192, QKV_ROWS, False))


LEFT_SHAPES = ((4, 2, 96, ROWS), (4, 2, 144, ROWS), (4, 2, 96, ROWS), (4, 2, 96, ROWS))
RIGHT_SHAPES = ((ROWS, 2 * FF), (ROWS, D), (ROWS, D))
HELD_SHAPES = (
    ((2, 4, GW, ROWS), BF16),
    ((2, CTX, 2 * GW, ROWS), BF16),
    ((2, 4, GW, ROWS), F32),
    ((2, GH, 8, 512), F32),
    ((2, ROWS, D), F32),
    ((2, ROWS, 2 * FF), F32),
    ((2, ROWS, D), BF16),
)


def backward_kernel(*refs):
    (
        (cos, sin, gains, cotangent, inputs, outs), full, far_held, lefts,
        (activations, input_grads, fin_m, fin_q), weights, held, left_meets, right_meets, gp_meets,
        (comb_m, comb_q), reduced, scratch,
    ) = split_refs(refs, 6, 4, 6, 4, 4, 4, 7, 12, 9, 3, 2, 16, 21)
    (
        d_ot, d_o, gg, branch, grads, gp, starts, gain_sums, gains_far, grad_hidden, d_gain, gp_f32,
        dq, dkv, dqo, theirs, total, sums, load_sem, held_sem, lines_sem,
    ) = scratch
    s, c, z = here()
    lines = Lines(lines_sem.at[0], lines_sem.at[1])
    w_q, w_o, w_u, w_d = weights
    loads = [
        [
            shard_loads(full[i], layer, weights[i], load_sem.at[layer, i]) for i in range(4)
        ]
        for layer in range(2)
    ]

    def begin(layer, which):
        for i in which:
            for copy in loads[layer][i]:
                copy.start()

    def loaded(layer, i):
        for copy in loads[layer][i]:
            copy.wait()

    cot_load = fetch(cotangent.at[s, 0], grads.at[1], held_sem.at[2, 0])
    q, kv, wide, totals, hidden, gate_up, x = held
    hold = {}
    for layer in (1, 0):
        for i in (5, 4, 0, 1, 2, 3):
            hold[layer, i] = fetch(far_held[i].at[layer], held[i].at[layer], held_sem.at[layer, i])
        begin(1, [3, 2, 1, 0] if layer == 1 else [])
    x_loads = [fetch(inputs.at[s, 0], x.at[0], held_sem.at[0, 6]), fetch(outs.at[0], x.at[1], held_sem.at[1, 6])]
    greet(
        [sibling_of(s, c, z), *z_peers(), *beside_peers()]
        + [(s, flip(c, 8), peer[2]) for peer in z_peers()]
        + [(s, flip(c, delta), z) for delta in range(2, CTX, 2)]
    )
    meets = [Meet(lines, left, *left_meets[3 * i : 3 * i + 3]) for i, left in enumerate(lefts)]
    shown = [Show(lines, outs, activations)]
    cot_load.wait()

    def run_mlp_back(layer):
        hold[layer, 5].wait()
        hold[layer, 4].wait()
        mlp_back(
            grads.at[layer], hidden.at[layer], gate_up.at[layer], gains[layer, 1:2, :], w_o, w_u, w_d,
            lambda i: loaded(layer, i + 1),
            d_ot.at[layer], grad_hidden, gg.at[layer], branch.at[layer], d_gain,
        )

    def run_attend_back(layer, h):
        if h == 0:
            for i in range(4):
                hold[layer, i].wait()
        attend_back(
            h, h + 1, q.at[layer], kv.at[layer], wide.at[layer], totals.at[layer], d_o.at[layer], dq, dkv
        )

    def give_back(layer):
        return GiveBack(lines, dq, dkv, dqo.at[layer], theirs.at[layer], total, sums.at[layer])

    def run_qkv_back(layer, ready):
        x_loads[layer].wait()
        return qkv_back(
            dqo.at[layer], sums.at[layer], x.at[layer], gains[layer, 0:1, :], cos, sin, grad_hidden, d_gain,
            w_q, lambda: loaded(layer, 0), ready,
            [starts.at[1], grads.at[0]] if layer else [starts.at[0]],
            gp.at[layer], gain_sums.at[layer], gp_f32,
        )

    run_mlp_back(1)
    begin(0, [3, 2, 1])
    turn = Turn(lines, d_ot.at[1], d_o.at[1]).start()
    for work in meets:
        work.forward()
    turn.finish()
    back = give_back(1)
    for h in range(GH):
        run_attend_back(1, h)
        back.head(h)
        if h:
            back.add(h - 1)
    back.add(GH - 1)
    back.finish()
    for work in meets + shown:
        work.finish()
    run_qkv_back(1, lambda: None)
    begin(0, [0])
    run_mlp_back(0)
    turn = Turn(lines, d_ot.at[0], d_o.at[0]).start()
    rights = (gg, grads, branch)
    meets = [Meet(lines, right, *right_meets[3 * i : 3 * i + 3]) for i, right in enumerate(rights)]
    turn.finish()
    back = give_back(0)
    run_attend_back(0, 0)
    back.head(0)
    for work in meets:
        work.forward()
    run_attend_back(0, 1)
    back.head(1)
    back.add(0)
    for work in meets:
        work.finish()
    parts = [
        Reduce(lines, comb, fin, *cut, *reduced[4 * i : 4 * i + 4])
        for i, (comb, fin, cut) in enumerate(
            [(comb_m, fin_m, cut) for cut in CUTS_M] + [(comb_q, fin_q, cut) for cut in CUTS_Q]
        )
    ]
    parts_m, parts_q = parts[:2], parts[2:]

    def along(parts, form):
        for i, r in ((2, 2), (0, 1), (1, 3), (3, 0)):
            shard = lax.rem(z + r, 4)
            form(shard)
            for part in parts:
                part.along(shard, i)

    def form_m(shard):
        for i, at in ((0, 0), (2, 288), (1, 384)):
            weight_product(
                comb_m, shard, at, lefts[i], left_meets[3 * i : 3 * i + 3],
                rights[i], right_meets[3 * i : 3 * i + 3],
            )
        comb_m[shard, 528:, :] = jnp.zeros((48, D), BF16)

    along(parts_m, form_m)
    run_attend_back(0, 2)
    back.head(2)
    back.add(1)
    back.add(2)
    back.finish()
    gp_meet = run_qkv_back(0, lambda: Meet(lines, gp, *gp_meets))
    gain_meet = Meet(lines, gain_sums, None, gains_far, None)
    shown = [Show(lines, starts, input_grads)]
    for work in (gp_meet, gain_meet):
        work.forward()
    for work in (gp_meet, gain_meet):
        work.finish()
    gain_rows = (gain_sums[s].astype(F32) + gains_far[...].astype(F32)).astype(BF16)

    def form_q(shard):
        weight_product(comb_q, shard, 0, lefts[3], left_meets[9:], gp, gp_meets)
        comb_q[shard, 288:304, :] = gain_rows
        comb_q[shard, 304:, :] = jnp.zeros((16, D), BF16)

    along(parts_q, form_q)
    for part in parts_m:
        part.plane()
    for part in parts_m:
        part.spread()
    for part in parts_q:
        part.plane()
    for part in parts_m:
        part.forward()
    for part in parts_q:
        part.spread()
    for part in parts_m:
        part.finish()
    for part in parts_q:
        part.forward()
    for work in [*parts_q, *shown]:
        work.finish()


def backward(tables, gains, cotangent, inputs, full, stored):
    q, kv, wide, totals, ot, outs, hidden, gate_up, normed_two, product, normed = stored
    lefts = [
        a.reshape(2, *shape) for a, shape in zip((normed_two, product, ot, normed), LEFT_SHAPES)
    ]
    scratch = [
        *[pltpu.VMEM((4 * w.shape[2], w.shape[3]), BF16) for w in full],
        *[pltpu.VMEM(*held) for held in HELD_SHAPES],
        *[buffer for shape in LEFT_SHAPES for buffer in meet_buffers(shape)],
        *[buffer for shape in RIGHT_SHAPES for buffer in meet_buffers(shape)],
        *meet_buffers((ROWS, 3 * D)),
        pltpu.VMEM((4, MLP_ROWS, D), BF16),
        pltpu.VMEM((4, QKV_ROWS, D), BF16),
        *[buffer for cut in CUTS_M + CUTS_Q for buffer in reduce_buffers(*cut)],
        pltpu.VMEM((2, 4, GW, ROWS), BF16),
        pltpu.VMEM((2, 4, GW, ROWS), BF16),
        pltpu.VMEM((2, ROWS, 2 * FF), BF16),
        pltpu.VMEM((2, ROWS, D), BF16),
        pltpu.VMEM((2, ROWS, D), BF16),
        pltpu.VMEM((2, ROWS, 3 * D), BF16),
        pltpu.VMEM((2, ROWS, D), BF16),
        pltpu.VMEM((2, 16, D), BF16),
        pltpu.VMEM((16, D), BF16),
        pltpu.VMEM((ROWS, D), F32),
        pltpu.VMEM((1, D), F32),
        pltpu.VMEM((3 * D, ROWS), F32),
        pltpu.VMEM((4, GW, ROWS), BF16),
        pltpu.VMEM((CTX, 2 * GW, ROWS), BF16),
        pltpu.VMEM((2, 4, GW, ROWS), BF16),
        pltpu.VMEM((2, 8, 2 * GW, ROWS), BF16),
        pltpu.VMEM((8, 2 * GW, ROWS), BF16),
        pltpu.VMEM((2, 8, 2 * GW, ROWS), BF16),
        DMA((2, 4, 4)),
        DMA((3, 7)),
        DMA((2, Lines.count)),
    ]
    return pl.pallas_call(
        backward_kernel,
        out_shape=[
            sds((2, ROWS, D), BF16), sds((2, ROWS, D), BF16),
            sds((2, MLP_ROWS, D), BF16), sds((2, QKV_ROWS, D), BF16),
        ],
        in_specs=[VM] * 3 + [ANY] * 3 + [ANY] * 4 + [ANY] * 6 + [VM] * 4,
        out_specs=[ANY, ANY, VM, VM],
        scratch_shapes=scratch,
        compiler_params=pltpu.CompilerParams(
            collective_id=next(ids), has_side_effects=True, vmem_limit_bytes=VMEM_LIMIT
        ),
        name="backward",
    )(*tables, gains, cotangent, inputs, outs, *full, q, kv, wide, totals, hidden, gate_up, *lefts)


def rope_tables():
    positions = (lax.axis_index("ctx") * ROWS + lax.iota(jnp.int32, ROWS)).astype(F32)
    frequency = 1.0 / 160000.0 ** (jnp.arange(HEAD_DIM // 2, dtype=F32) * 2.0 / HEAD_DIM)
    angles = frequency[:, None] * positions[None, :]
    return jnp.cos(angles), jnp.sin(angles)


def local(inputs, cotangent, attn_gain, qkv_weight, out_weight, mlp_gain, up_weight, down_weight):
    z = lax.axis_index("wshard")
    gain = jnp.concatenate([attn_gain, mlp_gain], axis=0)
    lanes = lax.broadcasted_iota(jnp.int32, (2, 4, 192), 1) == z
    gain = jnp.where(lanes, gain[:, None, :], jnp.zeros((), BF16)).reshape(2, D)
    gain = jnp.pad(gain, ((0, 14), (0, 0)))
    tables = rope_tables()
    stored, full, gains = forward(
        inputs, gain, [w[0] for w in (qkv_weight, out_weight, up_weight, down_weight)], tables
    )
    activations, input_grads, fin_m, fin_q = backward(tables, gains, cotangent, inputs, full, stored)
    shapes = [(192, 3 * D), (192, D), (288, D), (192, 3 * D), (1, 192), (1, 192)]
    grad_up, grad_out, grad_down, grad_qkv, gain_one, gain_two, activations, input_grads = compute_call(
        assemble_kernel,
        (fin_m, fin_q, activations, input_grads),
        [sds(shape, F32) for shape in shapes] + [sds((2, ROWS, D), BF16)] * 2,
        name="assemble",
    )
    return (
        activations[None, :, None],
        input_grads[None, :, None],
        gain_one,
        grad_qkv[None],
        grad_out[None],
        gain_two,
        grad_up[None],
        grad_down[None],
    )


def solution(mesh):
    global ids
    ids = iter(range(1, 64))
    placed = (
        P(None, "wshard", "ctx", None),
        P(None, "wshard", "ctx", None),
        P("section", "wshard"),
        P("section", "wshard", None),
        P("section", "wshard", None),
        P("section", "wshard"),
        P("section", "wshard", None),
        P("section", "wshard", None),
    )
    return jax.shard_map(
        local,
        mesh=mesh,
        in_specs=placed,
        out_specs=(
            P("section", None, "wshard", "ctx", None),
            P("section", None, "wshard", "ctx", None),
            P("section", "wshard"),
            P("section", "wshard", None),
            P("section", "wshard", None),
            P("section", "wshard"),
            P("section", "wshard", None),
            P("section", "wshard", None),
        ),
        check_vma=False,
    )
```

```python
import functools

import jax
import jax.numpy as jnp
from jax import lax
from jax.experimental import pallas as pl
from jax.experimental.pallas import tpu as pltpu
from jax.sharding import PartitionSpec as P

D = 768
HEADS = 12
HEAD_DIM = 64
FF = 1152
ROWS = 128
GROUPS = 4
GH = HEADS // GROUPS
GW = GH * HEAD_DIM
CTX = 16
SCALE = HEAD_DIM ** (-0.5)
F32 = jnp.float32
BF16 = jnp.bfloat16
MESH = pl.DeviceIdType.MESH
DMA = pltpu.SemaphoreType.DMA
ANY = pl.BlockSpec(memory_space=pl.ANY)
VM = pl.BlockSpec(memory_space=pltpu.VMEM)
VMEM_LIMIT = 60 * 1024 * 1024


def dot(a, b):
    return jnp.dot(a, b, preferred_element_type=F32)


def dot_nt(a, b):
    return lax.dot_general(a, b, (((1,), (1,)), ((), ())), preferred_element_type=F32)


def sds(shape, dtype):
    return jax.ShapeDtypeStruct(shape, dtype)


def compute_call(kernel, args, outs, name):
    return pl.pallas_call(
        kernel,
        out_shape=outs,
        in_specs=[VM] * len(args),
        out_specs=jax.tree.map(lambda _: VM, outs),
        compiler_params=pltpu.CompilerParams(vmem_limit_bytes=VMEM_LIMIT),
        name=name,
    )(*args)


def fetch(src, dst, sem):
    copy = pltpu.make_async_copy(src, dst, sem)
    copy.start()
    return copy


def turned_low(x):
    return x.astype(F32).T.astype(BF16)


def norm_parts(source):
    centered = source - jnp.mean(source, axis=-1, keepdims=True)
    variance = jnp.mean(centered * centered, axis=-1, keepdims=True)
    rstd = lax.rsqrt(variance + 1e-05)
    return centered * rstd, rstd


def norm_back(grad, normalized, rstd, gain):
    inner = grad * gain
    mean_one = jnp.mean(inner, axis=-1, keepdims=True)
    mean_two = jnp.mean(inner * normalized, axis=-1, keepdims=True)
    grad_gain = jnp.sum(grad * normalized, axis=0, keepdims=True)
    return rstd * (inner - mean_one - normalized * mean_two), grad_gain


def split_refs(refs, *counts):
    refs = list(refs)
    out = []
    for count in counts:
        out.append(refs[:count])
        refs = refs[count:]
    return out


def project(x_ref, gain, cos_ref, sin_ref, w_ref, loaded, qkv_ref, normed_ref):
    normalized, _ = norm_parts(x_ref[...].astype(F32))
    normed = (normalized * gain).astype(BF16)
    normed_ref[...] = turned_low(normed)
    loaded()
    cos = cos_ref[...]
    sin = sin_ref[...]
    for part in range(3):
        for block in range(3):
            at = part * D + block * 256
            turned = dot(normed, w_ref[:, at : at + 256]).T
            for head_at in range(4):
                head = block * 4 + head_at
                one = turned[head_at * 64 : head_at * 64 + 32]
                two = turned[head_at * 64 + 32 : head_at * 64 + 64]
                if part < 2:
                    one, two = one * cos - two * sin, two * cos + one * sin
                if part == 0:
                    one, two = one * SCALE, two * SCALE
                inner = head % GH
                row = inner * HEAD_DIM if part == 0 else GW + (2 * inner + part - 1) * HEAD_DIM
                qkv_ref[head // GH, row : row + 32, :] = one.astype(BF16)
                qkv_ref[head // GH, row + 32 : row + 64, :] = two.astype(BF16)


CHUNK = 256
CHUNKS = 2048 // CHUNK
PAIR = CHUNK // ROWS


def attend(start, stop, q_ref, kv_ref, low_ref, wide_ref, totals_ref, s_ref):
    @pl.loop(start, stop)
    def _(h):
        at = pl.multiple_of(h * HEAD_DIM, HEAD_DIM)
        key_at = pl.multiple_of(h * ROWS, ROWS)
        value_at = pl.multiple_of(h * ROWS + HEAD_DIM, HEAD_DIM)
        qt = jnp.concatenate([q_ref[i, pl.ds(at, HEAD_DIM), :] for i in range(4)], axis=1)
        top = jnp.full((8, 512), -jnp.inf, F32)
        for c in range(CHUNKS):
            keys = jnp.concatenate(
                [kv_ref[c * PAIR + i, pl.ds(key_at, HEAD_DIM), :].T for i in range(PAIR)], axis=0
            )
            scores = dot(keys, qt)
            s_ref[c * CHUNK : (c + 1) * CHUNK, :] = scores
            top = jnp.maximum(top, jnp.max(scores.reshape(CHUNK // 8, 8, 512), axis=0))
        top = jnp.max(top, axis=0, keepdims=True)
        total = jnp.zeros((8, 512), F32)
        acc = jnp.zeros((HEAD_DIM, 512), F32)
        for c in range(CHUNKS):
            p = jnp.exp(s_ref[c * CHUNK : (c + 1) * CHUNK, :] - top)
            total = total + jnp.sum(p.reshape(CHUNK // 8, 8, 512), axis=0)
            values = jnp.concatenate(
                [kv_ref[c * PAIR + i, pl.ds(value_at, HEAD_DIM), :] for i in range(PAIR)], axis=1
            )
            acc = acc + dot(values, p.astype(BF16))
        total = jnp.sum(total, axis=0, keepdims=True)
        out = acc / total
        totals_ref[h] = jnp.broadcast_to(top + jnp.log(total), (8, 512))
        for i in range(4):
            piece = out[:, i * ROWS : (i + 1) * ROWS]
            wide_ref[i, pl.ds(at, HEAD_DIM), :] = piece
            low_ref[i, pl.ds(at, HEAD_DIM), :] = piece.astype(BF16)


def attend_back(start, stop, q_ref, kv_ref, wide_ref, totals_ref, do_ref, dq_ref, dkv_ref):
    @pl.loop(start, stop)
    def _(h):
        at = pl.multiple_of(h * HEAD_DIM, HEAD_DIM)
        key_at = pl.multiple_of(h * ROWS, ROWS)
        value_at = pl.multiple_of(h * ROWS + HEAD_DIM, HEAD_DIM)
        qt = jnp.concatenate([q_ref[i, pl.ds(at, HEAD_DIM), :] for i in range(4)], axis=1)
        dot_t = jnp.concatenate([do_ref[i, pl.ds(at, HEAD_DIM), :] for i in range(4)], axis=1)
        wide = jnp.concatenate([wide_ref[i, pl.ds(at, HEAD_DIM), :] for i in range(4)], axis=1)
        delta = jnp.sum(wide * dot_t.astype(F32), axis=0, keepdims=True)
        totals = totals_ref[h, 0:1, :]
        zero = jnp.zeros((512, HEAD_DIM), BF16)
        sides = jnp.concatenate(
            [
                jnp.concatenate([qt.T, zero], axis=1),
                jnp.concatenate([zero, dot_t.T], axis=1),
            ],
            axis=0,
        )

        def step(c, acc):
            keys_t = [kv_ref[c * PAIR + i, pl.ds(key_at, HEAD_DIM), :] for i in range(PAIR)]
            values_t = [kv_ref[c * PAIR + i, pl.ds(value_at, HEAD_DIM), :] for i in range(PAIR)]
            keys = jnp.concatenate([k.T for k in keys_t], axis=0)
            values = jnp.concatenate([v.T for v in values_t], axis=0)
            p = jnp.exp(dot(keys, qt) - totals)
            ds = (p * (dot(values, dot_t) - delta)).astype(BF16)
            both = jnp.concatenate([ds, p.astype(BF16)], axis=1)
            grads = dot(both, sides).astype(BF16)
            for i in range(PAIR):
                dkv_ref[c * PAIR + i, pl.ds(key_at, ROWS), :] = grads[i * ROWS : (i + 1) * ROWS]
            return acc + dot(jnp.concatenate(keys_t, axis=1), ds)

        acc = lax.fori_loop(0, CHUNKS, step, jnp.zeros((HEAD_DIM, 512), F32)) * SCALE
        for i in range(4):
            dq_ref[i, pl.ds(at, HEAD_DIM), :] = acc[:, i * ROWS : (i + 1) * ROWS].astype(BF16)


def mlp(
    ot_ref, x_ref, gain, wo_ref, wu_ref, wd_ref, loaded,
    out_ref, hidden_ref, gate_up_ref, normed_ref, product_ref,
):
    attended = turned_low(ot_ref[...].reshape(D, ROWS))
    loaded(0)
    hidden = x_ref[...].astype(F32) + dot(attended, wo_ref[...])
    hidden_ref[...] = hidden
    normalized, _ = norm_parts(hidden)
    normed = (normalized * gain).astype(BF16)
    normed_ref[...] = turned_low(normed)
    loaded(1)
    gate_up = dot(normed, wu_ref[...])
    gate_up_ref[...] = gate_up
    gate = gate_up[:, :FF]
    phi = 0.5 * (1.0 + lax.erf(gate * 0.5**0.5))
    product = (gate * phi * gate_up[:, FF:]).astype(BF16)
    product_ref[...] = turned_low(product)
    loaded(2)
    out_ref[...] = (hidden + dot(product, wd_ref[...])).astype(BF16)


def mlp_back(
    grad_ref, hidden_ref, gate_up_ref, gain, wo_ref, wu_ref, wd_ref, loaded,
    dot_ref, grad_hidden_ref, gg_ref, branch_ref, d_gain_ref,
):
    grad = grad_ref[...]
    loaded(2)
    grad_product = dot_nt(grad, wd_ref[...])
    gate = gate_up_ref[:, :FF]
    up = gate_up_ref[:, FF:]
    phi = 0.5 * (1.0 + lax.erf(gate * 0.5**0.5))
    density = jnp.exp(-0.5 * gate * gate) * 0.3989422804014327
    grad_gate = (grad_product * up * (phi + gate * density)).astype(BF16)
    grad_up = (grad_product * gate * phi).astype(BF16)
    gg_ref[:, :FF] = grad_gate
    gg_ref[:, FF:] = grad_up
    loaded(1)
    grad_normed = dot_nt(grad_gate, wu_ref[:, :FF]) + dot_nt(grad_up, wu_ref[:, FF:])
    normalized, rstd = norm_parts(hidden_ref[...])
    part, d_gain = norm_back(grad_normed, normalized, rstd, gain)
    d_gain_ref[...] = d_gain
    grad_hidden = grad.astype(F32) + part
    grad_hidden_ref[...] = grad_hidden
    branch = grad_hidden.astype(BF16)
    branch_ref[...] = branch
    loaded(0)
    turned = dot_nt(branch, wo_ref[...]).T.astype(BF16)
    for group in range(GROUPS):
        dot_ref[group] = turned[group * GW : (group + 1) * GW]


def qkv_back(
    dq_ref, dkv_ref, x_ref, gain, cos_ref, sin_ref, grad_hidden_ref, gain_two_ref, w_ref, loaded, ready,
    grad_x_refs, gp_out_ref, gains_ref, gp_ref,
):
    cos = cos_ref[...]
    sin = sin_ref[...]

    def back(one, two):
        return one * cos + two * sin, two * cos - one * sin

    for head in range(HEADS):
        group, inner = head // GH, head % GH
        at = inner * HEAD_DIM
        one = dq_ref[group, at : at + 32, :].astype(F32)
        two = dq_ref[group, at + 32 : at + 64, :].astype(F32)
        gq = back(one, two)
        rows = slice(inner * ROWS, (inner + 1) * ROWS)
        kv = (dkv_ref[2 * group, rows, :].astype(F32) + dkv_ref[2 * group + 1, rows, :].astype(F32)).T
        gk = back(kv[:32], kv[32:64])
        base = head * HEAD_DIM
        gp_ref[base : base + 32, :] = gq[0]
        gp_ref[base + 32 : base + 64, :] = gq[1]
        gp_ref[D + base : D + base + 32, :] = gk[0]
        gp_ref[D + base + 32 : D + base + 64, :] = gk[1]
        gp_ref[2 * D + base : 2 * D + base + 64, :] = kv[64:]
    for block in range(9):
        cols = slice(block * 256, (block + 1) * 256)
        gp_out_ref[:, cols] = gp_ref[cols, :].T.astype(BF16)
    result = ready()
    loaded()
    grad_normed = jnp.zeros((ROWS, D), F32)
    for block in range(9):
        cols = slice(block * 256, (block + 1) * 256)
        grad_normed = grad_normed + dot_nt(gp_out_ref[:, cols], w_ref[:, cols])
    normalized, rstd = norm_parts(x_ref[...].astype(F32))
    part, d_gain = norm_back(grad_normed, normalized, rstd, gain)
    gains_ref[...] = jnp.concatenate(
        [d_gain, gain_two_ref[...], jnp.zeros((14, D), F32)], axis=0
    ).astype(BF16)
    for ref in grad_x_refs:
        ref[...] = (grad_hidden_ref[...] + part).astype(BF16)
    return result


MLP_ROWS = 576
QKV_ROWS = 320
SUM_ROWS = MLP_ROWS + QKV_ROWS


def weight_product(out_ref, shard, at, left, lefts, right, rights):
    section = lax.axis_index("section")
    core = lax.rem(lax.axis_index("ctx"), 2)
    (a_sib, a_far, a_both), (g_sib, g_far, g_both) = lefts, rights
    height = a_sib.shape[1]
    a = [left[section, shard, core], a_sib[shard], a_far[shard, core], a_both[shard]]
    a = jnp.concatenate(a, axis=1)
    for block in range(g_sib.shape[1] // D):
        cols = slice(block * D, (block + 1) * D)
        g = [right[section, :, cols], g_sib[:, cols], g_far[:, cols], g_both[:, cols]]
        row = at + block * height
        out_ref[shard, row : row + height, :] = dot(a, jnp.concatenate(g, axis=0)).astype(BF16)


def assemble_kernel(
    mlp_ref, qkv_in_ref, act_ref, grad_ref, up_ref, out_ref, down_ref, qkv_ref, one_ref, two_ref, act_out, grad_out
):
    act_out[...] = act_ref[...]
    grad_out[...] = grad_ref[...]
    for half in range(2):
        rows = slice(half * 96, half * 96 + 96)
        for block in range(3):
            cols = slice(block * D, (block + 1) * D)
            at = slice(block * 96, block * 96 + 96)
            up_ref[rows, cols] = mlp_ref[half, at, :].astype(F32)
            qkv_ref[rows, cols] = qkv_in_ref[half, at, :].astype(F32)
        out_ref[rows, :] = mlp_ref[half, 288:384, :].astype(F32)
        down_ref[half * 144 : half * 144 + 144, :] = mlp_ref[half, 384:528, :].astype(F32)
    gains = qkv_in_ref[0, 288:304, :].astype(F32) + qkv_in_ref[1, 288:304, :].astype(F32)
    z = lax.axis_index("wshard")
    mine = gains[:, :192]
    for shard in range(1, 4):
        mine = jnp.where(z == shard, gains[:, shard * 192 : shard * 192 + 192], mine)
    one_ref[...] = mine[0:1]
    two_ref[...] = mine[1:2]


def here():
    return lax.axis_index("section"), lax.axis_index("ctx"), lax.axis_index("wshard")


def flip(index, delta):
    for bit in (1, 2, 4, 8):
        if delta & bit:
            index = index + bit - 2 * bit * lax.rem(index // bit, 2)
    return index


def greet(peers):
    barrier = pltpu.get_barrier_semaphore()
    for peer in peers:
        pl.semaphore_signal(barrier, inc=1, device_id=peer, device_id_type=MESH)
    pl.semaphore_wait(barrier, len(peers))


def remote(src, dst, send, recv, peer):
    return pltpu.make_async_remote_copy(
        src_ref=src, dst_ref=dst, send_sem=send, recv_sem=recv, device_id=peer, device_id_type=MESH
    )


class Lines:
    count = 288

    def __init__(self, send, recv):
        self.send, self.recv, self.used, self.places = send, recv, 0, {}

    def make(self, src, dst, peer):
        at = self.used
        self.used += 1
        assert at < self.count
        copy = remote(src, dst, self.send.at[at], self.recv.at[at], peer)
        self.places[id(copy)] = at
        return copy

    def put(self, src, dst, peer):
        copy = self.make(src, dst, peer)
        copy.start()
        return copy

    def again(self, made, src, dst, peer):
        at = self.places[id(made)]
        remote(src, dst, self.send.at[at], self.recv.at[at], peer).start()

    def keep(self, src, dst):
        at = self.used
        self.used += 1
        assert at < self.count
        copy = pltpu.make_async_copy(src, dst, self.send.at[at])
        copy.start()
        return copy


ids = iter(range(1, 64))


def sibling_of(s, c, z):
    return (s, flip(c, 1), z)


def z_peers():
    s, c, z = here()
    return [(s, c, lax.rem(z + r, 4)) for r in (1, 3, 2)]


def beside_peers():
    s, c, z = here()
    return [(1 - s, c, z), (1 - s, flip(c, 8), z)]


class Gather:
    def __init__(self, lines, own, full):
        s, c, z = here()
        rows, cols = full.shape[2] // 2, full.shape[3] // 2
        self.rows = pl.ds(pl.multiple_of(lax.rem(c, 2) * rows, 16), rows)
        self.halves = [pl.ds(0, cols), pl.ds(cols, cols)]
        self.lines, self.own, self.full = lines, own, full
        self.sibling = sibling_of(s, c, z)
        self.peers = z_peers()[:2]
        at = self.rows, pl.ds(pl.multiple_of(c // 8 * cols, 128), cols)
        self.aside = [lines.put(own.at[at], full.at[(s, z, *at)], peer) for peer in beside_peers()]
        self.kept = lines.keep(own.at[self.rows], full.at[s, z, self.rows])
        self.step, self.second, self.passed = {}, {}, {}

    def ring(self, layer):
        s, _, z = here()
        whole = self.full.at[layer, z, self.rows]
        self.step[layer] = [
            [self.lines.make(block, block, peer) for peer in self.peers]
            for block in (whole.at[:, half] for half in self.halves)
        ]
        self.passed[layer] = [self.lines.make(whole, whole, self.sibling)]

        def start(src):
            for copies, half in zip(self.step[layer], self.halves):
                for copy, peer in zip(copies, self.peers):
                    self.lines.again(copy, src.at[:, half], whole.at[:, half], peer)
            self.lines.again(self.passed[layer][0], src, whole, self.sibling)

        @pl.when(s == layer)
        def _():
            start(self.own.at[self.rows])

        @pl.when(s != layer)
        def _():
            for copy in self.aside:
                copy.wait_recv()
            start(whole)

    def onward(self, layer, z):
        block = self.full.at[layer, z, self.rows]
        self.passed[layer].append(self.lines.put(block, block, self.sibling))

    def neighbours(self, layer):
        _, _, z = here()
        sources = [lax.rem(z + 3, 4), lax.rem(z + 1, 4)]
        self.second[layer] = []
        for side in (0, 1):
            self.step[layer][side][side].wait_recv()
            block = self.full.at[layer, sources[side], self.rows, self.halves[side]]
            self.second[layer].append(self.lines.put(block, block, self.peers[side]))
        for side in (0, 1):
            self.step[layer][1 - side][side].wait_recv()
            self.onward(layer, sources[side])

    def opposite(self, layer):
        _, _, z = here()
        for copy in self.second[layer]:
            copy.wait_recv()
        self.onward(layer, lax.rem(z + 2, 4))

    def finish(self, layer):
        for copies in (*self.step[layer], self.second[layer]):
            for copy in copies:
                copy.wait_send()
        for copy in self.passed[layer]:
            copy.wait()

        @pl.when(lax.axis_index("section") == layer)
        def _():
            self.kept.wait()

    def crossed(self):
        for copy in self.aside:
            copy.wait_send()


def full_shapes(weights):
    return [sds((2, 4, *w.shape), BF16) for w in weights]


def gather_peers():
    return [sibling_of(*here()), *z_peers()[:2], *beside_peers()]


def shard_loads(full, layer, dst, sems):
    rows = full.shape[2]
    return [
        pltpu.make_async_copy(full.at[layer, i], dst.at[pl.ds(i * rows, rows)], sems.at[i])
        for i in range(4)
    ]


class Spread:
    order = [14, 10, 12, 8, 6, 4, 2]

    def __init__(self, lines, qkv_ref, q_ref, kv_ref):
        s, c, z = here()
        self.lines, self.kv_ref = lines, kv_ref
        self.sibling = sibling_of(s, c, z)
        self.kv_sends, self.whole, self.passed = {}, {}, {}
        for h in range(GH):
            kv_rows, rows = pl.ds(GW + h * ROWS, ROWS), pl.ds(h * ROWS, ROWS)
            q_rows = pl.ds(h * HEAD_DIM, HEAD_DIM)
            self.whole[h] = []
            for delta in self.order:
                peer = (s, flip(c, delta), z)
                group = peer[1] // 4
                block = qkv_ref.at[group, kv_rows]
                self.kv_sends[h, delta] = lines.put(block, kv_ref.at[c, rows], peer)
                if delta % 4 == 0:
                    block = qkv_ref.at[group, q_rows]
                    self.whole[h].append(lines.put(block, q_ref.at[c // 4, q_rows], peer))
            own = qkv_ref.at[c // 4, kv_rows]
            self.passed[h] = [lines.put(own, kv_ref.at[c, rows], self.sibling)]
            self.whole[h] += [
                lines.keep(own, kv_ref.at[c, rows]),
                lines.keep(qkv_ref.at[c // 4, q_rows], q_ref.at[c // 4, q_rows]),
            ]

    def head(self, h):
        _, c, _ = here()
        for delta in reversed(self.order):
            self.kv_sends[h, delta].wait_recv()
            block = self.kv_ref.at[flip(c, delta), pl.ds(h * ROWS, ROWS)]
            self.passed[h].append(self.lines.put(block, block, self.sibling))
        for copy in self.whole[h] + self.passed[h]:
            copy.wait()

    def finish(self):
        for copy in self.kv_sends.values():
            copy.wait_send()


class Turn:
    def __init__(self, lines, x_ref, o_ref):
        self.lines, self.x_ref, self.o_ref, self.copies = lines, x_ref, o_ref, []

    def start(self, at=0, size=GW):
        s, c, z = here()
        rows = pl.ds(at, size)
        for delta in (12, 8, 4):
            peer = (s, flip(c, delta), z)
            src = self.x_ref.at[peer[1] // 4, rows]
            self.copies.append(self.lines.put(src, self.o_ref.at[c // 4, rows], peer))
        self.copies.append(self.lines.keep(self.x_ref.at[c // 4, rows], self.o_ref.at[c // 4, rows]))
        return self

    def head(self, h):
        self.start(h * HEAD_DIM, HEAD_DIM)

    def finish(self):
        for copy in self.copies:
            copy.wait()


def forward_kernel(*refs):
    (cos, sin, inputs, gain), own, per_layer, full, (gains,), scratch = split_refs(refs, 4, 4, 11, 4, 1, 14)
    x_s, w_q, w_o, w_u, w_d, qkv_s, low_s, s_ref, got_gain, load_sem, in_sem, send, recv, gain_s = scratch
    s, c, z = here()
    lines = Lines(send, recv)
    x_load = fetch(inputs.at[s, 0], x_s, in_sem.at[0])
    across = [(1 - s, c, lax.rem(z + r, 4)) for r in (1, 3, 2)]
    ctx_peers = [(s, flip(c, delta), z) for delta in range(2, CTX, 2)]
    greet([*gather_peers(), z_peers()[2], *across, *ctx_peers])

    first = Gather(lines, own[0], full[0])
    first.ring(0)
    gain_copies = [
        lines.put(gain, got_gain.at[s, z], peer) for peer in (*z_peers(), beside_peers()[0], *across)
    ]
    gain_copies.append(lines.keep(gain, got_gain.at[s, z]))
    first.crossed()
    w_out, w_up, w_down = rest = [Gather(lines, own[i], full[i]) for i in (1, 2, 3)]
    first.neighbours(0)
    first.opposite(0)
    for gather in rest:
        gather.ring(0)
    first.finish(0)

    def progress(layer, stage):
        steps = {
            "spread": [w_out.neighbours],
            "come 0": [w_out.opposite, w_up.neighbours],
            "attend 0": [w_down.neighbours],
            "attend 1": [w_up.opposite],
            "attend 2": [w_down.opposite],
        }
        for step in steps.get(stage, ()):
            step(layer)
        if layer == 0:
            if stage == "attend 0":
                first.ring(1)
            if stage == "turn":
                first.neighbours(1)
            if stage == "mlp":
                first.opposite(1)
                for gather in rest:
                    gather.ring(1)
                first.finish(1)
                begin(1, [0])

    targets = (w_q, w_o, w_u, w_d)
    loads = [
        [shard_loads(full[i], layer, targets[i], load_sem.at[layer, i]) for i in range(4)]
        for layer in range(2)
    ]

    def begin(layer, which):
        for i in which:
            for copy in loads[layer][i]:
                copy.start()

    def loaded(layer, i):
        for copy in loads[layer][i]:
            copy.wait()

    begin(0, [0])
    for copy in gain_copies:
        copy.wait()
    for layer in range(2):
        total = got_gain[layer, 0].astype(F32) + got_gain[layer, 1].astype(F32)
        gain_s[layer] = total + got_gain[layer, 2].astype(F32) + got_gain[layer, 3].astype(F32)
    gains[...] = gain_s[...]
    x_load.wait()
    source = x_s
    for layer in range(2):
        q, kv, wide, totals, ot, out, hidden, gate_up, normed_two, product, normed = [
            ref.at[layer] for ref in per_layer
        ]
        project(
            source, gain_s[layer, 0:1, :], cos, sin, w_q, lambda: loaded(layer, 0), qkv_s.at[layer], normed
        )
        spread = Spread(lines, qkv_s.at[layer], q, kv)
        progress(layer, "spread")
        turn = Turn(lines, low_s.at[layer], ot)
        for h in range(GH):
            spread.head(h)
            progress(layer, f"come {h}")
            attend(h, h + 1, q, kv, low_s.at[layer], wide, totals, s_ref)
            turn.head(h)
            progress(layer, f"attend {h}")
        for gather in rest:
            gather.finish(layer)
        begin(layer, [1, 2, 3])
        spread.finish()
        turn.finish()
        progress(layer, "turn")
        mlp(
            ot, source, gain_s[layer, 1:2, :], w_o, w_u, w_d, lambda i: loaded(layer, i + 1),
            out, hidden, gate_up, normed_two, product,
        )
        progress(layer, "mlp")
        source = out
    for gather in rest:
        gather.crossed()


LAYER_SHAPES = (
    sds((4, GW, ROWS), BF16),
    sds((CTX, 2 * GW, ROWS), BF16),
    sds((4, GW, ROWS), F32),
    sds((GH, 8, 512), F32),
    sds((4, GW, ROWS), BF16),
    sds((ROWS, D), BF16),
    sds((ROWS, D), F32),
    sds((ROWS, 2 * FF), F32),
    sds((D, ROWS), BF16),
    sds((FF, ROWS), BF16),
    sds((D, ROWS), BF16),
)


def forward(inputs, gain, weights, tables):
    per_layer = [sds((2, *a.shape), a.dtype) for a in LAYER_SHAPES]
    full = full_shapes(weights)
    scratch = [
        pltpu.VMEM((ROWS, D), BF16),
        *[pltpu.VMEM((4 * w.shape[0], w.shape[1]), BF16) for w in weights],
        pltpu.VMEM((2, 4, 3 * GW, ROWS), BF16),
        pltpu.VMEM((2, 4, GW, ROWS), BF16),
        pltpu.VMEM((2048, 512), F32),
        pltpu.VMEM((2, 4, 16, D), BF16),
        DMA((2, 4, 4)),
        DMA((1,)),
        DMA((Lines.count,)),
        DMA((Lines.count,)),
        pltpu.VMEM((2, 16, D), F32),
    ]
    res = pl.pallas_call(
        forward_kernel,
        out_shape=[*per_layer, *full, sds((2, 16, D), F32)],
        in_specs=[VM, VM, ANY, ANY] + [ANY] * 4,
        out_specs=[VM] * 11 + [ANY] * 4 + [VM],
        scratch_shapes=scratch,
        compiler_params=pltpu.CompilerParams(
            collective_id=next(ids), has_side_effects=True, vmem_limit_bytes=VMEM_LIMIT
        ),
        name="forward",
    )(*tables, inputs, gain, *weights)
    return res[:11], res[11:15], res[15]


class Meet:
    def __init__(self, lines, layers, sib, far, both):
        s, c, z = here()
        self.core = core = lax.rem(c, 2)
        self.lines, self.far, self.both = lines, far, both
        self.sibling = sibling_of(s, c, z)
        peer = (1 - s, flip(c, 8) * core + c * (1 - core), z)
        self.apart = lines.put(layers.at[1 - s], far, peer)
        if sib is not None:
            self.close = lines.put(self.half(layers.at[s]), sib, self.sibling)

    def half(self, ref):
        return ref.at[:, 1 - self.core] if len(ref.shape) == 4 else ref

    def forward(self):
        self.apart.wait_recv()
        if self.both is not None:
            self.passed = self.lines.put(self.half(self.far), self.both, self.sibling)

    def finish(self):
        self.apart.wait_send()
        if self.both is not None:
            self.close.wait()
            self.passed.wait()


def meet_buffers(shape):
    half = (shape[0], *shape[2:]) if len(shape) == 4 else shape
    return [pltpu.VMEM(each, BF16) for each in (half, shape, half)]


class Show:
    def __init__(self, lines, layers, out):
        s, c, z = here()
        self.copy = lines.put(layers.at[1 - s], out.at[s], (1 - s, c, z))
        self.kept = lines.keep(layers.at[s], out.at[s])

    def finish(self):
        self.copy.wait()
        self.kept.wait()


class GiveBack:
    order = [14, 10, 12, 8, 6, 4, 2, 0]

    def __init__(self, lines, dq_ref, dkv_ref, dqo_ref, theirs, total, sums):
        self.lines, self.dkv, self.theirs, self.total, self.sums = lines, dkv_ref, theirs, total, sums
        self.turn = Turn(lines, dq_ref, dqo_ref)
        self.passed, self.sends = {}, []

    def head(self, h):
        s, c, z = here()
        rows = pl.ds(h * ROWS, ROWS)
        sibling = sibling_of(s, c, z)
        for delta in self.order:
            src = self.dkv.at[flip(flip(c, 1), delta), rows]
            self.passed[h, delta] = self.lines.put(src, self.theirs.at[delta // 2, rows], sibling)
        self.turn.head(h)

    def add(self, h):
        s, c, z = here()
        rows = slice(h * ROWS, (h + 1) * ROWS)
        for delta in self.order:
            self.passed[h, delta].wait_recv()
            at = delta // 2
            both = self.dkv[flip(c, delta), rows].astype(F32) + self.theirs[at, rows].astype(F32)
            self.total[at, rows] = both.astype(BF16)
            src, dst = self.total.at[at, rows], self.sums.at[c // 2, rows]
            if delta:
                self.sends.append(self.lines.put(src, dst, (s, flip(c, delta), z)))
            else:
                self.sends.append(self.lines.keep(src, dst))

    def finish(self):
        for copy in self.passed.values():
            copy.wait_send()
        for copy in self.sends:
            copy.wait()
        self.turn.finish()


class Reduce:
    order = [14, 10, 12, 8, 6, 4, 2]

    def __init__(self, lines, comb, fin, start, stop, along_z, got, own_sum, parts, red):
        self.lines, self.along_z, self.start = lines, along_z, start
        self.comb = comb.at[:, pl.ds(start, stop - start)]
        self.fin = fin.at[:, pl.ds(start, stop - start)]
        self.got, self.own_sum, self.parts, self.red = got, own_sum, parts, red
        self.rows = stop - start
        self.quarter = self.rows // 4
        s, c, z = here()
        self.peers = {delta: (s, flip(c, delta), z) for delta in self.order}
        self.sibling = sibling_of(s, c, z)
        self.scatter, self.sends = {}, []

    def strip(self, at):
        return pl.ds(pl.multiple_of(lax.rem(at // 2, 4) * self.quarter, 16), self.quarter)

    def side(self, at):
        return pl.ds(pl.multiple_of(at // 8 * (D // 2), 128), D // 2)

    def block(self, at):
        return self.strip(at), self.side(at)

    def along(self, shard, i):
        s, c, z = here()
        if self.along_z and i < 3:
            self.scatter[i] = self.lines.put(self.comb.at[shard], self.got.at[i], z_peers()[i])
        if not self.along_z:
            for j, delta in enumerate((4, 2, 6)):
                peer = (s, flip(c, delta), z)
                src = self.comb.at[shard, self.strip(peer[1])]
                self.scatter[i, j] = self.lines.put(src, self.got.at[j, shard], peer)

    def plane(self):
        s, c, z = here()
        for copy in self.scatter.values():
            copy.wait()
        if self.along_z:
            for at in range(0, self.rows, 64):
                rows = slice(at, at + 64)
                both = self.comb[z, rows].astype(F32) + self.got[0, rows].astype(F32)
                both += self.got[1, rows].astype(F32) + self.got[2, rows].astype(F32)
                self.own_sum[rows] = both.astype(BF16)
            for peer in self.peers.values():
                src = self.own_sum.at[self.block(peer[1])]
                self.sends.append(self.lines.put(src, self.parts.at[c // 2], peer))
            self.sends.append(self.lines.keep(self.own_sum.at[self.block(c)], self.parts.at[c // 2]))
            return
        for shard in range(4):
            both = self.comb[shard, self.strip(c)].astype(F32) + self.got[0, shard].astype(F32)
            both += self.got[1, shard].astype(F32) + self.got[2, shard].astype(F32)
            self.own_sum[shard] = both.astype(BF16)
        slot = c // 8 * 4 + z
        for far in (0, 8):
            for r in (2, 1, 3, 0):
                peer = (s, flip(c, far), lax.rem(z + r, 4))
                src = self.own_sum.at[peer[2], :, self.side(peer[1])]
                if far or r:
                    self.sends.append(self.lines.put(src, self.parts.at[slot], peer))
                else:
                    self.sends.append(self.lines.keep(src, self.parts.at[slot]))

    def spread(self):
        _, c, _ = here()
        for copy in self.sends:
            copy.wait()
        for at in range(0, self.quarter, 16):
            rows = slice(at, at + 16)
            total = self.parts[0, rows].astype(F32)
            for i in range(1, 8):
                total += self.parts[i, rows].astype(F32)
            self.red[rows] = total.astype(BF16)
        self.target = self.fin.at[lax.rem(c, 2)]
        place = self.target.at[self.block(c)]
        self.shown = {delta: self.lines.put(self.red, place, peer) for delta, peer in self.peers.items()}
        self.kept = self.lines.keep(self.red, place)
        self.passed = [self.lines.put(self.red, place, self.sibling)]

    def forward(self):
        _, c, _ = here()
        for delta in reversed(self.order):
            self.shown[delta].wait_recv()
            piece = self.target.at[self.block(flip(c, delta))]
            self.passed.append(self.lines.put(piece, piece, self.sibling))

    def finish(self):
        self.kept.wait()
        for copy in self.shown.values():
            copy.wait_send()
        for copy in self.passed:
            copy.wait()


def reduce_buffers(start, stop, along_z):
    rows = stop - start
    return [
        pltpu.VMEM((3, rows, D) if along_z else (3, 4, rows // 4, D), BF16),
        pltpu.VMEM((rows, D) if along_z else (4, rows // 4, D), BF16),
        pltpu.VMEM((8, rows // 4, D // 2), BF16),
        pltpu.VMEM((rows // 4, D // 2), BF16),
    ]


CUTS_M = ((0, 256, True), (256, MLP_ROWS, True))
CUTS_Q = ((0, 192, True), (192, QKV_ROWS, False))


LEFT_SHAPES = ((4, 2, 96, ROWS), (4, 2, 144, ROWS), (4, 2, 96, ROWS), (4, 2, 96, ROWS))
RIGHT_SHAPES = ((ROWS, 2 * FF), (ROWS, D), (ROWS, D))
HELD_SHAPES = (
    ((2, 4, GW, ROWS), BF16),
    ((2, CTX, 2 * GW, ROWS), BF16),
    ((2, 4, GW, ROWS), F32),
    ((2, GH, 8, 512), F32),
    ((2, ROWS, D), F32),
    ((2, ROWS, 2 * FF), F32),
    ((2, ROWS, D), BF16),
)


def backward_kernel(*refs):
    (
        (cos, sin, gains, cotangent, inputs, outs), full, far_held, lefts,
        (activations, input_grads, fin_m, fin_q), weights, held, left_meets, right_meets, gp_meets,
        (comb_m, comb_q), reduced, scratch,
    ) = split_refs(refs, 6, 4, 6, 4, 4, 4, 7, 12, 9, 3, 2, 16, 21)
    (
        d_ot, d_o, gg, branch, grads, gp, starts, gain_sums, gains_far, grad_hidden, d_gain, gp_f32,
        dq, dkv, dqo, theirs, total, sums, load_sem, held_sem, lines_sem,
    ) = scratch
    s, c, z = here()
    lines = Lines(lines_sem.at[0], lines_sem.at[1])
    w_q, w_o, w_u, w_d = weights
    loads = [
        [
            shard_loads(full[i], layer, weights[i], load_sem.at[layer, i]) for i in range(4)
        ]
        for layer in range(2)
    ]

    def begin(layer, which):
        for i in which:
            for copy in loads[layer][i]:
                copy.start()

    def loaded(layer, i):
        for copy in loads[layer][i]:
            copy.wait()

    cot_load = fetch(cotangent.at[s, 0], grads.at[1], held_sem.at[2, 0])
    q, kv, wide, totals, hidden, gate_up, x = held
    hold = {}
    for layer in (1, 0):
        for i in (5, 4, 0, 1, 2, 3):
            hold[layer, i] = fetch(far_held[i].at[layer], held[i].at[layer], held_sem.at[layer, i])
        begin(1, [3, 2, 1, 0] if layer == 1 else [])
    x_loads = [fetch(inputs.at[s, 0], x.at[0], held_sem.at[0, 6]), fetch(outs.at[0], x.at[1], held_sem.at[1, 6])]
    greet(
        [sibling_of(s, c, z), *z_peers(), *beside_peers()]
        + [(s, flip(c, 8), peer[2]) for peer in z_peers()]
        + [(s, flip(c, delta), z) for delta in range(2, CTX, 2)]
    )
    meets = [Meet(lines, left, *left_meets[3 * i : 3 * i + 3]) for i, left in enumerate(lefts)]
    shown = [Show(lines, outs, activations)]
    cot_load.wait()

    def run_mlp_back(layer):
        hold[layer, 5].wait()
        hold[layer, 4].wait()
        mlp_back(
            grads.at[layer], hidden.at[layer], gate_up.at[layer], gains[layer, 1:2, :], w_o, w_u, w_d,
            lambda i: loaded(layer, i + 1),
            d_ot.at[layer], grad_hidden, gg.at[layer], branch.at[layer], d_gain,
        )

    def run_attend_back(layer, h):
        if h == 0:
            for i in range(4):
                hold[layer, i].wait()
        attend_back(
            h, h + 1, q.at[layer], kv.at[layer], wide.at[layer], totals.at[layer], d_o.at[layer], dq, dkv
        )

    def give_back(layer):
        return GiveBack(lines, dq, dkv, dqo.at[layer], theirs.at[layer], total, sums.at[layer])

    def run_qkv_back(layer, ready):
        x_loads[layer].wait()
        return qkv_back(
            dqo.at[layer], sums.at[layer], x.at[layer], gains[layer, 0:1, :], cos, sin, grad_hidden, d_gain,
            w_q, lambda: loaded(layer, 0), ready,
            [starts.at[1], grads.at[0]] if layer else [starts.at[0]],
            gp.at[layer], gain_sums.at[layer], gp_f32,
        )

    run_mlp_back(1)
    begin(0, [3, 2, 1])
    turn = Turn(lines, d_ot.at[1], d_o.at[1]).start()
    for work in meets:
        work.forward()
    turn.finish()
    back = give_back(1)
    for h in range(GH):
        run_attend_back(1, h)
        back.head(h)
        if h:
            back.add(h - 1)
    back.add(GH - 1)
    back.finish()
    for work in meets + shown:
        work.finish()
    run_qkv_back(1, lambda: None)
    begin(0, [0])
    run_mlp_back(0)
    turn = Turn(lines, d_ot.at[0], d_o.at[0]).start()
    rights = (gg, grads, branch)
    meets = [Meet(lines, right, *right_meets[3 * i : 3 * i + 3]) for i, right in enumerate(rights)]
    turn.finish()
    back = give_back(0)
    run_attend_back(0, 0)
    back.head(0)
    for work in meets:
        work.forward()
    run_attend_back(0, 1)
    back.head(1)
    back.add(0)
    for work in meets:
        work.finish()
    parts = [
        Reduce(lines, comb, fin, *cut, *reduced[4 * i : 4 * i + 4])
        for i, (comb, fin, cut) in enumerate(
            [(comb_m, fin_m, cut) for cut in CUTS_M] + [(comb_q, fin_q, cut) for cut in CUTS_Q]
        )
    ]
    parts_m, parts_q = parts[:2], parts[2:]

    def along(parts, form):
        steps = [(i, lax.rem(z + r, 4)) for i, r in ((2, 2), (0, 1), (1, 3), (3, 0))]
        for i, shard in steps:
            form(shard)
            parts[0].along(shard, i)
        for i, shard in steps:
            parts[1].along(shard, i)

    def form_m(shard):
        for i, at in ((0, 0), (2, 288), (1, 384)):
            weight_product(
                comb_m, shard, at, lefts[i], left_meets[3 * i : 3 * i + 3],
                rights[i], right_meets[3 * i : 3 * i + 3],
            )
        comb_m[shard, 528:, :] = jnp.zeros((48, D), BF16)

    along(parts_m, form_m)
    run_attend_back(0, 2)
    back.head(2)
    back.add(1)
    back.add(2)
    back.finish()
    gp_meet = run_qkv_back(0, lambda: Meet(lines, gp, *gp_meets))
    gain_meet = Meet(lines, gain_sums, None, gains_far, None)
    shown = [Show(lines, starts, input_grads)]
    for work in (gp_meet, gain_meet):
        work.forward()
    parts_m[0].plane()
    for work in (gp_meet, gain_meet):
        work.finish()
    gain_rows = (gain_sums[s].astype(F32) + gains_far[...].astype(F32)).astype(BF16)

    def form_q(shard):
        weight_product(comb_q, shard, 0, lefts[3], left_meets[9:], gp, gp_meets)
        comb_q[shard, 288:304, :] = gain_rows
        comb_q[shard, 304:, :] = jnp.zeros((16, D), BF16)

    along(parts_q, form_q)
    parts_m[0].spread()
    parts_m[1].plane()
    parts_m[1].spread()
    for part in parts_q:
        part.plane()
    for part in parts_m:
        part.forward()
    for part in parts_q:
        part.spread()
    for part in parts_m:
        part.finish()
    for part in parts_q:
        part.forward()
    for work in [*parts_q, *shown]:
        work.finish()


def backward(tables, gains, cotangent, inputs, full, stored):
    q, kv, wide, totals, ot, outs, hidden, gate_up, normed_two, product, normed = stored
    lefts = [
        a.reshape(2, *shape) for a, shape in zip((normed_two, product, ot, normed), LEFT_SHAPES)
    ]
    scratch = [
        *[pltpu.VMEM((4 * w.shape[2], w.shape[3]), BF16) for w in full],
        *[pltpu.VMEM(*held) for held in HELD_SHAPES],
        *[buffer for shape in LEFT_SHAPES for buffer in meet_buffers(shape)],
        *[buffer for shape in RIGHT_SHAPES for buffer in meet_buffers(shape)],
        *meet_buffers((ROWS, 3 * D)),
        pltpu.VMEM((4, MLP_ROWS, D), BF16),
        pltpu.VMEM((4, QKV_ROWS, D), BF16),
        *[buffer for cut in CUTS_M + CUTS_Q for buffer in reduce_buffers(*cut)],
        pltpu.VMEM((2, 4, GW, ROWS), BF16),
        pltpu.VMEM((2, 4, GW, ROWS), BF16),
        pltpu.VMEM((2, ROWS, 2 * FF), BF16),
        pltpu.VMEM((2, ROWS, D), BF16),
        pltpu.VMEM((2, ROWS, D), BF16),
        pltpu.VMEM((2, ROWS, 3 * D), BF16),
        pltpu.VMEM((2, ROWS, D), BF16),
        pltpu.VMEM((2, 16, D), BF16),
        pltpu.VMEM((16, D), BF16),
        pltpu.VMEM((ROWS, D), F32),
        pltpu.VMEM((1, D), F32),
        pltpu.VMEM((3 * D, ROWS), F32),
        pltpu.VMEM((4, GW, ROWS), BF16),
        pltpu.VMEM((CTX, 2 * GW, ROWS), BF16),
        pltpu.VMEM((2, 4, GW, ROWS), BF16),
        pltpu.VMEM((2, 8, 2 * GW, ROWS), BF16),
        pltpu.VMEM((8, 2 * GW, ROWS), BF16),
        pltpu.VMEM((2, 8, 2 * GW, ROWS), BF16),
        DMA((2, 4, 4)),
        DMA((3, 7)),
        DMA((2, Lines.count)),
    ]
    return pl.pallas_call(
        backward_kernel,
        out_shape=[
            sds((2, ROWS, D), BF16), sds((2, ROWS, D), BF16),
            sds((2, MLP_ROWS, D), BF16), sds((2, QKV_ROWS, D), BF16),
        ],
        in_specs=[VM] * 3 + [ANY] * 3 + [ANY] * 4 + [ANY] * 6 + [VM] * 4,
        out_specs=[ANY, ANY, VM, VM],
        scratch_shapes=scratch,
        compiler_params=pltpu.CompilerParams(
            collective_id=next(ids), has_side_effects=True, vmem_limit_bytes=VMEM_LIMIT
        ),
        name="backward",
    )(*tables, gains, cotangent, inputs, outs, *full, q, kv, wide, totals, hidden, gate_up, *lefts)


def rope_tables():
    positions = (lax.axis_index("ctx") * ROWS + lax.iota(jnp.int32, ROWS)).astype(F32)
    frequency = 1.0 / 160000.0 ** (jnp.arange(HEAD_DIM // 2, dtype=F32) * 2.0 / HEAD_DIM)
    angles = frequency[:, None] * positions[None, :]
    return jnp.cos(angles), jnp.sin(angles)


def local(inputs, cotangent, attn_gain, qkv_weight, out_weight, mlp_gain, up_weight, down_weight):
    z = lax.axis_index("wshard")
    gain = jnp.concatenate([attn_gain, mlp_gain], axis=0)
    lanes = lax.broadcasted_iota(jnp.int32, (2, 4, 192), 1) == z
    gain = jnp.where(lanes, gain[:, None, :], jnp.zeros((), BF16)).reshape(2, D)
    gain = jnp.pad(gain, ((0, 14), (0, 0)))
    tables = rope_tables()
    stored, full, gains = forward(
        inputs, gain, [w[0] for w in (qkv_weight, out_weight, up_weight, down_weight)], tables
    )
    activations, input_grads, fin_m, fin_q = backward(tables, gains, cotangent, inputs, full, stored)
    shapes = [(192, 3 * D), (192, D), (288, D), (192, 3 * D), (1, 192), (1, 192)]
    grad_up, grad_out, grad_down, grad_qkv, gain_one, gain_two, activations, input_grads = compute_call(
        assemble_kernel,
        (fin_m, fin_q, activations, input_grads),
        [sds(shape, F32) for shape in shapes] + [sds((2, ROWS, D), BF16)] * 2,
        name="assemble",
    )
    return (
        activations[None, :, None],
        input_grads[None, :, None],
        gain_one,
        grad_qkv[None],
        grad_out[None],
        gain_two,
        grad_up[None],
        grad_down[None],
    )


def solution(mesh):
    global ids
    ids = iter(range(1, 64))
    placed = (
        P(None, "wshard", "ctx", None),
        P(None, "wshard", "ctx", None),
        P("section", "wshard"),
        P("section", "wshard", None),
        P("section", "wshard", None),
        P("section", "wshard"),
        P("section", "wshard", None),
        P("section", "wshard", None),
    )
    return jax.shard_map(
        local,
        mesh=mesh,
        in_specs=placed,
        out_specs=(
            P("section", None, "wshard", "ctx", None),
            P("section", None, "wshard", "ctx", None),
            P("section", "wshard"),
            P("section", "wshard", None),
            P("section", "wshard", None),
            P("section", "wshard"),
            P("section", "wshard", None),
            P("section", "wshard", None),
        ),
        check_vma=False,
    )
```
